32 devices in a mesh: groups: 2 (over y), blk: 4 (over z), clus: 4 (over x, core).
Axes of the slice: x: 2, y: 2, z: 4, core: 2. Of those that a mesh axis runs over, the one named last changes fastest.
Arguments:
- embeddings: bfloat16 [8192, 1024], P(('groups', 'blk', 'clus')), parts along dimension 0
- cluster: int32 [8192], P(('groups', 'blk', 'clus')), parts along dimension 0, may hold values from 0 to 3, as said below
- row_ids: int32 [8192], P(('groups', 'blk', 'clus')), parts along dimension 0, may hold values from 0 to 4095, each once
Outputs:
- best_sim: float32 [8192], P(('groups', 'blk', 'clus')), parts along dimension 0
The draws below stay inside these ranges and needn't reach their ends.
There are 2 independent parts, one for each index of `groups`. The reference program is written for one: setup_inputs(seed, part) draws one part's arguments, and reference() takes and returns one part's arrays. A program takes and returns all parts, laid end to end along the dimension named above; each array names one. Nothing has to cross between parts.
Inputs may be any that keep to these rules, and one draw needn't show every extreme that they name: In each device's aligned block of 256 rows no cluster appears more than 64 times, and some cluster appears exactly 64 times. `row_ids`: each index appears once.
All inputs are finite; a program needn't handle non-finite values.
Results may differ from the reference program's by a relative error of at most 0.00055.
Values may be sent and summed in bfloat16 or wider, within the bound.
No kernel may reach another device: no remote copies, remote signals or barrier semaphores. Data moves between devices by JAX's collectives and lax.ppermute only.
A program may use at most 64 MiB of HBM per device.

```python
import math
import jax
import jax.numpy as jnp
from jax import lax

D = 1024
ROWS_DEV = 256
CAP = 64
ROWS = 4096
N_CLUS = 4


def draw_cluster(key, part):
    key = jax.random.fold_in(key, 11)
    key_rank, key_noise, key_full, key_order = jax.random.split(key, 4)
    block_count = ROWS // ROWS_DEV
    slot_count = N_CLUS * CAP
    slot_cluster = jnp.arange(slot_count, dtype=jnp.int32) // CAP
    priority = jax.random.permutation(key_rank, N_CLUS).astype(jnp.int32)
    noise_score = jax.random.randint(key_noise, (block_count, slot_count), 0, 1 << 16).astype(jnp.int32)
    full_cluster = jax.random.randint(key_full, (block_count // N_CLUS,), 0, N_CLUS).astype(jnp.int32)
    full_block = jnp.repeat(full_cluster, N_CLUS)
    score = noise_score + priority[slot_cluster][None, :] * (1 << 14)
    score = jnp.where(slot_cluster[None, :] == full_block[:, None], -1, score)
    score = score * slot_count + jnp.arange(slot_count, dtype=jnp.int32)[None, :]
    chosen = jnp.argsort(score, axis=1)[:, :ROWS_DEV]
    assigned = slot_cluster[chosen]
    shuffle_key = jax.random.randint(key_order, (block_count, ROWS_DEV), 0, 1 << 16).astype(jnp.int32) * ROWS_DEV + jnp.arange(ROWS_DEV, dtype=jnp.int32)[None, :]
    placed = jnp.take_along_axis(assigned, jnp.argsort(shuffle_key, axis=1), axis=1)
    return placed.reshape(ROWS).astype(jnp.int32)


def draw_embeddings(key, part):
    key = jax.random.fold_in(key, 23)
    key_family, key_vector, key_weight, key_noise, key_scale = jax.random.split(key, 5)
    family_count = max(ROWS // 4, 1)
    family = jax.random.randint(key_family, (ROWS,), 0, family_count)
    family_vector = jax.random.normal(key_vector, (family_count, D), jnp.float32)
    weight = jax.random.uniform(key_weight, (ROWS, 1), jnp.float32, 0.3, 1.5)
    noise = jax.random.normal(key_noise, (ROWS, D), jnp.float32)
    scale = jnp.exp(jax.random.uniform(key_scale, (ROWS, 1), jnp.float32, 0.0, math.log(10.0)))
    return ((family_vector[family] * weight + 0.6 * noise) * scale).astype(jnp.bfloat16)


def setup_inputs(seed: int = 0, part: int = 0) -> dict:
    key_list = jax.random.split(jax.random.key(seed), 4)
    part_keys = jax.random.split(jax.random.fold_in(key_list[3], part), 4)
    embeddings = draw_embeddings(jax.random.fold_in(jax.random.fold_in(key_list[3], part), 71), part)
    cluster = draw_cluster(jax.random.fold_in(jax.random.fold_in(key_list[3], part), 71), part)
    row_ids = jax.random.permutation(part_keys[2], ROWS).astype(jnp.int32)
    return {"embeddings": embeddings, "cluster": cluster, "row_ids": row_ids}


def reference(embeddings, cluster, row_ids):
    values = embeddings.astype(jnp.float32)
    unit_rows = (values * lax.rsqrt(lax.optimization_barrier(jnp.mean(values * values, axis=1, keepdims=True)) + 1e-06) * D ** (-0.5)).astype(jnp.bfloat16)
    order_key = cluster * ROWS + row_ids
    sorted_order = jnp.argsort(order_key).astype(jnp.int32)
    sorted_unit = unit_rows[sorted_order]
    sorted_cluster = cluster[sorted_order]
    sorted_ids = row_ids[sorted_order]
    counts = lax.optimization_barrier(jnp.sum((sorted_cluster[:, None] == jnp.arange(N_CLUS, dtype=jnp.int32)[None, :]).astype(jnp.int32), axis=0))
    starts = (jnp.cumsum(counts) - counts).astype(jnp.int32)
    block_len = math.gcd(512, ROWS)
    block_count = ROWS // block_len

    def one_block(query_block):
        offset = (query_block * block_len).astype(jnp.int32)
        query = lax.dynamic_slice_in_dim(sorted_unit, offset, block_len, 0)
        query_cluster = lax.dynamic_slice_in_dim(sorted_cluster, offset, block_len, 0)
        query_ids = lax.dynamic_slice_in_dim(sorted_ids, offset, block_len, 0)
        first_block = (starts[query_cluster[0]] // block_len).astype(jnp.int32)

        def step_keys(key_block, best_now):
            key_offset = (key_block * block_len).astype(jnp.int32)
            keys = lax.dynamic_slice_in_dim(sorted_unit, key_offset, block_len, 0)
            key_cluster = lax.dynamic_slice_in_dim(sorted_cluster, key_offset, block_len, 0)
            key_ids = lax.dynamic_slice_in_dim(sorted_ids, key_offset, block_len, 0)
            scores = lax.dot_general(query, keys, (((1,), (1,)), ((), ())), preferred_element_type=jnp.float32)
            allowed = (query_cluster[:, None] == key_cluster[None, :]) & (key_ids[None, :] < query_ids[:, None])
            return jnp.maximum(best_now, lax.optimization_barrier(jnp.max(jnp.where(allowed, scores, -1.0), axis=1)))
        return lax.fori_loop(first_block, (query_block + 1).astype(jnp.int32), step_keys, jnp.full((block_len,), -1.0, jnp.float32))
    best_sorted = lax.map(one_block, jnp.arange(block_count, dtype=jnp.int32)).reshape(ROWS)
    return jnp.zeros((ROWS,), jnp.float32).at[sorted_order].set(best_sorted)
```

```python
import functools

import jax
import jax.numpy as jnp
from jax import lax
from jax.experimental import pallas as pl
from jax.experimental.pallas import tpu as pltpu
from jax.sharding import PartitionSpec as P

CAP = 64
EPS = 1e-06
sentinel_id = 1 << 30
VMEM = pl.BlockSpec(memory_space=pltpu.VMEM)


def passed_along(value, axis, by):
    size = lax.axis_size(axis)
    return lax.ppermute(value, axis, [(i, (i + by) % size) for i in range(size)])


def ring(embeddings, cluster, row_ids):
    owners = lax.axis_size("clus")
    loop_size = lax.axis_size("blk")
    feature_width = embeddings.shape[1]
    slot_count = owners * CAP
    values = embeddings.astype(jnp.float32)
    unit_rows = (
        values
        * lax.rsqrt(jnp.mean(values * values, axis=1, keepdims=True) + EPS)
        * feature_width ** (-0.5)
    ).astype(jnp.bfloat16)
    onehot = (cluster[:, None] == jnp.arange(owners, dtype=jnp.int32)[None, :]).astype(jnp.int32)
    before = jnp.cumsum(onehot, axis=0) - onehot
    position = jnp.sum(before * onehot, axis=1)
    target = cluster * CAP + position
    send_unit = jnp.zeros((slot_count, feature_width), jnp.bfloat16).at[target].set(unit_rows)
    send_ids = jnp.full((slot_count,), sentinel_id, jnp.int32).at[target].set(row_ids)
    exchange = functools.partial(
        lax.all_to_all, axis_name="clus", split_axis=0, concat_axis=0, tiled=True
    )
    keys_unit = exchange(send_unit.reshape(owners, CAP, feature_width)).reshape(
        slot_count, feature_width
    )
    keys_ids = exchange(send_ids.reshape(owners, CAP)).reshape(slot_count)

    def absorb(best_now, other_unit, other_ids):
        scores = lax.dot_general(
            keys_unit, other_unit, (((1,), (1,)), ((), ())), preferred_element_type=jnp.float32
        )
        allowed = other_ids[None, :] < keys_ids[:, None]
        return jnp.maximum(best_now, jnp.max(jnp.where(allowed, scores, -1.0), axis=1))

    start_best = jnp.full((slot_count,), -1.0, jnp.float32)

    def advance(step_index, state_now):
        best_now, moving_unit, moving_ids = state_now
        moving_unit, moving_ids = passed_along((moving_unit, moving_ids), "blk", 1)
        return (absorb(best_now, moving_unit, moving_ids), moving_unit, moving_ids)

    best_sim, _, _ = lax.fori_loop(
        0, loop_size - 1, advance, (absorb(start_best, keys_unit, keys_ids), keys_unit, keys_ids)
    )
    returned = exchange(best_sim.reshape(owners, CAP)).reshape(slot_count)
    return returned[target]


def meeting_blk(c, blocks):
    return (blocks - 1) // 2 + (c % 2 if blocks > 1 else 0)


def meeting_here(owners, blocks):
    u = lax.axis_index("clus")
    b = lax.axis_index("blk")
    middle = (blocks - 1) // 2 + (lax.rem(u, 2) if blocks > 1 else 0)
    return u, b, b == middle


def sort_kernel(owners, emb_ref, cluster_ref, ids_ref, *outs):
    slot_refs, sorted_ids_ref, target_ref = outs[:owners], outs[owners], outs[owners + 1]
    rows, width = emb_ref.shape
    slots = owners * CAP
    u = lax.axis_index("clus")
    slot = lax.rem(cluster_ref[...] - u + owners, owners)
    onehot = lax.broadcasted_iota(jnp.int32, (8, rows), 0) == slot
    earlier = (
        lax.broadcasted_iota(jnp.int32, (rows, rows), 0)
        < lax.broadcasted_iota(jnp.int32, (rows, rows), 1)
    ).astype(jnp.bfloat16)
    before = jnp.dot(
        onehot.astype(jnp.bfloat16), earlier, preferred_element_type=jnp.float32
    )
    position = jnp.sum(jnp.where(onehot, before, 0.0), axis=0, keepdims=True)
    target = slot * CAP + position.astype(jnp.int32)
    target_ref[...] = target
    place = (lax.broadcasted_iota(jnp.int32, (slots, rows), 0) == target).astype(jnp.bfloat16)
    values = jnp.dot(place, emb_ref[...], preferred_element_type=jnp.float32)
    mean = jnp.mean(values * values, axis=1, keepdims=True)
    unit = (values * lax.rsqrt(mean + EPS) * width ** (-0.5)).astype(jnp.bfloat16)
    for j in range(owners):
        slot_refs[j][...] = unit[j * CAP : (j + 1) * CAP]
    ids = ids_ref[...]
    row = lax.broadcasted_iota(jnp.int32, (8, rows), 0)
    parts = jnp.where(row == 0, ids >> 8, jnp.where(row == 1, ids & 255, 1))
    moved = lax.dot_general(
        parts.astype(jnp.float32).astype(jnp.bfloat16),
        place,
        (((1,), (1,)), ((), ())),
        preferred_element_type=jnp.float32,
    ).astype(jnp.int32)
    sorted_ids = moved[0:1] * 256 + moved[1:2]
    sorted_ids_ref[...] = jnp.where(moved[2:3] > 0, sorted_ids, sentinel_id)


def order_kernel(owners, blocks, all_ids_ref, row_ref, column_ref):
    u, b, _ = meeting_here(owners, blocks)
    pieces = []
    for j in range(owners):
        for k in range(blocks):
            source = lax.rem(b - k + blocks, blocks) * owners + lax.rem(u - j + owners, owners)
            pieces.append(all_ids_ref[pl.ds(source, 1), :][:, j * CAP : (j + 1) * CAP])
    ids = jnp.concatenate(pieces, axis=1)
    row_ref[...] = ids
    for q in range(ids.shape[1] // 128):
        piece = ids[:, q * 128 : (q + 1) * 128]
        column_ref[q * 128 : (q + 1) * 128, :] = jnp.broadcast_to(piece, (128, 128)).T


def meet_kernel(owners, blocks, *refs):
    count = owners * blocks
    block_refs, row_ref, column_ref, best_ref = refs[:count], refs[count], refs[count + 1], refs[-1]
    _, _, here = meeting_here(owners, blocks)
    tile = 256
    per = tile // CAP
    tiles = count // per

    @pl.when(jnp.logical_not(here))
    def _():
        best_ref[...] = jnp.full(best_ref.shape, -1.0, jnp.float32)

    @pl.when(here)
    def _():
        def rows_of(t):
            return jnp.concatenate([r[...] for r in block_refs[t * per : (t + 1) * per]], axis=0)

        for query in range(tiles):
            query_rows = rows_of(query)
            query_ids = row_ref[:, query * tile : (query + 1) * tile]
            best = jnp.full((1, tile), -1.0, jnp.float32)
            for key in range(tiles):
                scores = lax.dot_general(
                    rows_of(key),
                    query_rows,
                    (((1,), (1,)), ((), ())),
                    preferred_element_type=jnp.float32,
                )
                key_ids = column_ref[key * tile : (key + 1) * tile, :]
                key_ids = jnp.concatenate([key_ids] * (tile // 128), axis=1)
                allowed = key_ids < query_ids
                best = jnp.maximum(
                    best, jnp.max(jnp.where(allowed, scores, -1.0), axis=0, keepdims=True)
                )
            for part in range(tile // 128):
                at = query * (tile // 128) + part
                best_ref[at : at + 1, :] = best[:, part * 128 : (part + 1) * 128]


def home_kernel(owners, blocks, *refs):
    count = owners * blocks
    got_refs, target_ref, out_ref = refs[:count], refs[count], refs[-1]
    u = lax.axis_index("clus")
    b = lax.axis_index("blk")
    slots = owners * CAP
    rows = target_ref.shape[1]
    pieces = []
    for j in range(owners):
        c = lax.rem(u + j, owners)
        middle = (blocks - 1) // 2 + (lax.rem(c, 2) if blocks > 1 else 0)
        want = lax.rem(middle - b + blocks, blocks)
        piece = None
        for k in range(blocks):
            q = j * blocks + k
            lane = q * CAP % 128
            value = got_refs[q][q * CAP // 128 : q * CAP // 128 + 1, lane : lane + CAP]
            piece = value if piece is None else jnp.where(want == k, value, piece)
        pieces.append(piece)
    best = jnp.concatenate(pieces, axis=1)
    high = best.astype(jnp.bfloat16).astype(jnp.float32)
    rest = best - high
    middle_part = rest.astype(jnp.bfloat16).astype(jnp.float32)
    low = rest - middle_part
    row = lax.broadcasted_iota(jnp.int32, (8, slots), 0)
    parts = jnp.where(row == 0, high, jnp.where(row == 1, middle_part, jnp.where(row == 2, low, 0.0)))
    place = lax.broadcasted_iota(jnp.int32, (slots, rows), 0) == target_ref[...]
    moved = jnp.dot(
        parts.astype(jnp.bfloat16), place.astype(jnp.bfloat16), preferred_element_type=jnp.float32
    )
    out_ref[...] = moved[0:1] + moved[1:2] + moved[2:3]


def meet(embeddings, cluster, row_ids):
    owners = lax.axis_size("clus")
    blocks = lax.axis_size("blk")
    rows, width = embeddings.shape
    slots = owners * CAP
    count = owners * blocks
    everyone = ("blk", "clus")

    def pairs(j, k):
        found = []
        for c in range(owners):
            middle = meeting_blk(c, blocks)
            source = ((middle - k) % blocks) * owners + (c - j) % owners
            found.append((source, middle * owners + c))
        return found

    *slot_rows, sorted_ids, target = pl.pallas_call(
        functools.partial(sort_kernel, owners),
        out_shape=[jax.ShapeDtypeStruct((CAP, width), jnp.bfloat16)] * owners
        + [
            jax.ShapeDtypeStruct((1, slots), jnp.int32),
            jax.ShapeDtypeStruct((1, rows), jnp.int32),
        ],
        in_specs=[VMEM] * 3,
        out_specs=[VMEM] * (owners + 2),
        name="sort_rows",
    )(embeddings, cluster.reshape(1, rows), row_ids.reshape(1, rows))
    all_ids = lax.all_gather(sorted_ids, everyone, axis=0, tiled=True)
    arrived = []
    for j in range(owners):
        for k in range(blocks):
            if j == 0 and k == 0:
                arrived.append(slot_rows[0])
            else:
                arrived.append(lax.ppermute(slot_rows[j], everyone, pairs(j, k)))
    ids_row, ids_column = pl.pallas_call(
        functools.partial(order_kernel, owners, blocks),
        out_shape=[
            jax.ShapeDtypeStruct((1, count * CAP), jnp.int32),
            jax.ShapeDtypeStruct((count * CAP, 128), jnp.int32),
        ],
        in_specs=[VMEM],
        out_specs=[VMEM] * 2,
        name="order_ids",
    )(all_ids)
    best = pl.pallas_call(
        functools.partial(meet_kernel, owners, blocks),
        out_shape=jax.ShapeDtypeStruct((count * CAP // 128, 128), jnp.float32),
        in_specs=[VMEM] * (count + 2),
        out_specs=VMEM,
        name="meet_scores",
    )(*arrived, ids_row, ids_column)
    returned = []
    for j in range(owners):
        for k in range(blocks):
            if j == 0 and k == 0:
                returned.append(best)
            else:
                returned.append(
                    lax.ppermute(best, everyone, [(t, s) for s, t in pairs(j, k)])
                )
    out = pl.pallas_call(
        functools.partial(home_kernel, owners, blocks),
        out_shape=jax.ShapeDtypeStruct((1, rows), jnp.float32),
        in_specs=[VMEM] * (count + 1),
        out_specs=VMEM,
        name="home_scores",
    )(*returned, target)
    return out.reshape(rows)


def solution(mesh):
    one_device_takes_a_cluster = mesh.shape["blk"] * mesh.shape["clus"] <= 16
    return jax.shard_map(
        meet if one_device_takes_a_cluster else ring,
        mesh=mesh,
        in_specs=(
            P(("groups", "blk", "clus"), None),
            P(("groups", "blk", "clus")),
            P(("groups", "blk", "clus")),
        ),
        out_specs=P(("groups", "blk", "clus")),
        check_vma=False,
    )
```

```python
import functools

import jax
import jax.numpy as jnp
from jax import lax
from jax.experimental import pallas as pl
from jax.experimental.pallas import tpu as pltpu
from jax.sharding import PartitionSpec as P

CAP = 64
EPS = 1e-06
sentinel_id = 1 << 30
VMEM = pl.BlockSpec(memory_space=pltpu.VMEM)


def passed_along(value, axis, by):
    size = lax.axis_size(axis)
    return lax.ppermute(value, axis, [(i, (i + by) % size) for i in range(size)])


def ring(embeddings, cluster, row_ids):
    owners = lax.axis_size("clus")
    loop_size = lax.axis_size("blk")
    feature_width = embeddings.shape[1]
    slot_count = owners * CAP
    values = embeddings.astype(jnp.float32)
    unit_rows = (
        values
        * lax.rsqrt(jnp.mean(values * values, axis=1, keepdims=True) + EPS)
        * feature_width ** (-0.5)
    ).astype(jnp.bfloat16)
    onehot = (cluster[:, None] == jnp.arange(owners, dtype=jnp.int32)[None, :]).astype(jnp.int32)
    before = jnp.cumsum(onehot, axis=0) - onehot
    position = jnp.sum(before * onehot, axis=1)
    target = cluster * CAP + position
    send_unit = jnp.zeros((slot_count, feature_width), jnp.bfloat16).at[target].set(unit_rows)
    send_ids = jnp.full((slot_count,), sentinel_id, jnp.int32).at[target].set(row_ids)
    exchange = functools.partial(
        lax.all_to_all, axis_name="clus", split_axis=0, concat_axis=0, tiled=True
    )
    keys_unit = exchange(send_unit.reshape(owners, CAP, feature_width)).reshape(
        slot_count, feature_width
    )
    keys_ids = exchange(send_ids.reshape(owners, CAP)).reshape(slot_count)

    def absorb(best_now, other_unit, other_ids):
        scores = lax.dot_general(
            keys_unit, other_unit, (((1,), (1,)), ((), ())), preferred_element_type=jnp.float32
        )
        allowed = other_ids[None, :] < keys_ids[:, None]
        return jnp.maximum(best_now, jnp.max(jnp.where(allowed, scores, -1.0), axis=1))

    start_best = jnp.full((slot_count,), -1.0, jnp.float32)

    def advance(step_index, state_now):
        best_now, moving_unit, moving_ids = state_now
        moving_unit, moving_ids = passed_along((moving_unit, moving_ids), "blk", 1)
        return (absorb(best_now, moving_unit, moving_ids), moving_unit, moving_ids)

    best_sim, _, _ = lax.fori_loop(
        0, loop_size - 1, advance, (absorb(start_best, keys_unit, keys_ids), keys_unit, keys_ids)
    )
    returned = exchange(best_sim.reshape(owners, CAP)).reshape(slot_count)
    return returned[target]


SLABS_ROWS = 2 * CAP


def middle_of(core):
    return 1 + core


def sources():
    return [(0, 3), (1, 3), (0, 0), (0, 2), (1, 0), (1, 2), (1, 1)]


def blk_of(far_blk, core):
    return far_blk if core == 0 else 3 - far_blk


def here():
    u = lax.axis_index("clus")
    b = lax.axis_index("blk")
    return u, b


def put_slabs(ref, start, rows):
    for t in range(rows.shape[1] // 128):
        ref[pl.ds(start + t * SLABS_ROWS, rows.shape[0]), :] = rows[:, t * 128 : (t + 1) * 128]


def get_slabs(ref, start, count, slabs):
    return jnp.concatenate(
        [ref[t * SLABS_ROWS + start : t * SLABS_ROWS + start + count, :] for t in range(slabs)], axis=1
    )


def sort_kernel(emb_ref, cluster_ref, ids_ref, keep_ref, give_ref, target_ref):
    rows, width = emb_ref.shape
    slots = 4 * CAP
    u, _ = here()
    cluster = cluster_ref[...]
    slot = cluster ^ u
    onehot = lax.broadcasted_iota(jnp.int32, (8, rows), 0) == slot
    earlier = (
        lax.broadcasted_iota(jnp.int32, (rows, rows), 0)
        < lax.broadcasted_iota(jnp.int32, (rows, rows), 1)
    ).astype(jnp.bfloat16)
    before = jnp.dot(onehot.astype(jnp.bfloat16), earlier, preferred_element_type=jnp.float32)
    position = jnp.sum(jnp.where(onehot, before, 0.0), axis=0, keepdims=True).astype(jnp.int32)
    target_ref[...] = cluster * CAP + position
    order = (slot & 1) * 2 + (slot >> 1)
    place = (
        lax.broadcasted_iota(jnp.int32, (slots, rows), 0) == order * CAP + position
    ).astype(jnp.bfloat16)
    values = jnp.dot(place, emb_ref[...], preferred_element_type=jnp.float32)
    mean = jnp.mean(values * values, axis=1, keepdims=True)
    unit = (values * lax.rsqrt(mean + EPS) * width ** (-0.5)).astype(jnp.bfloat16)
    put_slabs(keep_ref, 0, unit[: 2 * CAP])
    put_slabs(give_ref, 0, unit[2 * CAP :])
    ids = ids_ref[...]
    row = lax.broadcasted_iota(jnp.int32, (16, rows), 0)
    parts = jnp.where(row == 0, ids >> 8, jnp.where(row == 1, ids & 255, 1))
    moved = lax.dot_general(
        parts.astype(jnp.float32).astype(jnp.bfloat16),
        place,
        (((1,), (1,)), ((), ())),
        preferred_element_type=jnp.float32,
    )
    row = lax.broadcasted_iota(jnp.int32, (16, slots), 0)
    moved = jnp.where((moved[2:3] == 0.0) & (row == 0), 256.0, moved).astype(jnp.bfloat16)
    tail = width // 128 * SLABS_ROWS
    keep_ref[tail : tail + 16, :] = moved[:, : 2 * CAP]
    give_ref[tail : tail + 16, :] = moved[:, 2 * CAP :]


def join_kernel(keep_ref, got_ref, near_ref, far_ref):
    u, _ = here()
    core = lax.rem(u, 2)
    tail = keep_ref.shape[0] - 16
    own_at = pl.multiple_of(core * CAP, CAP)
    other_at = pl.multiple_of((1 - core) * CAP, CAP)
    for out_ref, start in ((near_ref, 0), (far_ref, CAP)):
        for t in range(tail // SLABS_ROWS):
            base = t * SLABS_ROWS
            out_ref[pl.ds(base + own_at, CAP), :] = keep_ref[base + start : base + start + CAP, :]
            out_ref[pl.ds(base + other_at, CAP), :] = got_ref[base + start : base + start + CAP, :]
        own = keep_ref[tail:, :].astype(jnp.float32)[:, start : start + CAP]
        other = got_ref[tail:, :].astype(jnp.float32)[:, start : start + CAP]
        first = jnp.where(core == 0, own, other)
        second = jnp.where(core == 0, other, own)
        out_ref[tail:, :] = jnp.concatenate([first, second], axis=1).astype(jnp.bfloat16)


def meet_kernel(*refs):
    count = 8
    block_refs, best_ref = refs[:count], refs[-1]
    u, b = here()
    core = lax.rem(u, 2)
    tail = block_refs[0].shape[0] - 16
    slabs = tail // SLABS_ROWS
    tile = 256
    per = tile // SLABS_ROWS
    tiles = count // per

    @pl.when(b == middle_of(core))
    def _():
        def rows_of(t):
            return jnp.concatenate(
                [get_slabs(r, 0, SLABS_ROWS, slabs) for r in block_refs[t * per : (t + 1) * per]],
                axis=0,
            )

        ids_of = []
        for r in block_refs:
            parts = r[tail:, :].astype(jnp.float32)
            ids_of.append(parts[0:1] * 256.0 + parts[1:2])
        down = [jnp.broadcast_to(i, (SLABS_ROWS, 128)).T for i in ids_of]
        for query in range(tiles):
            query_rows = rows_of(query)
            query_ids = jnp.concatenate(ids_of[query * per : (query + 1) * per], axis=1)
            best = jnp.full((1, tile), -1.0, jnp.float32)
            for key in range(tiles):
                scores = lax.dot_general(
                    rows_of(key),
                    query_rows,
                    (((1,), (1,)), ((), ())),
                    preferred_element_type=jnp.float32,
                )
                key_ids = jnp.concatenate(down[key * per : (key + 1) * per], axis=0)
                key_ids = jnp.concatenate([key_ids] * (tile // 128), axis=1)
                best = jnp.maximum(
                    best,
                    jnp.max(jnp.where(key_ids < query_ids, scores, -1.0), axis=0, keepdims=True),
                )
            for part in range(per):
                q = query * per + part
                other, far_blk = (0, 0) if q == 0 else sources()[q - 1]
                if q == 0:
                    at_blk = b
                else:
                    at_blk = jnp.where(core == 0, far_blk, 3 - far_blk)
                chip = (u >> 1) ^ other
                row = best[:, part * 128 : (part + 1) * 128]
                for c in range(2):
                    best_ref[at_blk * 4 + chip * 2 + c] = row


def home_kernel(got_ref, target_ref, out_ref):
    u, _ = here()
    core = lax.rem(u, 2)
    slots = 4 * CAP
    rows = target_ref.shape[1]
    pieces = []
    for c in range(4):
        row = got_ref[middle_of(c % 2) * 4 + c]
        pieces.append(jnp.where(core == 0, row[:, :CAP], row[:, CAP:]))
    best = jnp.concatenate(pieces, axis=1)
    high = best.astype(jnp.bfloat16).astype(jnp.float32)
    rest = best - high
    middle_part = rest.astype(jnp.bfloat16).astype(jnp.float32)
    low = rest - middle_part
    row = lax.broadcasted_iota(jnp.int32, (8, slots), 0)
    parts = jnp.where(row == 0, high, jnp.where(row == 1, middle_part, jnp.where(row == 2, low, 0.0)))
    place = lax.broadcasted_iota(jnp.int32, (slots, rows), 0) == target_ref[...]
    moved = jnp.dot(
        parts.astype(jnp.bfloat16), place.astype(jnp.bfloat16), preferred_element_type=jnp.float32
    )
    out_ref[...] = moved[0:1] + moved[1:2] + moved[2:3]


def meet(embeddings, cluster, row_ids):
    rows, width = embeddings.shape
    everyone = ("blk", "clus")
    payload = jax.ShapeDtypeStruct((width // 128 * SLABS_ROWS + 16, 128), jnp.bfloat16)

    def pairs(other, far_blk):
        found = []
        for c in range(4):
            source = blk_of(far_blk, c % 2) * 4 + (c ^ (2 * other))
            found.append((source, middle_of(c % 2) * 4 + c))
        return found

    keep, give, target = pl.pallas_call(
        sort_kernel,
        out_shape=[payload, payload, jax.ShapeDtypeStruct((1, rows), jnp.int32)],
        in_specs=[VMEM] * 3,
        out_specs=[VMEM] * 3,
        name="sort_rows",
    )(embeddings, cluster.reshape(1, rows), row_ids.reshape(1, rows))
    got = lax.ppermute(give, "clus", [(c, c ^ 1) for c in range(4)])
    near, far = pl.pallas_call(
        join_kernel,
        out_shape=[payload] * 2,
        in_specs=[VMEM] * 2,
        out_specs=[VMEM] * 2,
        name="join_cores",
    )(keep, got)
    arrived = [near]
    for other, far_blk in sources():
        arrived.append(lax.ppermute(far if other else near, everyone, pairs(other, far_blk)))
    best = pl.pallas_call(
        meet_kernel,
        out_shape=jax.ShapeDtypeStruct((16, 1, 128), jnp.float32),
        in_specs=[VMEM] * 8,
        out_specs=VMEM,
        name="meet_scores",
    )(*arrived)
    returned = lax.all_to_all(best, everyone, split_axis=0, concat_axis=0, tiled=True)
    out = pl.pallas_call(
        home_kernel,
        out_shape=jax.ShapeDtypeStruct((1, rows), jnp.float32),
        in_specs=[VMEM] * 2,
        out_specs=VMEM,
        name="home_scores",
    )(returned, target)
    return out.reshape(rows)


def solution(mesh):
    takes_a_cluster = mesh.shape["blk"] == 4 and mesh.shape["clus"] == 4
    return jax.shard_map(
        meet if takes_a_cluster else ring,
        mesh=mesh,
        in_specs=(
            P(("groups", "blk", "clus"), None),
            P(("groups", "blk", "clus")),
            P(("groups", "blk", "clus")),
        ),
        out_specs=P(("groups", "blk", "clus")),
        check_vma=False,
    )
```

```python
import functools

import jax
import jax.numpy as jnp
from jax import lax
from jax.experimental import pallas as pl
from jax.experimental.pallas import tpu as pltpu
from jax.sharding import PartitionSpec as P

CAP = 64
EPS = 1e-06
sentinel_id = 1 << 30
VMEM = pl.BlockSpec(memory_space=pltpu.VMEM)


def passed_along(value, axis, by):
    size = lax.axis_size(axis)
    return lax.ppermute(value, axis, [(i, (i + by) % size) for i in range(size)])


def ring(embeddings, cluster, row_ids):
    owners = lax.axis_size("clus")
    loop_size = lax.axis_size("blk")
    feature_width = embeddings.shape[1]
    slot_count = owners * CAP
    values = embeddings.astype(jnp.float32)
    unit_rows = (
        values
        * lax.rsqrt(jnp.mean(values * values, axis=1, keepdims=True) + EPS)
        * feature_width ** (-0.5)
    ).astype(jnp.bfloat16)
    onehot = (cluster[:, None] == jnp.arange(owners, dtype=jnp.int32)[None, :]).astype(jnp.int32)
    before = jnp.cumsum(onehot, axis=0) - onehot
    position = jnp.sum(before * onehot, axis=1)
    target = cluster * CAP + position
    send_unit = jnp.zeros((slot_count, feature_width), jnp.bfloat16).at[target].set(unit_rows)
    send_ids = jnp.full((slot_count,), sentinel_id, jnp.int32).at[target].set(row_ids)
    exchange = functools.partial(
        lax.all_to_all, axis_name="clus", split_axis=0, concat_axis=0, tiled=True
    )
    keys_unit = exchange(send_unit.reshape(owners, CAP, feature_width)).reshape(
        slot_count, feature_width
    )
    keys_ids = exchange(send_ids.reshape(owners, CAP)).reshape(slot_count)

    def absorb(best_now, other_unit, other_ids):
        scores = lax.dot_general(
            keys_unit, other_unit, (((1,), (1,)), ((), ())), preferred_element_type=jnp.float32
        )
        allowed = other_ids[None, :] < keys_ids[:, None]
        return jnp.maximum(best_now, jnp.max(jnp.where(allowed, scores, -1.0), axis=1))

    start_best = jnp.full((slot_count,), -1.0, jnp.float32)

    def advance(step_index, state_now):
        best_now, moving_unit, moving_ids = state_now
        moving_unit, moving_ids = passed_along((moving_unit, moving_ids), "blk", 1)
        return (absorb(best_now, moving_unit, moving_ids), moving_unit, moving_ids)

    best_sim, _, _ = lax.fori_loop(
        0, loop_size - 1, advance, (absorb(start_best, keys_unit, keys_ids), keys_unit, keys_ids)
    )
    returned = exchange(best_sim.reshape(owners, CAP)).reshape(slot_count)
    return returned[target]


SLABS_ROWS = 2 * CAP
SMALL = pltpu.CompilerParams(vmem_limit_bytes=8 << 20)


def middle_of(core):
    return 1 + core


FAR_BLKS = (2, 0, 3)


def blk_of(far_blk, core):
    return far_blk if core == 0 else 3 - far_blk


def here():
    u = lax.axis_index("clus")
    b = lax.axis_index("blk")
    return u, b


def put_slabs(ref, start, rows):
    for t in range(rows.shape[1] // 128):
        ref[pl.ds(start + t * SLABS_ROWS, rows.shape[0]), :] = rows[:, t * 128 : (t + 1) * 128]


def get_slabs(ref, start, count, slabs):
    return jnp.concatenate(
        [ref[t * SLABS_ROWS + start : t * SLABS_ROWS + start + count, :] for t in range(slabs)], axis=1
    )


def sort_kernel(emb_ref, cluster_ref, ids_ref, keep_ref, give_ref, target_ref):
    rows, width = emb_ref.shape
    slots = 4 * CAP
    u, _ = here()
    cluster = cluster_ref[...]
    slot = cluster ^ u
    onehot = lax.broadcasted_iota(jnp.int32, (8, rows), 0) == slot
    earlier = (
        lax.broadcasted_iota(jnp.int32, (rows, rows), 0)
        < lax.broadcasted_iota(jnp.int32, (rows, rows), 1)
    ).astype(jnp.bfloat16)
    before = jnp.dot(onehot.astype(jnp.bfloat16), earlier, preferred_element_type=jnp.float32)
    position = jnp.sum(jnp.where(onehot, before, 0.0), axis=0, keepdims=True).astype(jnp.int32)
    target_ref[...] = cluster * CAP + position
    order = (slot & 1) * 2 + (slot >> 1)
    place = (
        lax.broadcasted_iota(jnp.int32, (slots, rows), 0) == order * CAP + position
    ).astype(jnp.bfloat16)
    values = jnp.dot(place, emb_ref[...], preferred_element_type=jnp.float32)
    mean = jnp.mean(values * values, axis=1, keepdims=True)
    unit = (values * lax.rsqrt(mean + EPS) * width ** (-0.5)).astype(jnp.bfloat16)
    put_slabs(keep_ref, 0, unit[: 2 * CAP])
    put_slabs(give_ref, 0, unit[2 * CAP :])
    ids = ids_ref[...]
    row = lax.broadcasted_iota(jnp.int32, (16, rows), 0)
    parts = jnp.where(row == 0, ids >> 8, jnp.where(row == 1, ids & 255, 1))
    moved = lax.dot_general(
        parts.astype(jnp.float32).astype(jnp.bfloat16),
        place,
        (((1,), (1,)), ((), ())),
        preferred_element_type=jnp.float32,
    )
    row = lax.broadcasted_iota(jnp.int32, (16, slots), 0)
    moved = jnp.where((moved[2:3] == 0.0) & (row == 0), 256.0, moved).astype(jnp.bfloat16)
    tail = width // 128 * SLABS_ROWS
    keep_ref[tail : tail + 16, :] = moved[:, : 2 * CAP]
    give_ref[tail : tail + 16, :] = moved[:, 2 * CAP :]


def join_kernel(keep_ref, got_ref, near_ref, far_ref):
    u, _ = here()
    core = lax.rem(u, 2)
    tail = keep_ref.shape[0] - 16
    own_at = pl.multiple_of(core * CAP, CAP)
    other_at = pl.multiple_of((1 - core) * CAP, CAP)
    for out_ref, start in ((far_ref, CAP), (near_ref, 0)):
        for t in range(tail // SLABS_ROWS):
            base = t * SLABS_ROWS
            out_ref[pl.ds(base + own_at, CAP), :] = keep_ref[base + start : base + start + CAP, :]
            out_ref[pl.ds(base + other_at, CAP), :] = got_ref[base + start : base + start + CAP, :]
        own = keep_ref[tail:, :].astype(jnp.float32)[:, start : start + CAP]
        other = got_ref[tail:, :].astype(jnp.float32)[:, start : start + CAP]
        first = jnp.where(core == 0, own, other)
        second = jnp.where(core == 0, other, own)
        out_ref[tail:, :] = jnp.concatenate([first, second], axis=1).astype(jnp.bfloat16)


def meet_kernel(*refs):
    count = 8
    block_refs, best_ref = refs[:count], refs[-1]
    u, b = here()
    core = lax.rem(u, 2)
    tail = block_refs[0].shape[0] - 16
    slabs = tail // SLABS_ROWS
    tile = 256
    per = tile // SLABS_ROWS
    tiles = count // per

    @pl.when(b == middle_of(core))
    def _():
        def rows_of(t):
            return jnp.concatenate(
                [get_slabs(r, 0, SLABS_ROWS, slabs) for r in block_refs[t * per : (t + 1) * per]],
                axis=0,
            )

        ids_of = []
        for r in block_refs:
            parts = r[tail:, :].astype(jnp.float32)
            ids_of.append(parts[0:1] * 256.0 + parts[1:2])
        down = [jnp.broadcast_to(i, (SLABS_ROWS, 128)).T for i in ids_of]
        for query in range(tiles):
            query_rows = rows_of(query)
            query_ids = jnp.concatenate(ids_of[query * per : (query + 1) * per], axis=1)
            best = jnp.full((1, tile), -1.0, jnp.float32)
            for key in range(tiles):
                scores = lax.dot_general(
                    rows_of(key),
                    query_rows,
                    (((1,), (1,)), ((), ())),
                    preferred_element_type=jnp.float32,
                )
                key_ids = jnp.concatenate(down[key * per : (key + 1) * per], axis=0)
                key_ids = jnp.concatenate([key_ids] * (tile // 128), axis=1)
                best = jnp.maximum(
                    best,
                    jnp.max(jnp.where(key_ids < query_ids, scores, -1.0), axis=0, keepdims=True),
                )
            for part in range(per):
                q = query * per + part
                other, place = divmod(q, 4)
                far_blk = FAR_BLKS[place - 1]
                at_blk = jnp.where(core == 0, far_blk, 3 - far_blk) if place else b
                chip = (u >> 1) ^ other
                row = best[:, part * 128 : (part + 1) * 128]
                for c in range(2):
                    best_ref[at_blk * 4 + chip * 2 + c] = row


def home_kernel(got_ref, target_ref, out_ref):
    u, _ = here()
    core = lax.rem(u, 2)
    slots = 4 * CAP
    rows = target_ref.shape[1]
    pieces = []
    for c in range(4):
        row = got_ref[middle_of(c % 2) * 4 + c]
        pieces.append(jnp.where(core == 0, row[:, :CAP], row[:, CAP:]))
    best = jnp.concatenate(pieces, axis=1)
    high = best.astype(jnp.bfloat16).astype(jnp.float32)
    rest = best - high
    middle_part = rest.astype(jnp.bfloat16).astype(jnp.float32)
    low = rest - middle_part
    row = lax.broadcasted_iota(jnp.int32, (8, slots), 0)
    parts = jnp.where(row == 0, high, jnp.where(row == 1, middle_part, jnp.where(row == 2, low, 0.0)))
    place = lax.broadcasted_iota(jnp.int32, (slots, rows), 0) == target_ref[...]
    moved = jnp.dot(
        parts.astype(jnp.bfloat16), place.astype(jnp.bfloat16), preferred_element_type=jnp.float32
    )
    out_ref[...] = moved[0:1] + moved[1:2] + moved[2:3]


def meet(embeddings, cluster, row_ids):
    rows, width = embeddings.shape
    everyone = ("blk", "clus")
    payload = jax.ShapeDtypeStruct((width // 128 * SLABS_ROWS + 16, 128), jnp.bfloat16)

    def to_meeting(value, far_blk):
        pairs = [(blk_of(far_blk, c % 2) * 4 + c, middle_of(c % 2) * 4 + c) for c in range(4)]
        return lax.ppermute(value, everyone, pairs)

    keep, give, target = pl.pallas_call(
        sort_kernel,
        out_shape=[payload, payload, jax.ShapeDtypeStruct((1, rows), jnp.int32)],
        in_specs=[VMEM] * 3,
        out_specs=[VMEM] * 3,
        compiler_params=SMALL,
        name="sort_rows",
    )(embeddings, cluster.reshape(1, rows), row_ids.reshape(1, rows))
    got = lax.ppermute(give, "clus", [(c, c ^ 1) for c in range(4)])
    near, far = pl.pallas_call(
        join_kernel,
        out_shape=[payload] * 2,
        in_specs=[VMEM] * 2,
        out_specs=[VMEM] * 2,
        compiler_params=SMALL,
        name="join_cores",
    )(keep, got)
    crossed = lax.ppermute(far, "clus", [(c, c ^ 2) for c in range(4)])
    arrived = []
    for value in (near, crossed):
        arrived.append(value)
        arrived += [to_meeting(value, far_blk) for far_blk in FAR_BLKS]
    best = pl.pallas_call(
        meet_kernel,
        out_shape=jax.ShapeDtypeStruct((16, 1, 128), jnp.float32),
        in_specs=[VMEM] * 8,
        out_specs=VMEM,
        compiler_params=SMALL,
        name="meet_scores",
    )(*arrived)
    returned = lax.all_to_all(best, everyone, split_axis=0, concat_axis=0, tiled=True)
    out = pl.pallas_call(
        home_kernel,
        out_shape=jax.ShapeDtypeStruct((1, rows), jnp.float32),
        in_specs=[VMEM] * 2,
        out_specs=VMEM,
        compiler_params=SMALL,
        name="home_scores",
    )(returned, target)
    return out.reshape(rows)


def solution(mesh):
    takes_a_cluster = mesh.shape["blk"] == 4 and mesh.shape["clus"] == 4
    return jax.shard_map(
        meet if takes_a_cluster else ring,
        mesh=mesh,
        in_specs=(
            P(("groups", "blk", "clus"), None),
            P(("groups", "blk", "clus")),
            P(("groups", "blk", "clus")),
        ),
        out_specs=P(("groups", "blk", "clus")),
        check_vma=False,
    )
```

```python
import functools

import jax
import jax.numpy as jnp
from jax import lax
from jax.experimental import pallas as pl
from jax.experimental.pallas import tpu as pltpu
from jax.sharding import PartitionSpec as P

CAP = 64
EPS = 1e-06
sentinel_id = 1 << 30
VMEM = pl.BlockSpec(memory_space=pltpu.VMEM)


def passed_along(value, axis, by):
    size = lax.axis_size(axis)
    return lax.ppermute(value, axis, [(i, (i + by) % size) for i in range(size)])


def ring(embeddings, cluster, row_ids):
    owners = lax.axis_size("clus")
    loop_size = lax.axis_size("blk")
    feature_width = embeddings.shape[1]
    slot_count = owners * CAP
    values = embeddings.astype(jnp.float32)
    unit_rows = (
        values
        * lax.rsqrt(jnp.mean(values * values, axis=1, keepdims=True) + EPS)
        * feature_width ** (-0.5)
    ).astype(jnp.bfloat16)
    onehot = (cluster[:, None] == jnp.arange(owners, dtype=jnp.int32)[None, :]).astype(jnp.int32)
    before = jnp.cumsum(onehot, axis=0) - onehot
    position = jnp.sum(before * onehot, axis=1)
    target = cluster * CAP + position
    send_unit = jnp.zeros((slot_count, feature_width), jnp.bfloat16).at[target].set(unit_rows)
    send_ids = jnp.full((slot_count,), sentinel_id, jnp.int32).at[target].set(row_ids)
    exchange = functools.partial(
        lax.all_to_all, axis_name="clus", split_axis=0, concat_axis=0, tiled=True
    )
    keys_unit = exchange(send_unit.reshape(owners, CAP, feature_width)).reshape(
        slot_count, feature_width
    )
    keys_ids = exchange(send_ids.reshape(owners, CAP)).reshape(slot_count)

    def absorb(best_now, other_unit, other_ids):
        scores = lax.dot_general(
            keys_unit, other_unit, (((1,), (1,)), ((), ())), preferred_element_type=jnp.float32
        )
        allowed = other_ids[None, :] < keys_ids[:, None]
        return jnp.maximum(best_now, jnp.max(jnp.where(allowed, scores, -1.0), axis=1))

    start_best = jnp.full((slot_count,), -1.0, jnp.float32)

    def advance(step_index, state_now):
        best_now, moving_unit, moving_ids = state_now
        moving_unit, moving_ids = passed_along((moving_unit, moving_ids), "blk", 1)
        return (absorb(best_now, moving_unit, moving_ids), moving_unit, moving_ids)

    best_sim, _, _ = lax.fori_loop(
        0, loop_size - 1, advance, (absorb(start_best, keys_unit, keys_ids), keys_unit, keys_ids)
    )
    returned = exchange(best_sim.reshape(owners, CAP)).reshape(slot_count)
    return returned[target]


SLABS_ROWS = 2 * CAP
SMALL = pltpu.CompilerParams(vmem_limit_bytes=8 << 20)


def middle_of(core):
    return 1 + core


NEAR = (0, (((1, 0), (0, 0)), ((2, 1), (3, 1))))
ACROSS = (2, (((1, 0), (1, 1)), ((2, 1), (2, 0))))
FAR = (3, (((1, 0), (0, 1)), ((2, 1), (3, 0))))
BLOCKS = (
    (0, None), (0, FAR), (0, ACROSS), (0, NEAR), (1, None), (1, FAR), (1, ACROSS), (1, NEAR),
)


def blk_of(far_blk, core):
    return far_blk if core == 0 else 3 - far_blk


def here():
    u = lax.axis_index("clus")
    b = lax.axis_index("blk")
    return u, b


def put_slabs(ref, start, rows):
    for t in range(rows.shape[1] // 128):
        ref[pl.ds(start + t * SLABS_ROWS, rows.shape[0]), :] = rows[:, t * 128 : (t + 1) * 128]


def get_slabs(ref, start, count, slabs):
    return jnp.concatenate(
        [ref[t * SLABS_ROWS + start : t * SLABS_ROWS + start + count, :] for t in range(slabs)], axis=1
    )


def sort_kernel(emb_ref, cluster_ref, ids_ref, keep_ref, give_ref, target_ref):
    rows, width = emb_ref.shape
    slots = 4 * CAP
    u, _ = here()
    cluster = cluster_ref[...]
    slot = cluster ^ u
    onehot = lax.broadcasted_iota(jnp.int32, (8, rows), 0) == slot
    earlier = (
        lax.broadcasted_iota(jnp.int32, (rows, rows), 0)
        < lax.broadcasted_iota(jnp.int32, (rows, rows), 1)
    ).astype(jnp.bfloat16)
    before = jnp.dot(onehot.astype(jnp.bfloat16), earlier, preferred_element_type=jnp.float32)
    position = jnp.sum(jnp.where(onehot, before, 0.0), axis=0, keepdims=True).astype(jnp.int32)
    target_ref[...] = cluster * CAP + position
    order = (slot & 1) * 2 + (slot >> 1)
    place = (
        lax.broadcasted_iota(jnp.int32, (slots, rows), 0) == order * CAP + position
    ).astype(jnp.bfloat16)
    values = jnp.dot(place, emb_ref[...], preferred_element_type=jnp.float32)
    mean = jnp.mean(values * values, axis=1, keepdims=True)
    unit = (values * lax.rsqrt(mean + EPS) * width ** (-0.5)).astype(jnp.bfloat16)
    put_slabs(keep_ref, 0, unit[: 2 * CAP])
    put_slabs(give_ref, 0, unit[2 * CAP :])
    ids = ids_ref[...]
    row = lax.broadcasted_iota(jnp.int32, (16, rows), 0)
    parts = jnp.where(row == 0, ids >> 8, jnp.where(row == 1, ids & 255, 1))
    moved = lax.dot_general(
        parts.astype(jnp.float32).astype(jnp.bfloat16),
        place,
        (((1,), (1,)), ((), ())),
        preferred_element_type=jnp.float32,
    )
    row = lax.broadcasted_iota(jnp.int32, (16, slots), 0)
    moved = jnp.where((moved[2:3] == 0.0) & (row == 0), 256.0, moved).astype(jnp.bfloat16)
    tail = width // 128 * SLABS_ROWS
    keep_ref[tail : tail + 16, :] = moved[:, : 2 * CAP]
    give_ref[tail : tail + 16, :] = moved[:, 2 * CAP :]


def join_kernel(keep_ref, got_ref, near_ref, far_ref):
    u, _ = here()
    core = lax.rem(u, 2)
    tail = keep_ref.shape[0] - 16
    own_at = pl.multiple_of(core * CAP, CAP)
    other_at = pl.multiple_of((1 - core) * CAP, CAP)
    for out_ref, start in ((far_ref, CAP), (near_ref, 0)):
        for t in range(tail // SLABS_ROWS):
            base = t * SLABS_ROWS
            out_ref[pl.ds(base + own_at, CAP), :] = keep_ref[base + start : base + start + CAP, :]
            out_ref[pl.ds(base + other_at, CAP), :] = got_ref[base + start : base + start + CAP, :]
        own = keep_ref[tail:, :].astype(jnp.float32)[:, start : start + CAP]
        other = got_ref[tail:, :].astype(jnp.float32)[:, start : start + CAP]
        first = jnp.where(core == 0, own, other)
        second = jnp.where(core == 0, other, own)
        out_ref[tail:, :] = jnp.concatenate([first, second], axis=1).astype(jnp.bfloat16)


def take_in(refs, best, first, last):
    tail = refs[0].shape[0] - 16
    slabs = tail // SLABS_ROWS
    ids_of = []
    for r in refs[:last]:
        parts = r[tail:, :].astype(jnp.float32)
        ids_of.append(parts[0:1] * 256.0 + parts[1:2])
    best = list(best)
    for new in range(first, last):
        rows = get_slabs(refs[new], 0, SLABS_ROWS, slabs)
        down = jnp.broadcast_to(ids_of[new], (SLABS_ROWS, 128)).T
        own = jnp.full((SLABS_ROWS, 128), -1.0, jnp.float32)
        for start in range(0, new + 1, 2):
            group = range(start, min(start + 2, new + 1))
            others = jnp.concatenate(
                [get_slabs(refs[q], 0, SLABS_ROWS, slabs) for q in group], axis=0
            )
            scores = lax.dot_general(
                rows, others, (((1,), (1,)), ((), ())), preferred_element_type=jnp.float32
            )
            for n, q in enumerate(group):
                part = scores[:, n * 128 : (n + 1) * 128]
                own = jnp.maximum(own, jnp.where(ids_of[q] < down, part, -1.0))
                if q != new:
                    theirs = jnp.where(down < ids_of[q], part, -1.0)
                    best[q] = jnp.maximum(best[q], jnp.max(theirs, axis=0, keepdims=True))
        best.append(jnp.max(own.T, axis=0, keepdims=True))
    return best


def meet_kernel(first, last, *refs):
    block_refs, best_ref = refs[:last], refs[-1]
    u, b = here()

    @pl.when(b == middle_of(lax.rem(u, 2)))
    def _():
        known = [refs[last][q : q + 1, :] for q in range(first)]
        for q, row in enumerate(take_in(block_refs, known, first, last)):
            best_ref[q : q + 1, :] = row


def last_meet_kernel(first, last, *refs):
    block_refs, best_ref = refs[:last], refs[-1]
    u, b = here()
    core = lax.rem(u, 2)

    @pl.when(b == middle_of(core))
    def _():
        known = [refs[last][q : q + 1, :] for q in range(first)]
        for q, row in enumerate(take_in(block_refs, known, first, last)):
            other, place = BLOCKS[q]
            at_blk = b if place is None else jnp.where(core == 0, place[0], 3 - place[0])
            chip = (u >> 1) ^ other
            for c in range(2):
                best_ref[at_blk * 4 + chip * 2 + c] = row


def home_kernel(got_ref, target_ref, out_ref):
    u, _ = here()
    core = lax.rem(u, 2)
    slots = 4 * CAP
    rows = target_ref.shape[1]
    pieces = []
    for c in range(4):
        row = got_ref[middle_of(c % 2) * 4 + c]
        pieces.append(jnp.where(core == 0, row[:, :CAP], row[:, CAP:]))
    best = jnp.concatenate(pieces, axis=1)
    high = best.astype(jnp.bfloat16).astype(jnp.float32)
    rest = best - high
    middle_part = rest.astype(jnp.bfloat16).astype(jnp.float32)
    low = rest - middle_part
    row = lax.broadcasted_iota(jnp.int32, (8, slots), 0)
    parts = jnp.where(row == 0, high, jnp.where(row == 1, middle_part, jnp.where(row == 2, low, 0.0)))
    place = lax.broadcasted_iota(jnp.int32, (slots, rows), 0) == target_ref[...]
    moved = jnp.dot(
        parts.astype(jnp.bfloat16), place.astype(jnp.bfloat16), preferred_element_type=jnp.float32
    )
    out_ref[...] = moved[0:1] + moved[1:2] + moved[2:3]


def meet(embeddings, cluster, row_ids):
    rows, width = embeddings.shape
    everyone = ("blk", "clus")
    payload = jax.ShapeDtypeStruct((width // 128 * SLABS_ROWS + 16, 128), jnp.bfloat16)

    def to_meeting(value, place):
        far_blk, others = place
        moves = [((blk_of(far_blk, core), core), (middle_of(core), core)) for core in range(2)]
        moves += others
        sent = {source for source, _ in moves}
        moves += [((b, core),) * 2 for b in range(4) for core in range(2) if (b, core) not in sent]
        pairs = [
            (sb * 4 + chip * 2 + sc, tb * 4 + chip * 2 + tc)
            for (sb, sc), (tb, tc) in moves
            for chip in range(2)
        ]
        return lax.ppermute(value, everyone, pairs)

    keep, give, target = pl.pallas_call(
        sort_kernel,
        out_shape=[payload, payload, jax.ShapeDtypeStruct((1, rows), jnp.int32)],
        in_specs=[VMEM] * 3,
        out_specs=[VMEM] * 3,
        compiler_params=SMALL,
        name="sort_rows",
    )(embeddings, cluster.reshape(1, rows), row_ids.reshape(1, rows))
    got = lax.ppermute(give, "clus", [(c, c ^ 1) for c in range(4)])
    near, far = pl.pallas_call(
        join_kernel,
        out_shape=[payload] * 2,
        in_specs=[VMEM] * 2,
        out_specs=[VMEM] * 2,
        compiler_params=SMALL,
        name="join_cores",
    )(keep, got)
    crossed = lax.ppermute(far, "clus", [(c, c ^ 2) for c in range(4)])
    arrived = [crossed if other else near for other, _ in BLOCKS]
    for q in (3, 2, 1, 7, 6, 5):
        arrived[q] = to_meeting(arrived[q], BLOCKS[q][1])

    def meeting(kernel, first, last, known, shape):
        return pl.pallas_call(
            functools.partial(kernel, first, last),
            out_shape=jax.ShapeDtypeStruct(shape, jnp.float32),
            in_specs=[VMEM] * (last + len(known)),
            out_specs=VMEM,
            compiler_params=SMALL,
            name=f"meet_{first}_{last}",
        )(*arrived[:last], *known)

    best = meeting(meet_kernel, 0, 5, [], (8, 128))
    best = meeting(meet_kernel, 5, 6, [best], (8, 128))
    best = meeting(meet_kernel, 6, 7, [best], (8, 128))
    best = meeting(last_meet_kernel, 7, 8, [best], (16, 1, 128))
    returned = lax.all_to_all(best, everyone, split_axis=0, concat_axis=0, tiled=True)
    out = pl.pallas_call(
        home_kernel,
        out_shape=jax.ShapeDtypeStruct((1, rows), jnp.float32),
        in_specs=[VMEM] * 2,
        out_specs=VMEM,
        compiler_params=SMALL,
        name="home_scores",
    )(returned, target)
    return out.reshape(rows)


def solution(mesh):
    takes_a_cluster = mesh.shape["blk"] == 4 and mesh.shape["clus"] == 4
    return jax.shard_map(
        meet if takes_a_cluster else ring,
        mesh=mesh,
        in_specs=(
            P(("groups", "blk", "clus"), None),
            P(("groups", "blk", "clus")),
            P(("groups", "blk", "clus")),
        ),
        out_specs=P(("groups", "blk", "clus")),
        check_vma=False,
    )
```

```python
import functools

import jax
import jax.numpy as jnp
from jax import lax
from jax.experimental import pallas as pl
from jax.experimental.pallas import tpu as pltpu
from jax.sharding import PartitionSpec as P

CAP = 64
EPS = 1e-06
sentinel_id = 1 << 30
VMEM = pl.BlockSpec(memory_space=pltpu.VMEM)


def passed_along(value, axis, by):
    size = lax.axis_size(axis)
    return lax.ppermute(value, axis, [(i, (i + by) % size) for i in range(size)])


def ring(embeddings, cluster, row_ids):
    owners = lax.axis_size("clus")
    loop_size = lax.axis_size("blk")
    feature_width = embeddings.shape[1]
    slot_count = owners * CAP
    values = embeddings.astype(jnp.float32)
    unit_rows = (
        values
        * lax.rsqrt(jnp.mean(values * values, axis=1, keepdims=True) + EPS)
        * feature_width ** (-0.5)
    ).astype(jnp.bfloat16)
    onehot = (cluster[:, None] == jnp.arange(owners, dtype=jnp.int32)[None, :]).astype(jnp.int32)
    before = jnp.cumsum(onehot, axis=0) - onehot
    position = jnp.sum(before * onehot, axis=1)
    target = cluster * CAP + position
    send_unit = jnp.zeros((slot_count, feature_width), jnp.bfloat16).at[target].set(unit_rows)
    send_ids = jnp.full((slot_count,), sentinel_id, jnp.int32).at[target].set(row_ids)
    exchange = functools.partial(
        lax.all_to_all, axis_name="clus", split_axis=0, concat_axis=0, tiled=True
    )
    keys_unit = exchange(send_unit.reshape(owners, CAP, feature_width)).reshape(
        slot_count, feature_width
    )
    keys_ids = exchange(send_ids.reshape(owners, CAP)).reshape(slot_count)

    def absorb(best_now, other_unit, other_ids):
        scores = lax.dot_general(
            keys_unit, other_unit, (((1,), (1,)), ((), ())), preferred_element_type=jnp.float32
        )
        allowed = other_ids[None, :] < keys_ids[:, None]
        return jnp.maximum(best_now, jnp.max(jnp.where(allowed, scores, -1.0), axis=1))

    start_best = jnp.full((slot_count,), -1.0, jnp.float32)

    def advance(step_index, state_now):
        best_now, moving_unit, moving_ids = state_now
        moving_unit, moving_ids = passed_along((moving_unit, moving_ids), "blk", 1)
        return (absorb(best_now, moving_unit, moving_ids), moving_unit, moving_ids)

    best_sim, _, _ = lax.fori_loop(
        0, loop_size - 1, advance, (absorb(start_best, keys_unit, keys_ids), keys_unit, keys_ids)
    )
    returned = exchange(best_sim.reshape(owners, CAP)).reshape(slot_count)
    return returned[target]


SLABS_ROWS = 2 * CAP
SMALL = pltpu.CompilerParams(vmem_limit_bytes=8 << 20)


def middle_of(core):
    return 1 + core


NEAR, ACROSS, FAR = 0, 2, 3
BLOCKS = (
    (0, None), (1, None), (0, FAR), (0, ACROSS), (1, FAR), (0, NEAR), (1, ACROSS), (1, NEAR),
)


def blk_of(far_blk, core):
    return far_blk if core == 0 else 3 - far_blk


def here():
    u = lax.axis_index("clus")
    b = lax.axis_index("blk")
    return u, b


def put_slabs(ref, start, rows):
    for t in range(rows.shape[1] // 128):
        ref[pl.ds(start + t * SLABS_ROWS, rows.shape[0]), :] = rows[:, t * 128 : (t + 1) * 128]


def get_slabs(ref, start, count, slabs):
    return jnp.concatenate(
        [ref[t * SLABS_ROWS + start : t * SLABS_ROWS + start + count, :] for t in range(slabs)], axis=1
    )


def sort_kernel(emb_ref, cluster_ref, ids_ref, keep_ref, give_ref, target_ref):
    rows, width = emb_ref.shape
    slots = 4 * CAP
    u, _ = here()
    cluster = cluster_ref[...]
    slot = cluster ^ u
    onehot = lax.broadcasted_iota(jnp.int32, (8, rows), 0) == slot
    earlier = (
        lax.broadcasted_iota(jnp.int32, (rows, rows), 0)
        < lax.broadcasted_iota(jnp.int32, (rows, rows), 1)
    ).astype(jnp.bfloat16)
    before = jnp.dot(onehot.astype(jnp.bfloat16), earlier, preferred_element_type=jnp.float32)
    position = jnp.sum(jnp.where(onehot, before, 0.0), axis=0, keepdims=True).astype(jnp.int32)
    target_ref[...] = cluster * CAP + position
    order = (slot & 1) * 2 + (slot >> 1)
    place = (
        lax.broadcasted_iota(jnp.int32, (slots, rows), 0) == order * CAP + position
    ).astype(jnp.bfloat16)
    values = jnp.dot(place, emb_ref[...], preferred_element_type=jnp.float32)
    mean = jnp.mean(values * values, axis=1, keepdims=True)
    unit = (values * lax.rsqrt(mean + EPS) * width ** (-0.5)).astype(jnp.bfloat16)
    put_slabs(keep_ref, 0, unit[: 2 * CAP])
    put_slabs(give_ref, 0, unit[2 * CAP :])
    ids = ids_ref[...]
    row = lax.broadcasted_iota(jnp.int32, (16, rows), 0)
    parts = jnp.where(row == 0, ids >> 8, jnp.where(row == 1, ids & 255, 1))
    moved = lax.dot_general(
        parts.astype(jnp.float32).astype(jnp.bfloat16),
        place,
        (((1,), (1,)), ((), ())),
        preferred_element_type=jnp.float32,
    )
    row = lax.broadcasted_iota(jnp.int32, (16, slots), 0)
    moved = jnp.where((moved[2:3] == 0.0) & (row == 0), 256.0, moved).astype(jnp.bfloat16)
    tail = width // 128 * SLABS_ROWS
    keep_ref[tail : tail + 16, :] = moved[:, : 2 * CAP]
    give_ref[tail : tail + 16, :] = moved[:, 2 * CAP :]


def join_kernel(keep_ref, got_ref, near_ref, far_ref):
    u, _ = here()
    core = lax.rem(u, 2)
    tail = keep_ref.shape[0] - 16
    own_at = pl.multiple_of(core * CAP, CAP)
    other_at = pl.multiple_of((1 - core) * CAP, CAP)
    for out_ref, start in ((far_ref, CAP), (near_ref, 0)):
        for t in range(tail // SLABS_ROWS):
            base = t * SLABS_ROWS
            out_ref[pl.ds(base + own_at, CAP), :] = keep_ref[base + start : base + start + CAP, :]
            out_ref[pl.ds(base + other_at, CAP), :] = got_ref[base + start : base + start + CAP, :]
        own = keep_ref[tail:, :].astype(jnp.float32)[:, start : start + CAP]
        other = got_ref[tail:, :].astype(jnp.float32)[:, start : start + CAP]
        first = jnp.where(core == 0, own, other)
        second = jnp.where(core == 0, other, own)
        out_ref[tail:, :] = jnp.concatenate([first, second], axis=1).astype(jnp.bfloat16)


def take_in(refs, best, first, last):
    tail = refs[0].shape[0] - 16
    slabs = tail // SLABS_ROWS
    ids_of = []
    for r in refs[:last]:
        parts = r[tail:, :].astype(jnp.float32)
        ids_of.append(parts[0:1] * 256.0 + parts[1:2])
    best = list(best)
    for new in range(first, last):
        rows = get_slabs(refs[new], 0, SLABS_ROWS, slabs)
        down = jnp.broadcast_to(ids_of[new], (SLABS_ROWS, 128)).T
        own = jnp.full((SLABS_ROWS, 128), -1.0, jnp.float32)
        for start in range(0, new + 1, 2):
            group = range(start, min(start + 2, new + 1))
            others = jnp.concatenate(
                [get_slabs(refs[q], 0, SLABS_ROWS, slabs) for q in group], axis=0
            )
            scores = lax.dot_general(
                rows, others, (((1,), (1,)), ((), ())), preferred_element_type=jnp.float32
            )
            for n, q in enumerate(group):
                part = scores[:, n * 128 : (n + 1) * 128]
                own = jnp.maximum(own, jnp.where(ids_of[q] < down, part, -1.0))
                if q != new:
                    theirs = jnp.where(down < ids_of[q], part, -1.0)
                    best[q] = jnp.maximum(best[q], jnp.max(theirs, axis=0, keepdims=True))
        best.append(jnp.max(own.T, axis=0, keepdims=True))
    return best


def meet_kernel(first, last, *refs):
    block_refs, best_ref = refs[:last], refs[-1]
    u, b = here()

    @pl.when(b == middle_of(lax.rem(u, 2)))
    def _():
        known = [refs[last][q : q + 1, :] for q in range(first)]
        for q, row in enumerate(take_in(block_refs, known, first, last)):
            best_ref[q : q + 1, :] = row


def last_meet_kernel(first, last, *refs):
    block_refs, best_ref = refs[:last], refs[-1]
    u, b = here()
    core = lax.rem(u, 2)

    @pl.when(b == middle_of(core))
    def _():
        known = [refs[last][q : q + 1, :] for q in range(first)]
        for q, row in enumerate(take_in(block_refs, known, first, last)):
            other, place = BLOCKS[q]
            at_blk = b if place is None else jnp.where(core == 0, place, 3 - place)
            chip = (u >> 1) ^ other
            for c in range(2):
                best_ref[at_blk * 4 + chip * 2 + c] = row


def home_kernel(got_ref, target_ref, out_ref):
    u, _ = here()
    core = lax.rem(u, 2)
    slots = 4 * CAP
    rows = target_ref.shape[1]
    pieces = []
    for c in range(4):
        row = got_ref[middle_of(c % 2) * 4 + c]
        pieces.append(jnp.where(core == 0, row[:, :CAP], row[:, CAP:]))
    best = jnp.concatenate(pieces, axis=1)
    high = best.astype(jnp.bfloat16).astype(jnp.float32)
    rest = best - high
    middle_part = rest.astype(jnp.bfloat16).astype(jnp.float32)
    low = rest - middle_part
    row = lax.broadcasted_iota(jnp.int32, (8, slots), 0)
    parts = jnp.where(row == 0, high, jnp.where(row == 1, middle_part, jnp.where(row == 2, low, 0.0)))
    place = lax.broadcasted_iota(jnp.int32, (slots, rows), 0) == target_ref[...]
    moved = jnp.dot(
        parts.astype(jnp.bfloat16), place.astype(jnp.bfloat16), preferred_element_type=jnp.float32
    )
    out_ref[...] = moved[0:1] + moved[1:2] + moved[2:3]


def meet(embeddings, cluster, row_ids):
    rows, width = embeddings.shape
    everyone = ("blk", "clus")
    payload = jax.ShapeDtypeStruct((width // 128 * SLABS_ROWS + 16, 128), jnp.bfloat16)

    def to_meeting(value, place, cross=0):
        pairs = [
            (blk_of(place, c % 2) * 4 + (c ^ 2 * cross), middle_of(c % 2) * 4 + c) for c in range(4)
        ]
        return lax.ppermute(value, everyone, pairs)

    keep, give, target = pl.pallas_call(
        sort_kernel,
        out_shape=[payload, payload, jax.ShapeDtypeStruct((1, rows), jnp.int32)],
        in_specs=[VMEM] * 3,
        out_specs=[VMEM] * 3,
        compiler_params=SMALL,
        name="sort_rows",
    )(embeddings, cluster.reshape(1, rows), row_ids.reshape(1, rows))
    got = lax.ppermute(give, "clus", [(c, c ^ 1) for c in range(4)])
    near, far = pl.pallas_call(
        join_kernel,
        out_shape=[payload] * 2,
        in_specs=[VMEM] * 2,
        out_specs=[VMEM] * 2,
        compiler_params=SMALL,
        name="join_cores",
    )(keep, got)
    crossed = lax.ppermute(far, "clus", [(c, c ^ 2) for c in range(4)])
    arrived = []
    for other, place in BLOCKS:
        if other and place == FAR:
            arrived.append(to_meeting(far, place, cross=1))
        else:
            value = crossed if other else near
            arrived.append(value if place is None else to_meeting(value, place))

    def meeting(kernel, first, last, known, shape):
        return pl.pallas_call(
            functools.partial(kernel, first, last),
            out_shape=jax.ShapeDtypeStruct(shape, jnp.float32),
            in_specs=[VMEM] * (last + len(known)),
            out_specs=VMEM,
            compiler_params=SMALL,
            name=f"meet_{first}_{last}",
        )(*arrived[:last], *known)

    best = meeting(meet_kernel, 0, 6, [], (8, 128))
    best = meeting(meet_kernel, 6, 7, [best], (8, 128))
    best = meeting(last_meet_kernel, 7, 8, [best], (16, 1, 128))
    returned = lax.all_to_all(best, everyone, split_axis=0, concat_axis=0, tiled=True)
    out = pl.pallas_call(
        home_kernel,
        out_shape=jax.ShapeDtypeStruct((1, rows), jnp.float32),
        in_specs=[VMEM] * 2,
        out_specs=VMEM,
        compiler_params=SMALL,
        name="home_scores",
    )(returned, target)
    return out.reshape(rows)


def solution(mesh):
    takes_a_cluster = mesh.shape["blk"] == 4 and mesh.shape["clus"] == 4
    return jax.shard_map(
        meet if takes_a_cluster else ring,
        mesh=mesh,
        in_specs=(
            P(("groups", "blk", "clus"), None),
            P(("groups", "blk", "clus")),
            P(("groups", "blk", "clus")),
        ),
        out_specs=P(("groups", "blk", "clus")),
        check_vma=False,
    )
```

```python
import functools

import jax
import jax.numpy as jnp
from jax import lax
from jax.experimental import pallas as pl
from jax.experimental.pallas import tpu as pltpu
from jax.sharding import PartitionSpec as P

CAP = 64
EPS = 1e-06
sentinel_id = 1 << 30
VMEM = pl.BlockSpec(memory_space=pltpu.VMEM)


def passed_along(value, axis, by):
    size = lax.axis_size(axis)
    return lax.ppermute(value, axis, [(i, (i + by) % size) for i in range(size)])


def ring(embeddings, cluster, row_ids):
    owners = lax.axis_size("clus")
    loop_size = lax.axis_size("blk")
    feature_width = embeddings.shape[1]
    slot_count = owners * CAP
    values = embeddings.astype(jnp.float32)
    unit_rows = (
        values
        * lax.rsqrt(jnp.mean(values * values, axis=1, keepdims=True) + EPS)
        * feature_width ** (-0.5)
    ).astype(jnp.bfloat16)
    onehot = (cluster[:, None] == jnp.arange(owners, dtype=jnp.int32)[None, :]).astype(jnp.int32)
    before = jnp.cumsum(onehot, axis=0) - onehot
    position = jnp.sum(before * onehot, axis=1)
    target = cluster * CAP + position
    send_unit = jnp.zeros((slot_count, feature_width), jnp.bfloat16).at[target].set(unit_rows)
    send_ids = jnp.full((slot_count,), sentinel_id, jnp.int32).at[target].set(row_ids)
    exchange = functools.partial(
        lax.all_to_all, axis_name="clus", split_axis=0, concat_axis=0, tiled=True
    )
    keys_unit = exchange(send_unit.reshape(owners, CAP, feature_width)).reshape(
        slot_count, feature_width
    )
    keys_ids = exchange(send_ids.reshape(owners, CAP)).reshape(slot_count)

    def absorb(best_now, other_unit, other_ids):
        scores = lax.dot_general(
            keys_unit, other_unit, (((1,), (1,)), ((), ())), preferred_element_type=jnp.float32
        )
        allowed = other_ids[None, :] < keys_ids[:, None]
        return jnp.maximum(best_now, jnp.max(jnp.where(allowed, scores, -1.0), axis=1))

    start_best = jnp.full((slot_count,), -1.0, jnp.float32)

    def advance(step_index, state_now):
        best_now, moving_unit, moving_ids = state_now
        moving_unit, moving_ids = passed_along((moving_unit, moving_ids), "blk", 1)
        return (absorb(best_now, moving_unit, moving_ids), moving_unit, moving_ids)

    best_sim, _, _ = lax.fori_loop(
        0, loop_size - 1, advance, (absorb(start_best, keys_unit, keys_ids), keys_unit, keys_ids)
    )
    returned = exchange(best_sim.reshape(owners, CAP)).reshape(slot_count)
    return returned[target]


SLABS_ROWS = 2 * CAP
SMALL = pltpu.CompilerParams(vmem_limit_bytes=8 << 20)


def middle_of(core):
    return 1 + core


NEAR, ACROSS, FAR = 0, 2, 3
BLOCKS = (
    (0, None), (1, None), (0, FAR), (0, ACROSS), (0, NEAR), (1, FAR), (1, ACROSS), (1, NEAR),
)


def blk_of(far_blk, core):
    return far_blk if core == 0 else 3 - far_blk


def here():
    u = lax.axis_index("clus")
    b = lax.axis_index("blk")
    return u, b


def put_slabs(ref, start, rows):
    for t in range(rows.shape[1] // 128):
        ref[pl.ds(start + t * SLABS_ROWS, rows.shape[0]), :] = rows[:, t * 128 : (t + 1) * 128]


def get_slabs(ref, start, count, slabs):
    return jnp.concatenate(
        [ref[t * SLABS_ROWS + start : t * SLABS_ROWS + start + count, :] for t in range(slabs)], axis=1
    )


def sort_kernel(emb_ref, cluster_ref, ids_ref, keep_ref, give_ref, target_ref):
    rows, width = emb_ref.shape
    slots = 4 * CAP
    u, _ = here()
    cluster = cluster_ref[...]
    slot = cluster ^ u
    onehot = lax.broadcasted_iota(jnp.int32, (8, rows), 0) == slot
    earlier = (
        lax.broadcasted_iota(jnp.int32, (rows, rows), 0)
        < lax.broadcasted_iota(jnp.int32, (rows, rows), 1)
    ).astype(jnp.bfloat16)
    before = jnp.dot(onehot.astype(jnp.bfloat16), earlier, preferred_element_type=jnp.float32)
    position = jnp.sum(jnp.where(onehot, before, 0.0), axis=0, keepdims=True).astype(jnp.int32)
    target_ref[...] = cluster * CAP + position
    order = (slot & 1) * 2 + (slot >> 1)
    place = (
        lax.broadcasted_iota(jnp.int32, (slots, rows), 0) == order * CAP + position
    ).astype(jnp.bfloat16)
    values = jnp.dot(place, emb_ref[...], preferred_element_type=jnp.float32)
    mean = jnp.mean(values * values, axis=1, keepdims=True)
    unit = (values * lax.rsqrt(mean + EPS) * width ** (-0.5)).astype(jnp.bfloat16)
    put_slabs(keep_ref, 0, unit[: 2 * CAP])
    put_slabs(give_ref, 0, unit[2 * CAP :])
    ids = ids_ref[...]
    row = lax.broadcasted_iota(jnp.int32, (16, rows), 0)
    parts = jnp.where(row == 0, ids >> 8, jnp.where(row == 1, ids & 255, 1))
    moved = lax.dot_general(
        parts.astype(jnp.float32).astype(jnp.bfloat16),
        place,
        (((1,), (1,)), ((), ())),
        preferred_element_type=jnp.float32,
    )
    row = lax.broadcasted_iota(jnp.int32, (16, slots), 0)
    moved = jnp.where((moved[2:3] == 0.0) & (row == 0), 256.0, moved).astype(jnp.bfloat16)
    tail = width // 128 * SLABS_ROWS
    keep_ref[tail : tail + 16, :] = moved[:, : 2 * CAP]
    give_ref[tail : tail + 16, :] = moved[:, 2 * CAP :]


def join_kernel(keep_ref, got_ref, *out_refs):
    u, _ = here()
    core = lax.rem(u, 2)
    tail = keep_ref.shape[0] - 16
    own_at = pl.multiple_of(core * CAP, CAP)
    other_at = pl.multiple_of((1 - core) * CAP, CAP)
    for out_ref, start in zip(out_refs, (0, CAP) * 2):
        for t in range(tail // SLABS_ROWS):
            base = t * SLABS_ROWS
            out_ref[pl.ds(base + own_at, CAP), :] = keep_ref[base + start : base + start + CAP, :]
            out_ref[pl.ds(base + other_at, CAP), :] = got_ref[base + start : base + start + CAP, :]
        own = keep_ref[tail:, :].astype(jnp.float32)[:, start : start + CAP]
        other = got_ref[tail:, :].astype(jnp.float32)[:, start : start + CAP]
        first = jnp.where(core == 0, own, other)
        second = jnp.where(core == 0, other, own)
        out_ref[tail:, :] = jnp.concatenate([first, second], axis=1).astype(jnp.bfloat16)


def take_in(refs, best, first, last):
    tail = refs[0].shape[0] - 16
    slabs = tail // SLABS_ROWS
    ids_of = []
    for r in refs[:last]:
        parts = r[tail:, :].astype(jnp.float32)
        ids_of.append(parts[0:1] * 256.0 + parts[1:2])
    best = list(best)
    for new in range(first, last):
        rows = get_slabs(refs[new], 0, SLABS_ROWS, slabs)
        down = jnp.broadcast_to(ids_of[new], (SLABS_ROWS, 128)).T
        own = jnp.full((SLABS_ROWS, 128), -1.0, jnp.float32)
        for start in range(0, new + 1, 2):
            group = range(start, min(start + 2, new + 1))
            others = jnp.concatenate(
                [get_slabs(refs[q], 0, SLABS_ROWS, slabs) for q in group], axis=0
            )
            scores = lax.dot_general(
                rows, others, (((1,), (1,)), ((), ())), preferred_element_type=jnp.float32
            )
            for n, q in enumerate(group):
                part = scores[:, n * 128 : (n + 1) * 128]
                own = jnp.maximum(own, jnp.where(ids_of[q] < down, part, -1.0))
                if q != new:
                    theirs = jnp.where(down < ids_of[q], part, -1.0)
                    best[q] = jnp.maximum(best[q], jnp.max(theirs, axis=0, keepdims=True))
        best.append(jnp.max(own.T, axis=0, keepdims=True))
    return best


def meet_kernel(first, last, *refs):
    block_refs, best_ref = refs[:last], refs[-1]
    u, b = here()

    @pl.when(b == middle_of(lax.rem(u, 2)))
    def _():
        known = [refs[last][q : q + 1, :] for q in range(first)]
        for q, row in enumerate(take_in(block_refs, known, first, last)):
            best_ref[q : q + 1, :] = row


def last_meet_kernel(first, last, *refs):
    block_refs, best_ref = refs[:last], refs[-1]
    u, b = here()
    core = lax.rem(u, 2)

    @pl.when(b == middle_of(core))
    def _():
        known = [refs[last][q : q + 1, :] for q in range(first)]
        for q, row in enumerate(take_in(block_refs, known, first, last)):
            other, place = BLOCKS[q]
            at_blk = b if place is None else jnp.where(core == 0, place, 3 - place)
            chip = (u >> 1) ^ other
            for c in range(2):
                best_ref[at_blk * 4 + chip * 2 + c] = row


def home_kernel(got_ref, target_ref, out_ref):
    u, _ = here()
    core = lax.rem(u, 2)
    slots = 4 * CAP
    rows = target_ref.shape[1]
    pieces = []
    for c in range(4):
        row = got_ref[middle_of(c % 2) * 4 + c]
        pieces.append(jnp.where(core == 0, row[:, :CAP], row[:, CAP:]))
    best = jnp.concatenate(pieces, axis=1)
    high = best.astype(jnp.bfloat16).astype(jnp.float32)
    rest = best - high
    middle_part = rest.astype(jnp.bfloat16).astype(jnp.float32)
    low = rest - middle_part
    row = lax.broadcasted_iota(jnp.int32, (8, slots), 0)
    parts = jnp.where(row == 0, high, jnp.where(row == 1, middle_part, jnp.where(row == 2, low, 0.0)))
    place = lax.broadcasted_iota(jnp.int32, (slots, rows), 0) == target_ref[...]
    moved = jnp.dot(
        parts.astype(jnp.bfloat16), place.astype(jnp.bfloat16), preferred_element_type=jnp.float32
    )
    out_ref[...] = moved[0:1] + moved[1:2] + moved[2:3]


def meet(embeddings, cluster, row_ids):
    rows, width = embeddings.shape
    everyone = ("blk", "clus")
    payload = jax.ShapeDtypeStruct((width // 128 * SLABS_ROWS + 16, 128), jnp.bfloat16)

    def to_meeting(value, place, cross=0):
        pairs = [
            (blk_of(place, c % 2) * 4 + (c ^ 2 * cross), middle_of(c % 2) * 4 + c) for c in range(4)
        ]
        return lax.ppermute(value, everyone, pairs)

    keep, give, target = pl.pallas_call(
        sort_kernel,
        out_shape=[payload, payload, jax.ShapeDtypeStruct((1, rows), jnp.int32)],
        in_specs=[VMEM] * 3,
        out_specs=[VMEM] * 3,
        compiler_params=SMALL,
        name="sort_rows",
    )(embeddings, cluster.reshape(1, rows), row_ids.reshape(1, rows))
    got = lax.ppermute(give, "clus", [(c, c ^ 1) for c in range(4)])
    near, direct, first, far = pl.pallas_call(
        join_kernel,
        out_shape=[payload] * 4,
        in_specs=[VMEM] * 2,
        out_specs=[VMEM] * 4,
        compiler_params=SMALL,
        name="join_cores",
    )(keep, got)
    crossed = lax.ppermute(far, "clus", [(c, c ^ 2) for c in range(4)])
    arrived = []
    for other, place in BLOCKS:
        if other and place == FAR:
            arrived.append(to_meeting(direct, place, cross=1))
        elif not other and place == NEAR:
            arrived.append(to_meeting(first, place))
        else:
            value = crossed if other else near
            arrived.append(value if place is None else to_meeting(value, place))

    def meeting(kernel, first, last, known, shape):
        return pl.pallas_call(
            functools.partial(kernel, first, last),
            out_shape=jax.ShapeDtypeStruct(shape, jnp.float32),
            in_specs=[VMEM] * (last + len(known)),
            out_specs=VMEM,
            compiler_params=SMALL,
            name=f"meet_{first}_{last}",
        )(*arrived[:last], *known)

    best = meeting(meet_kernel, 0, 6, [], (8, 128))
    best = meeting(meet_kernel, 6, 7, [best], (8, 128))
    best = meeting(last_meet_kernel, 7, 8, [best], (16, 1, 128))
    returned = lax.all_to_all(best, everyone, split_axis=0, concat_axis=0, tiled=True)
    out = pl.pallas_call(
        home_kernel,
        out_shape=jax.ShapeDtypeStruct((1, rows), jnp.float32),
        in_specs=[VMEM] * 2,
        out_specs=VMEM,
        compiler_params=SMALL,
        name="home_scores",
    )(returned, target)
    return out.reshape(rows)


def solution(mesh):
    takes_a_cluster = mesh.shape["blk"] == 4 and mesh.shape["clus"] == 4
    return jax.shard_map(
        meet if takes_a_cluster else ring,
        mesh=mesh,
        in_specs=(
            P(("groups", "blk", "clus"), None),
            P(("groups", "blk", "clus")),
            P(("groups", "blk", "clus")),
        ),
        out_specs=P(("groups", "blk", "clus")),
        check_vma=False,
    )
```

```python
import functools

import jax
import jax.numpy as jnp
from jax import lax
from jax.experimental import pallas as pl
from jax.experimental.pallas import tpu as pltpu
from jax.sharding import PartitionSpec as P

CAP = 64
EPS = 1e-06
sentinel_id = 1 << 30
VMEM = pl.BlockSpec(memory_space=pltpu.VMEM)


def passed_along(value, axis, by):
    size = lax.axis_size(axis)
    return lax.ppermute(value, axis, [(i, (i + by) % size) for i in range(size)])


def ring(embeddings, cluster, row_ids):
    owners = lax.axis_size("clus")
    loop_size = lax.axis_size("blk")
    feature_width = embeddings.shape[1]
    slot_count = owners * CAP
    values = embeddings.astype(jnp.float32)
    unit_rows = (
        values
        * lax.rsqrt(jnp.mean(values * values, axis=1, keepdims=True) + EPS)
        * feature_width ** (-0.5)
    ).astype(jnp.bfloat16)
    onehot = (cluster[:, None] == jnp.arange(owners, dtype=jnp.int32)[None, :]).astype(jnp.int32)
    before = jnp.cumsum(onehot, axis=0) - onehot
    position = jnp.sum(before * onehot, axis=1)
    target = cluster * CAP + position
    send_unit = jnp.zeros((slot_count, feature_width), jnp.bfloat16).at[target].set(unit_rows)
    send_ids = jnp.full((slot_count,), sentinel_id, jnp.int32).at[target].set(row_ids)
    exchange = functools.partial(
        lax.all_to_all, axis_name="clus", split_axis=0, concat_axis=0, tiled=True
    )
    keys_unit = exchange(send_unit.reshape(owners, CAP, feature_width)).reshape(
        slot_count, feature_width
    )
    keys_ids = exchange(send_ids.reshape(owners, CAP)).reshape(slot_count)

    def absorb(best_now, other_unit, other_ids):
        scores = lax.dot_general(
            keys_unit, other_unit, (((1,), (1,)), ((), ())), preferred_element_type=jnp.float32
        )
        allowed = other_ids[None, :] < keys_ids[:, None]
        return jnp.maximum(best_now, jnp.max(jnp.where(allowed, scores, -1.0), axis=1))

    start_best = jnp.full((slot_count,), -1.0, jnp.float32)

    def advance(step_index, state_now):
        best_now, moving_unit, moving_ids = state_now
        moving_unit, moving_ids = passed_along((moving_unit, moving_ids), "blk", 1)
        return (absorb(best_now, moving_unit, moving_ids), moving_unit, moving_ids)

    best_sim, _, _ = lax.fori_loop(
        0, loop_size - 1, advance, (absorb(start_best, keys_unit, keys_ids), keys_unit, keys_ids)
    )
    returned = exchange(best_sim.reshape(owners, CAP)).reshape(slot_count)
    return returned[target]


SLABS_ROWS = 2 * CAP
SMALL = pltpu.CompilerParams(vmem_limit_bytes=8 << 20)


def middle_of(core):
    return 1 + core


NEAR, ACROSS, FAR = 0, 2, 3
BLOCKS = (
    (0, None), (1, None), (0, NEAR), (0, ACROSS), (0, FAR), (1, FAR), (1, ACROSS), (1, NEAR),
)


def blk_of(far_blk, core):
    return far_blk if core == 0 else 3 - far_blk


def here():
    u = lax.axis_index("clus")
    b = lax.axis_index("blk")
    return u, b


def put_slabs(ref, start, rows):
    for t in range(rows.shape[1] // 128):
        ref[pl.ds(start + t * SLABS_ROWS, rows.shape[0]), :] = rows[:, t * 128 : (t + 1) * 128]


def get_slabs(ref, start, count, slabs):
    return jnp.concatenate(
        [ref[t * SLABS_ROWS + start : t * SLABS_ROWS + start + count, :] for t in range(slabs)], axis=1
    )


def sort_kernel(emb_ref, cluster_ref, ids_ref, keep_ref, give_ref, target_ref):
    rows, width = emb_ref.shape
    slots = 4 * CAP
    u, _ = here()
    cluster = cluster_ref[...]
    slot = cluster ^ u
    onehot = lax.broadcasted_iota(jnp.int32, (8, rows), 0) == slot
    earlier = (
        lax.broadcasted_iota(jnp.int32, (rows, rows), 0)
        < lax.broadcasted_iota(jnp.int32, (rows, rows), 1)
    ).astype(jnp.bfloat16)
    before = jnp.dot(onehot.astype(jnp.bfloat16), earlier, preferred_element_type=jnp.float32)
    position = jnp.sum(jnp.where(onehot, before, 0.0), axis=0, keepdims=True).astype(jnp.int32)
    target_ref[...] = cluster * CAP + position
    order = (slot & 1) * 2 + (slot >> 1)
    place = (
        lax.broadcasted_iota(jnp.int32, (slots, rows), 0) == order * CAP + position
    ).astype(jnp.bfloat16)
    values = jnp.dot(place, emb_ref[...], preferred_element_type=jnp.float32)
    mean = jnp.mean(values * values, axis=1, keepdims=True)
    unit = (values * lax.rsqrt(mean + EPS) * width ** (-0.5)).astype(jnp.bfloat16)
    put_slabs(keep_ref, 0, unit[: 2 * CAP])
    put_slabs(give_ref, 0, unit[2 * CAP :])
    ids = ids_ref[...]
    row = lax.broadcasted_iota(jnp.int32, (16, rows), 0)
    parts = jnp.where(row == 0, ids >> 8, jnp.where(row == 1, ids & 255, 1))
    moved = lax.dot_general(
        parts.astype(jnp.float32).astype(jnp.bfloat16),
        place,
        (((1,), (1,)), ((), ())),
        preferred_element_type=jnp.float32,
    )
    row = lax.broadcasted_iota(jnp.int32, (16, slots), 0)
    moved = jnp.where((moved[2:3] == 0.0) & (row == 0), 256.0, moved).astype(jnp.bfloat16)
    tail = width // 128 * SLABS_ROWS
    keep_ref[tail : tail + 16, :] = moved[:, : 2 * CAP]
    give_ref[tail : tail + 16, :] = moved[:, 2 * CAP :]


def join_kernel(keep_ref, got_ref, *out_refs):
    u, _ = here()
    core = lax.rem(u, 2)
    tail = keep_ref.shape[0] - 16
    own_at = pl.multiple_of(core * CAP, CAP)
    other_at = pl.multiple_of((1 - core) * CAP, CAP)
    for out_ref, start in zip(out_refs, (0, CAP) * 2):
        for t in range(tail // SLABS_ROWS):
            base = t * SLABS_ROWS
            out_ref[pl.ds(base + own_at, CAP), :] = keep_ref[base + start : base + start + CAP, :]
            out_ref[pl.ds(base + other_at, CAP), :] = got_ref[base + start : base + start + CAP, :]
        own = keep_ref[tail:, :].astype(jnp.float32)[:, start : start + CAP]
        other = got_ref[tail:, :].astype(jnp.float32)[:, start : start + CAP]
        first = jnp.where(core == 0, own, other)
        second = jnp.where(core == 0, other, own)
        out_ref[tail:, :] = jnp.concatenate([first, second], axis=1).astype(jnp.bfloat16)


def take_in(refs, best, first, last):
    tail = refs[0].shape[0] - 16
    slabs = tail // SLABS_ROWS
    ids_of = []
    for r in refs[:last]:
        parts = r[tail:, :].astype(jnp.float32)
        ids_of.append(parts[0:1] * 256.0 + parts[1:2])
    best = list(best)
    for new in range(first, last):
        rows = get_slabs(refs[new], 0, SLABS_ROWS, slabs)
        down = jnp.broadcast_to(ids_of[new], (SLABS_ROWS, 128)).T
        own = jnp.full((SLABS_ROWS, 128), -1.0, jnp.float32)
        for start in range(0, new + 1, 2):
            group = range(start, min(start + 2, new + 1))
            others = jnp.concatenate(
                [get_slabs(refs[q], 0, SLABS_ROWS, slabs) for q in group], axis=0
            )
            scores = lax.dot_general(
                rows, others, (((1,), (1,)), ((), ())), preferred_element_type=jnp.float32
            )
            for n, q in enumerate(group):
                part = scores[:, n * 128 : (n + 1) * 128]
                own = jnp.maximum(own, jnp.where(ids_of[q] < down, part, -1.0))
                if q != new:
                    theirs = jnp.where(down < ids_of[q], part, -1.0)
                    best[q] = jnp.maximum(best[q], jnp.max(theirs, axis=0, keepdims=True))
        best.append(jnp.max(own.T, axis=0, keepdims=True))
    return best


def meet_kernel(first, last, *refs):
    block_refs, best_ref = refs[:last], refs[-1]
    u, b = here()

    @pl.when(b == middle_of(lax.rem(u, 2)))
    def _():
        known = [refs[last][q : q + 1, :] for q in range(first)]
        for q, row in enumerate(take_in(block_refs, known, first, last)):
            best_ref[q : q + 1, :] = row


def last_meet_kernel(first, last, *refs):
    block_refs, best_ref = refs[:last], refs[-1]
    u, b = here()
    core = lax.rem(u, 2)

    @pl.when(b == middle_of(core))
    def _():
        known = [refs[last][q : q + 1, :] for q in range(first)]
        for q, row in enumerate(take_in(block_refs, known, first, last)):
            other, place = BLOCKS[q]
            at_blk = b if place is None else jnp.where(core == 0, place, 3 - place)
            chip = (u >> 1) ^ other
            for c in range(2):
                best_ref[at_blk * 4 + chip * 2 + c] = row


def home_kernel(got_ref, target_ref, out_ref):
    u, _ = here()
    core = lax.rem(u, 2)
    slots = 4 * CAP
    rows = target_ref.shape[1]
    pieces = []
    for c in range(4):
        row = got_ref[middle_of(c % 2) * 4 + c]
        pieces.append(jnp.where(core == 0, row[:, :CAP], row[:, CAP:]))
    best = jnp.concatenate(pieces, axis=1)
    high = best.astype(jnp.bfloat16).astype(jnp.float32)
    rest = best - high
    middle_part = rest.astype(jnp.bfloat16).astype(jnp.float32)
    low = rest - middle_part
    row = lax.broadcasted_iota(jnp.int32, (8, slots), 0)
    parts = jnp.where(row == 0, high, jnp.where(row == 1, middle_part, jnp.where(row == 2, low, 0.0)))
    place = lax.broadcasted_iota(jnp.int32, (slots, rows), 0) == target_ref[...]
    moved = jnp.dot(
        parts.astype(jnp.bfloat16), place.astype(jnp.bfloat16), preferred_element_type=jnp.float32
    )
    out_ref[...] = moved[0:1] + moved[1:2] + moved[2:3]


def meet(embeddings, cluster, row_ids):
    rows, width = embeddings.shape
    everyone = ("blk", "clus")
    payload = jax.ShapeDtypeStruct((width // 128 * SLABS_ROWS + 16, 128), jnp.bfloat16)

    def to_meeting(value, place, cross=0):
        pairs = [
            (blk_of(place, c % 2) * 4 + (c ^ 2 * cross), middle_of(c % 2) * 4 + c) for c in range(4)
        ]
        return lax.ppermute(value, everyone, pairs)

    keep, give, target = pl.pallas_call(
        sort_kernel,
        out_shape=[payload, payload, jax.ShapeDtypeStruct((1, rows), jnp.int32)],
        in_specs=[VMEM] * 3,
        out_specs=[VMEM] * 3,
        compiler_params=SMALL,
        name="sort_rows",
    )(embeddings, cluster.reshape(1, rows), row_ids.reshape(1, rows))
    got = lax.ppermute(give, "clus", [(c, c ^ 1) for c in range(4)])
    near, direct, first, far = pl.pallas_call(
        join_kernel,
        out_shape=[payload] * 4,
        in_specs=[VMEM] * 2,
        out_specs=[VMEM] * 4,
        compiler_params=SMALL,
        name="join_cores",
    )(keep, got)
    crossed = lax.ppermute(far, "clus", [(c, c ^ 2) for c in range(4)])
    arrived = []
    for other, place in BLOCKS:
        if other and place == FAR:
            arrived.append(to_meeting(direct, place, cross=1))
        elif not other and place == FAR:
            arrived.append(to_meeting(first, place))
        else:
            value = crossed if other else near
            arrived.append(value if place is None else to_meeting(value, place))

    def meeting(kernel, first, last, known, shape):
        return pl.pallas_call(
            functools.partial(kernel, first, last),
            out_shape=jax.ShapeDtypeStruct(shape, jnp.float32),
            in_specs=[VMEM] * (last + len(known)),
            out_specs=VMEM,
            compiler_params=SMALL,
            name=f"meet_{first}_{last}",
        )(*arrived[:last], *known)

    best = meeting(meet_kernel, 0, 6, [], (8, 128))
    best = meeting(meet_kernel, 6, 7, [best], (8, 128))
    best = meeting(last_meet_kernel, 7, 8, [best], (16, 1, 128))
    returned = lax.all_to_all(best, everyone, split_axis=0, concat_axis=0, tiled=True)
    out = pl.pallas_call(
        home_kernel,
        out_shape=jax.ShapeDtypeStruct((1, rows), jnp.float32),
        in_specs=[VMEM] * 2,
        out_specs=VMEM,
        compiler_params=SMALL,
        name="home_scores",
    )(returned, target)
    return out.reshape(rows)


def solution(mesh):
    takes_a_cluster = mesh.shape["blk"] == 4 and mesh.shape["clus"] == 4
    return jax.shard_map(
        meet if takes_a_cluster else ring,
        mesh=mesh,
        in_specs=(
            P(("groups", "blk", "clus"), None),
            P(("groups", "blk", "clus")),
            P(("groups", "blk", "clus")),
        ),
        out_specs=P(("groups", "blk", "clus")),
        check_vma=False,
    )
```

```python
import functools

import jax
import jax.numpy as jnp
from jax import lax
from jax.experimental import pallas as pl
from jax.experimental.pallas import tpu as pltpu
from jax.sharding import PartitionSpec as P

CAP = 64
EPS = 1e-06
sentinel_id = 1 << 30
VMEM = pl.BlockSpec(memory_space=pltpu.VMEM)


def passed_along(value, axis, by):
    size = lax.axis_size(axis)
    return lax.ppermute(value, axis, [(i, (i + by) % size) for i in range(size)])


def ring(embeddings, cluster, row_ids):
    owners = lax.axis_size("clus")
    loop_size = lax.axis_size("blk")
    feature_width = embeddings.shape[1]
    slot_count = owners * CAP
    values = embeddings.astype(jnp.float32)
    unit_rows = (
        values
        * lax.rsqrt(jnp.mean(values * values, axis=1, keepdims=True) + EPS)
        * feature_width ** (-0.5)
    ).astype(jnp.bfloat16)
    onehot = (cluster[:, None] == jnp.arange(owners, dtype=jnp.int32)[None, :]).astype(jnp.int32)
    before = jnp.cumsum(onehot, axis=0) - onehot
    position = jnp.sum(before * onehot, axis=1)
    target = cluster * CAP + position
    send_unit = jnp.zeros((slot_count, feature_width), jnp.bfloat16).at[target].set(unit_rows)
    send_ids = jnp.full((slot_count,), sentinel_id, jnp.int32).at[target].set(row_ids)
    exchange = functools.partial(
        lax.all_to_all, axis_name="clus", split_axis=0, concat_axis=0, tiled=True
    )
    keys_unit = exchange(send_unit.reshape(owners, CAP, feature_width)).reshape(
        slot_count, feature_width
    )
    keys_ids = exchange(send_ids.reshape(owners, CAP)).reshape(slot_count)

    def absorb(best_now, other_unit, other_ids):
        scores = lax.dot_general(
            keys_unit, other_unit, (((1,), (1,)), ((), ())), preferred_element_type=jnp.float32
        )
        allowed = other_ids[None, :] < keys_ids[:, None]
        return jnp.maximum(best_now, jnp.max(jnp.where(allowed, scores, -1.0), axis=1))

    start_best = jnp.full((slot_count,), -1.0, jnp.float32)

    def advance(step_index, state_now):
        best_now, moving_unit, moving_ids = state_now
        moving_unit, moving_ids = passed_along((moving_unit, moving_ids), "blk", 1)
        return (absorb(best_now, moving_unit, moving_ids), moving_unit, moving_ids)

    best_sim, _, _ = lax.fori_loop(
        0, loop_size - 1, advance, (absorb(start_best, keys_unit, keys_ids), keys_unit, keys_ids)
    )
    returned = exchange(best_sim.reshape(owners, CAP)).reshape(slot_count)
    return returned[target]


SLABS_ROWS = 2 * CAP
SMALL = pltpu.CompilerParams(vmem_limit_bytes=8 << 20)


def middle_of(core):
    return 1 + core


NEAR, ACROSS, FAR = 0, 2, 3
BLOCKS = (
    (0, None), (1, None), (0, FAR), (1, FAR), (0, NEAR), (0, ACROSS), (1, NEAR), (1, ACROSS),
)


def blk_of(far_blk, core):
    return far_blk if core == 0 else 3 - far_blk


def here():
    u = lax.axis_index("clus")
    b = lax.axis_index("blk")
    return u, b


def put_slabs(ref, rows):
    for t in range(rows.shape[1] // 128):
        ref[t * SLABS_ROWS : (t + 1) * SLABS_ROWS, :] = rows[:, t * 128 : (t + 1) * 128]


def get_slabs(ref):
    slabs = (ref.shape[0] - 16) // SLABS_ROWS
    return jnp.concatenate(
        [ref[t * SLABS_ROWS : (t + 1) * SLABS_ROWS, :] for t in range(slabs)], axis=1
    )


def sorted_rows(emb_ref, cluster_ref, ids_ref):
    rows, width = emb_ref.shape
    slots = 2 * CAP
    u, _ = here()
    cluster = cluster_ref[...]
    onehot = lax.broadcasted_iota(jnp.int32, (8, rows), 0) == cluster
    earlier = (
        lax.broadcasted_iota(jnp.int32, (rows, rows), 0)
        < lax.broadcasted_iota(jnp.int32, (rows, rows), 1)
    ).astype(jnp.bfloat16)
    before = jnp.dot(onehot.astype(jnp.bfloat16), earlier, preferred_element_type=jnp.float32)
    position = jnp.sum(jnp.where(onehot, before, 0.0), axis=0, keepdims=True).astype(jnp.int32)
    start = jnp.where(cluster == u, 0, jnp.where(cluster == u ^ 2, CAP, -4 * CAP))
    place = (
        lax.broadcasted_iota(jnp.int32, (slots, rows), 0) == start + position
    ).astype(jnp.bfloat16)
    values = jnp.dot(place, emb_ref[...], preferred_element_type=jnp.float32)
    mean = jnp.mean(values * values, axis=1, keepdims=True)
    unit = (values * lax.rsqrt(mean + EPS) * width ** (-0.5)).astype(jnp.bfloat16)
    ids = ids_ref[...]
    row = lax.broadcasted_iota(jnp.int32, (16, rows), 0)
    parts = jnp.where(row == 0, ids >> 8, jnp.where(row == 1, ids & 255, 1))
    moved = lax.dot_general(
        parts.astype(jnp.float32).astype(jnp.bfloat16),
        place,
        (((1,), (1,)), ((), ())),
        preferred_element_type=jnp.float32,
    )
    row = lax.broadcasted_iota(jnp.int32, (16, slots), 0)
    moved = jnp.where((moved[2:3] == 0.0) & (row == 0), 256.0, moved)
    return unit, moved, cluster * CAP + position


def sort_kernel(emb_ref, cluster_ref, ids_ref, keep_ref, target_ref):
    unit, moved, target = sorted_rows(emb_ref, cluster_ref, ids_ref)
    put_slabs(keep_ref, unit)
    keep_ref[keep_ref.shape[0] - 16 :, :] = moved.astype(jnp.bfloat16)
    target_ref[...] = target


def join_kernel(keep_ref, emb_ref, cluster_ref, ids_ref, *out_refs):
    unit, moved, _ = sorted_rows(emb_ref, cluster_ref, ids_ref)
    u, _ = here()
    core = lax.rem(u, 2)
    tail = keep_ref.shape[0] - 16
    own_at = pl.multiple_of(core * CAP, CAP)
    other_at = pl.multiple_of((1 - core) * CAP, CAP)
    kept = keep_ref[tail:, :].astype(jnp.float32)
    for out_ref, start in zip(out_refs, (0, CAP) * 2):
        for t in range(tail // SLABS_ROWS):
            base = t * SLABS_ROWS
            out_ref[pl.ds(base + own_at, CAP), :] = keep_ref[base + start : base + start + CAP, :]
            out_ref[pl.ds(base + other_at, CAP), :] = unit[
                start : start + CAP, t * 128 : (t + 1) * 128
            ]
        own = kept[:, start : start + CAP]
        other = moved[:, start : start + CAP]
        pieces = [jnp.where(core == 0, own, other), jnp.where(core == 0, other, own)]
        out_ref[tail:, :] = jnp.concatenate(pieces, axis=1).astype(jnp.bfloat16)


def take_in(refs, best, first, last):
    tail = refs[0].shape[0] - 16
    ids_of = []
    for r in refs[:last]:
        parts = r[tail:, :].astype(jnp.float32)
        ids_of.append(parts[0:1] * 256.0 + parts[1:2])
    best = list(best)

    def pair(q):
        return jnp.concatenate([get_slabs(refs[q]), get_slabs(refs[q + 1])], axis=0)

    for new in range(first, last, 2):
        rows = pair(new)
        down = jnp.concatenate(
            [jnp.broadcast_to(ids_of[q], (SLABS_ROWS, 128)).T for q in (new, new + 1)], axis=0
        )
        own = jnp.full((2 * SLABS_ROWS, 128), -1.0, jnp.float32)
        for start in range(0, new + 1, 2):
            scores = lax.dot_general(
                rows, pair(start), (((1,), (1,)), ((), ())), preferred_element_type=jnp.float32
            )
            for n in range(2):
                q = start + n
                part = scores[:, n * 128 : (n + 1) * 128]
                own = jnp.maximum(own, jnp.where(ids_of[q] < down, part, -1.0))
                if start != new:
                    theirs = jnp.where(down < ids_of[q], part, -1.0)
                    best[q] = jnp.maximum(best[q], jnp.max(theirs, axis=0, keepdims=True))
        for n in range(2):
            side = own[n * SLABS_ROWS : (n + 1) * SLABS_ROWS]
            best.append(jnp.max(side.T, axis=0, keepdims=True))
    return best


def meet_kernel(first, last, *refs):
    block_refs, best_ref = refs[:last], refs[-1]
    u, b = here()

    @pl.when(b == middle_of(lax.rem(u, 2)))
    def _():
        known = [refs[last][q : q + 1, :] for q in range(first)]
        for q, row in enumerate(take_in(block_refs, known, first, last)):
            best_ref[q : q + 1, :] = row


def last_meet_kernel(first, last, *refs):
    block_refs, best_ref = refs[:last], refs[-1]
    u, b = here()
    core = lax.rem(u, 2)

    @pl.when(b == middle_of(core))
    def _():
        known = [refs[last][q : q + 1, :] for q in range(first)]
        for q, row in enumerate(take_in(block_refs, known, first, last)):
            other, place = BLOCKS[q]
            at_blk = b if place is None else jnp.where(core == 0, place, 3 - place)
            chip = (u >> 1) ^ other
            for c in range(2):
                best_ref[at_blk * 4 + chip * 2 + c] = row


def home_kernel(got_ref, target_ref, out_ref):
    u, _ = here()
    core = lax.rem(u, 2)
    slots = 4 * CAP
    rows = target_ref.shape[1]
    pieces = []
    for c in range(4):
        row = got_ref[middle_of(c % 2) * 4 + c]
        pieces.append(jnp.where(core == 0, row[:, :CAP], row[:, CAP:]))
    best = jnp.concatenate(pieces, axis=1)
    high = best.astype(jnp.bfloat16).astype(jnp.float32)
    rest = best - high
    middle_part = rest.astype(jnp.bfloat16).astype(jnp.float32)
    low = rest - middle_part
    row = lax.broadcasted_iota(jnp.int32, (8, slots), 0)
    parts = jnp.where(row == 0, high, jnp.where(row == 1, middle_part, jnp.where(row == 2, low, 0.0)))
    place = lax.broadcasted_iota(jnp.int32, (slots, rows), 0) == target_ref[...]
    moved = jnp.dot(
        parts.astype(jnp.bfloat16), place.astype(jnp.bfloat16), preferred_element_type=jnp.float32
    )
    out_ref[...] = moved[0:1] + moved[1:2] + moved[2:3]


def meet(embeddings, cluster, row_ids):
    rows, width = embeddings.shape
    everyone = ("blk", "clus")
    payload = jax.ShapeDtypeStruct((width // 128 * SLABS_ROWS + 16, 128), jnp.bfloat16)

    def to_meeting(value, place, cross=0):
        pairs = [
            (blk_of(place, c % 2) * 4 + (c ^ 2 * cross), middle_of(c % 2) * 4 + c) for c in range(4)
        ]
        return lax.ppermute(value, everyone, pairs)

    raw = (embeddings, cluster, row_ids)
    swapped = [lax.ppermute(value, "clus", [(c, c ^ 1) for c in range(4)]) for value in raw]

    def flat(values):
        return [values[0], values[1].reshape(1, rows), values[2].reshape(1, rows)]

    keep, target = pl.pallas_call(
        sort_kernel,
        out_shape=[payload, jax.ShapeDtypeStruct((1, rows), jnp.int32)],
        in_specs=[VMEM] * 3,
        out_specs=[VMEM] * 2,
        compiler_params=SMALL,
        name="sort_rows",
    )(*flat(raw))
    near, direct, first, far = pl.pallas_call(
        join_kernel,
        out_shape=[payload] * 4,
        in_specs=[VMEM] * 4,
        out_specs=[VMEM] * 4,
        compiler_params=SMALL,
        name="join_cores",
    )(keep, *flat(swapped))
    crossed = lax.ppermute(far, "clus", [(c, c ^ 2) for c in range(4)])
    arrived = []
    for other, place in BLOCKS:
        if other and place == FAR:
            arrived.append(to_meeting(direct, place, cross=1))
        elif not other and place == FAR:
            arrived.append(to_meeting(first, place))
        else:
            value = crossed if other else near
            arrived.append(value if place is None else to_meeting(value, place))

    def meeting(kernel, first, last, known, shape):
        return pl.pallas_call(
            functools.partial(kernel, first, last),
            out_shape=jax.ShapeDtypeStruct(shape, jnp.float32),
            in_specs=[VMEM] * (last + len(known)),
            out_specs=VMEM,
            compiler_params=SMALL,
            name=f"meet_{first}_{last}",
        )(*arrived[:last], *known)

    best = meeting(meet_kernel, 0, 4, [], (8, 128))
    best = meeting(meet_kernel, 4, 6, [best], (8, 128))
    best = meeting(last_meet_kernel, 6, 8, [best], (16, 1, 128))
    returned = lax.all_to_all(best, everyone, split_axis=0, concat_axis=0, tiled=True)
    out = pl.pallas_call(
        home_kernel,
        out_shape=jax.ShapeDtypeStruct((1, rows), jnp.float32),
        in_specs=[VMEM] * 2,
        out_specs=VMEM,
        compiler_params=SMALL,
        name="home_scores",
    )(returned, target)
    return out.reshape(rows)


def solution(mesh):
    takes_a_cluster = mesh.shape["blk"] == 4 and mesh.shape["clus"] == 4
    return jax.shard_map(
        meet if takes_a_cluster else ring,
        mesh=mesh,
        in_specs=(
            P(("groups", "blk", "clus"), None),
            P(("groups", "blk", "clus")),
            P(("groups", "blk", "clus")),
        ),
        out_specs=P(("groups", "blk", "clus")),
        check_vma=False,
    )
```

```python
import functools

import jax
import jax.numpy as jnp
from jax import lax
from jax.experimental import pallas as pl
from jax.experimental.pallas import tpu as pltpu
from jax.sharding import PartitionSpec as P

CAP = 64
EPS = 1e-06
sentinel_id = 1 << 30
VMEM = pl.BlockSpec(memory_space=pltpu.VMEM)


def passed_along(value, axis, by):
    size = lax.axis_size(axis)
    return lax.ppermute(value, axis, [(i, (i + by) % size) for i in range(size)])


def ring(embeddings, cluster, row_ids):
    owners = lax.axis_size("clus")
    loop_size = lax.axis_size("blk")
    feature_width = embeddings.shape[1]
    slot_count = owners * CAP
    values = embeddings.astype(jnp.float32)
    unit_rows = (
        values
        * lax.rsqrt(jnp.mean(values * values, axis=1, keepdims=True) + EPS)
        * feature_width ** (-0.5)
    ).astype(jnp.bfloat16)
    onehot = (cluster[:, None] == jnp.arange(owners, dtype=jnp.int32)[None, :]).astype(jnp.int32)
    before = jnp.cumsum(onehot, axis=0) - onehot
    position = jnp.sum(before * onehot, axis=1)
    target = cluster * CAP + position
    send_unit = jnp.zeros((slot_count, feature_width), jnp.bfloat16).at[target].set(unit_rows)
    send_ids = jnp.full((slot_count,), sentinel_id, jnp.int32).at[target].set(row_ids)
    exchange = functools.partial(
        lax.all_to_all, axis_name="clus", split_axis=0, concat_axis=0, tiled=True
    )
    keys_unit = exchange(send_unit.reshape(owners, CAP, feature_width)).reshape(
        slot_count, feature_width
    )
    keys_ids = exchange(send_ids.reshape(owners, CAP)).reshape(slot_count)

    def absorb(best_now, other_unit, other_ids):
        scores = lax.dot_general(
            keys_unit, other_unit, (((1,), (1,)), ((), ())), preferred_element_type=jnp.float32
        )
        allowed = other_ids[None, :] < keys_ids[:, None]
        return jnp.maximum(best_now, jnp.max(jnp.where(allowed, scores, -1.0), axis=1))

    start_best = jnp.full((slot_count,), -1.0, jnp.float32)

    def advance(step_index, state_now):
        best_now, moving_unit, moving_ids = state_now
        moving_unit, moving_ids = passed_along((moving_unit, moving_ids), "blk", 1)
        return (absorb(best_now, moving_unit, moving_ids), moving_unit, moving_ids)

    best_sim, _, _ = lax.fori_loop(
        0, loop_size - 1, advance, (absorb(start_best, keys_unit, keys_ids), keys_unit, keys_ids)
    )
    returned = exchange(best_sim.reshape(owners, CAP)).reshape(slot_count)
    return returned[target]


SLABS_ROWS = 2 * CAP
SMALL = pltpu.CompilerParams(vmem_limit_bytes=8 << 20)


def middle_of(core):
    return 1 + core


NEAR, ACROSS, FAR = 0, 2, 3
BLOCKS = (
    (0, None), (0, FAR), (1, FAR), (1, None), (0, NEAR), (0, ACROSS), (1, NEAR), (1, ACROSS),
)


def blk_of(far_blk, core):
    return far_blk if core == 0 else 3 - far_blk


def here():
    u = lax.axis_index("clus")
    b = lax.axis_index("blk")
    return u, b


def put_slabs(ref, rows):
    for t in range(rows.shape[1] // 128):
        ref[t * SLABS_ROWS : (t + 1) * SLABS_ROWS, :] = rows[:, t * 128 : (t + 1) * 128]


def get_slabs(ref):
    slabs = (ref.shape[0] - 16) // SLABS_ROWS
    return jnp.concatenate(
        [ref[t * SLABS_ROWS : (t + 1) * SLABS_ROWS, :] for t in range(slabs)], axis=1
    )


def sorted_rows(emb_ref, cluster_ref, ids_ref):
    rows, width = emb_ref.shape
    slots = 2 * CAP
    u, _ = here()
    cluster = cluster_ref[...]
    onehot = lax.broadcasted_iota(jnp.int32, (8, rows), 0) == cluster
    earlier = (
        lax.broadcasted_iota(jnp.int32, (rows, rows), 0)
        < lax.broadcasted_iota(jnp.int32, (rows, rows), 1)
    ).astype(jnp.bfloat16)
    before = jnp.dot(onehot.astype(jnp.bfloat16), earlier, preferred_element_type=jnp.float32)
    position = jnp.sum(jnp.where(onehot, before, 0.0), axis=0, keepdims=True).astype(jnp.int32)
    start = jnp.where(cluster == u, 0, jnp.where(cluster == u ^ 2, CAP, -4 * CAP))
    place = (
        lax.broadcasted_iota(jnp.int32, (slots, rows), 0) == start + position
    ).astype(jnp.bfloat16)
    values = jnp.dot(place, emb_ref[...], preferred_element_type=jnp.float32)
    mean = jnp.mean(values * values, axis=1, keepdims=True)
    unit = (values * lax.rsqrt(mean + EPS) * width ** (-0.5)).astype(jnp.bfloat16)
    ids = ids_ref[...]
    row = lax.broadcasted_iota(jnp.int32, (16, rows), 0)
    parts = jnp.where(row == 0, ids >> 8, jnp.where(row == 1, ids & 255, 1))
    moved = lax.dot_general(
        parts.astype(jnp.float32).astype(jnp.bfloat16),
        place,
        (((1,), (1,)), ((), ())),
        preferred_element_type=jnp.float32,
    )
    row = lax.broadcasted_iota(jnp.int32, (16, slots), 0)
    moved = jnp.where((moved[2:3] == 0.0) & (row == 0), 256.0, moved)
    return unit, moved, cluster * CAP + position


def sort_kernel(emb_ref, cluster_ref, ids_ref, keep_ref, target_ref):
    unit, moved, target = sorted_rows(emb_ref, cluster_ref, ids_ref)
    put_slabs(keep_ref, unit)
    keep_ref[keep_ref.shape[0] - 16 :, :] = moved.astype(jnp.bfloat16)
    target_ref[...] = target


def join_kernel(keep_ref, emb_ref, cluster_ref, ids_ref, *out_refs):
    unit, moved, _ = sorted_rows(emb_ref, cluster_ref, ids_ref)
    u, _ = here()
    core = lax.rem(u, 2)
    tail = keep_ref.shape[0] - 16
    own_at = pl.multiple_of(core * CAP, CAP)
    other_at = pl.multiple_of((1 - core) * CAP, CAP)
    kept = keep_ref[tail:, :].astype(jnp.float32)
    for out_ref, start in zip(out_refs, (0, CAP) * 2):
        for t in range(tail // SLABS_ROWS):
            base = t * SLABS_ROWS
            out_ref[pl.ds(base + own_at, CAP), :] = keep_ref[base + start : base + start + CAP, :]
            out_ref[pl.ds(base + other_at, CAP), :] = unit[
                start : start + CAP, t * 128 : (t + 1) * 128
            ]
        own = kept[:, start : start + CAP]
        other = moved[:, start : start + CAP]
        pieces = [jnp.where(core == 0, own, other), jnp.where(core == 0, other, own)]
        out_ref[tail:, :] = jnp.concatenate(pieces, axis=1).astype(jnp.bfloat16)


def take_in(refs, best, first, last):
    tail = refs[0].shape[0] - 16
    ids_of = []
    for r in refs[:last]:
        parts = r[tail:, :].astype(jnp.float32)
        ids_of.append(parts[0:1] * 256.0 + parts[1:2])
    best = list(best)

    def pair(q):
        return jnp.concatenate([get_slabs(refs[q]), get_slabs(refs[q + 1])], axis=0)

    for new in range(first, last, 2):
        rows = pair(new)
        down = jnp.concatenate(
            [jnp.broadcast_to(ids_of[q], (SLABS_ROWS, 128)).T for q in (new, new + 1)], axis=0
        )
        own = jnp.full((2 * SLABS_ROWS, 128), -1.0, jnp.float32)
        for start in range(0, new + 1, 2):
            scores = lax.dot_general(
                rows, pair(start), (((1,), (1,)), ((), ())), preferred_element_type=jnp.float32
            )
            for n in range(2):
                q = start + n
                part = scores[:, n * 128 : (n + 1) * 128]
                own = jnp.maximum(own, jnp.where(ids_of[q] < down, part, -1.0))
                if start != new:
                    theirs = jnp.where(down < ids_of[q], part, -1.0)
                    best[q] = jnp.maximum(best[q], jnp.max(theirs, axis=0, keepdims=True))
        for n in range(2):
            side = own[n * SLABS_ROWS : (n + 1) * SLABS_ROWS]
            best.append(jnp.max(side.T, axis=0, keepdims=True))
    return best


def meet_kernel(first, last, *refs):
    block_refs, best_ref = refs[:last], refs[-1]
    u, b = here()

    @pl.when(b == middle_of(lax.rem(u, 2)))
    def _():
        known = [refs[last][q : q + 1, :] for q in range(first)]
        for q, row in enumerate(take_in(block_refs, known, first, last)):
            best_ref[q : q + 1, :] = row


def last_meet_kernel(first, last, *refs):
    block_refs, best_ref = refs[:last], refs[-1]
    u, b = here()
    core = lax.rem(u, 2)

    @pl.when(b == middle_of(core))
    def _():
        known = [refs[last][q : q + 1, :] for q in range(first)]
        for q, row in enumerate(take_in(block_refs, known, first, last)):
            other, place = BLOCKS[q]
            at_blk = b if place is None else jnp.where(core == 0, place, 3 - place)
            chip = (u >> 1) ^ other
            for c in range(2):
                best_ref[at_blk * 4 + chip * 2 + c] = row


def after_kernel(_, value_ref, out_ref):
    pass


def home_kernel(got_ref, target_ref, out_ref):
    u, _ = here()
    core = lax.rem(u, 2)
    slots = 4 * CAP
    rows = target_ref.shape[1]
    pieces = []
    for c in range(4):
        row = got_ref[middle_of(c % 2) * 4 + c]
        pieces.append(jnp.where(core == 0, row[:, :CAP], row[:, CAP:]))
    best = jnp.concatenate(pieces, axis=1)
    high = best.astype(jnp.bfloat16).astype(jnp.float32)
    rest = best - high
    middle_part = rest.astype(jnp.bfloat16).astype(jnp.float32)
    low = rest - middle_part
    row = lax.broadcasted_iota(jnp.int32, (8, slots), 0)
    parts = jnp.where(row == 0, high, jnp.where(row == 1, middle_part, jnp.where(row == 2, low, 0.0)))
    place = lax.broadcasted_iota(jnp.int32, (slots, rows), 0) == target_ref[...]
    moved = jnp.dot(
        parts.astype(jnp.bfloat16), place.astype(jnp.bfloat16), preferred_element_type=jnp.float32
    )
    out_ref[...] = moved[0:1] + moved[1:2] + moved[2:3]


def meet(embeddings, cluster, row_ids):
    rows, width = embeddings.shape
    everyone = ("blk", "clus")
    payload = jax.ShapeDtypeStruct((width // 128 * SLABS_ROWS + 16, 128), jnp.bfloat16)

    def to_meeting(value, place, cross=0):
        pairs = [
            (blk_of(place, c % 2) * 4 + (c ^ 2 * cross), middle_of(c % 2) * 4 + c) for c in range(4)
        ]
        return lax.ppermute(value, everyone, pairs)

    raw = (embeddings, cluster, row_ids)
    swapped = [lax.ppermute(value, "clus", [(c, c ^ 1) for c in range(4)]) for value in raw]

    def flat(values):
        return [values[0], values[1].reshape(1, rows), values[2].reshape(1, rows)]

    keep, target = pl.pallas_call(
        sort_kernel,
        out_shape=[payload, jax.ShapeDtypeStruct((1, rows), jnp.int32)],
        in_specs=[VMEM] * 3,
        out_specs=[VMEM] * 2,
        compiler_params=SMALL,
        name="sort_rows",
    )(*flat(raw))
    near, direct, first, far = pl.pallas_call(
        join_kernel,
        out_shape=[payload] * 4,
        in_specs=[VMEM] * 4,
        out_specs=[VMEM] * 4,
        compiler_params=SMALL,
        name="join_cores",
    )(keep, *flat(swapped))
    crossed = lax.ppermute(far, "clus", [(c, c ^ 2) for c in range(4)])
    def meeting(kernel, first, last, known, shape):
        return pl.pallas_call(
            functools.partial(kernel, first, last),
            out_shape=jax.ShapeDtypeStruct(shape, jnp.float32),
            in_specs=[VMEM] * (last + len(known)),
            out_specs=VMEM,
            compiler_params=SMALL,
            name=f"meet_{first}_{last}",
        )(*arrived[:last], *known)

    arrived = [near, to_meeting(first, FAR)]
    best = meeting(meet_kernel, 0, 2, [], (8, 128))
    crossed = pl.pallas_call(
        after_kernel,
        out_shape=payload,
        in_specs=[pl.BlockSpec(memory_space=pl.ANY)] * 2,
        out_specs=pl.BlockSpec(memory_space=pl.ANY),
        input_output_aliases={1: 0},
        compiler_params=SMALL,
        name="after_far",
    )(best, crossed)
    arrived += [to_meeting(direct, FAR, cross=1), crossed]
    arrived += [to_meeting(near, NEAR), to_meeting(near, ACROSS)]
    arrived += [to_meeting(crossed, NEAR), to_meeting(crossed, ACROSS)]
    best = meeting(meet_kernel, 2, 4, [best], (8, 128))
    best = meeting(meet_kernel, 4, 6, [best], (8, 128))
    best = meeting(last_meet_kernel, 6, 8, [best], (16, 1, 128))
    returned = lax.all_to_all(best, everyone, split_axis=0, concat_axis=0, tiled=True)
    out = pl.pallas_call(
        home_kernel,
        out_shape=jax.ShapeDtypeStruct((1, rows), jnp.float32),
        in_specs=[VMEM] * 2,
        out_specs=VMEM,
        compiler_params=SMALL,
        name="home_scores",
    )(returned, target)
    return out.reshape(rows)


def solution(mesh):
    takes_a_cluster = mesh.shape["blk"] == 4 and mesh.shape["clus"] == 4
    return jax.shard_map(
        meet if takes_a_cluster else ring,
        mesh=mesh,
        in_specs=(
            P(("groups", "blk", "clus"), None),
            P(("groups", "blk", "clus")),
            P(("groups", "blk", "clus")),
        ),
        out_specs=P(("groups", "blk", "clus")),
        check_vma=False,
    )
```

```python
import functools

import jax
import jax.numpy as jnp
from jax import lax
from jax.experimental import pallas as pl
from jax.experimental.pallas import tpu as pltpu
from jax.sharding import PartitionSpec as P

CAP = 64
EPS = 1e-06
sentinel_id = 1 << 30
VMEM = pl.BlockSpec(memory_space=pltpu.VMEM)


def passed_along(value, axis, by):
    size = lax.axis_size(axis)
    return lax.ppermute(value, axis, [(i, (i + by) % size) for i in range(size)])


def ring(embeddings, cluster, row_ids):
    owners = lax.axis_size("clus")
    loop_size = lax.axis_size("blk")
    feature_width = embeddings.shape[1]
    slot_count = owners * CAP
    values = embeddings.astype(jnp.float32)
    unit_rows = (
        values
        * lax.rsqrt(jnp.mean(values * values, axis=1, keepdims=True) + EPS)
        * feature_width ** (-0.5)
    ).astype(jnp.bfloat16)
    onehot = (cluster[:, None] == jnp.arange(owners, dtype=jnp.int32)[None, :]).astype(jnp.int32)
    before = jnp.cumsum(onehot, axis=0) - onehot
    position = jnp.sum(before * onehot, axis=1)
    target = cluster * CAP + position
    send_unit = jnp.zeros((slot_count, feature_width), jnp.bfloat16).at[target].set(unit_rows)
    send_ids = jnp.full((slot_count,), sentinel_id, jnp.int32).at[target].set(row_ids)
    exchange = functools.partial(
        lax.all_to_all, axis_name="clus", split_axis=0, concat_axis=0, tiled=True
    )
    keys_unit = exchange(send_unit.reshape(owners, CAP, feature_width)).reshape(
        slot_count, feature_width
    )
    keys_ids = exchange(send_ids.reshape(owners, CAP)).reshape(slot_count)

    def absorb(best_now, other_unit, other_ids):
        scores = lax.dot_general(
            keys_unit, other_unit, (((1,), (1,)), ((), ())), preferred_element_type=jnp.float32
        )
        allowed = other_ids[None, :] < keys_ids[:, None]
        return jnp.maximum(best_now, jnp.max(jnp.where(allowed, scores, -1.0), axis=1))

    start_best = jnp.full((slot_count,), -1.0, jnp.float32)

    def advance(step_index, state_now):
        best_now, moving_unit, moving_ids = state_now
        moving_unit, moving_ids = passed_along((moving_unit, moving_ids), "blk", 1)
        return (absorb(best_now, moving_unit, moving_ids), moving_unit, moving_ids)

    best_sim, _, _ = lax.fori_loop(
        0, loop_size - 1, advance, (absorb(start_best, keys_unit, keys_ids), keys_unit, keys_ids)
    )
    returned = exchange(best_sim.reshape(owners, CAP)).reshape(slot_count)
    return returned[target]


SLABS_ROWS = 2 * CAP
SMALL = pltpu.CompilerParams(vmem_limit_bytes=8 << 20)


def middle_of(core):
    return 1 + core


NEAR, ACROSS, FAR = 0, 2, 3
BLOCKS = (
    (0, None), (1, None), (0, FAR), (1, FAR), (0, NEAR), (1, ACROSS), (0, ACROSS), (1, NEAR),
)


def blk_of(far_blk, core):
    return far_blk if core == 0 else 3 - far_blk


def here():
    u = lax.axis_index("clus")
    b = lax.axis_index("blk")
    return u, b


def put_slabs(ref, rows):
    for t in range(rows.shape[1] // 128):
        ref[t * SLABS_ROWS : (t + 1) * SLABS_ROWS, :] = rows[:, t * 128 : (t + 1) * 128]


def get_slabs(ref):
    slabs = (ref.shape[0] - 16) // SLABS_ROWS
    return jnp.concatenate(
        [ref[t * SLABS_ROWS : (t + 1) * SLABS_ROWS, :] for t in range(slabs)], axis=1
    )


def sorted_rows(emb_ref, cluster_ref, ids_ref):
    rows, width = emb_ref.shape
    slots = 2 * CAP
    u, _ = here()
    cluster = cluster_ref[...]
    onehot = lax.broadcasted_iota(jnp.int32, (8, rows), 0) == cluster
    earlier = (
        lax.broadcasted_iota(jnp.int32, (rows, rows), 0)
        < lax.broadcasted_iota(jnp.int32, (rows, rows), 1)
    ).astype(jnp.bfloat16)
    before = jnp.dot(onehot.astype(jnp.bfloat16), earlier, preferred_element_type=jnp.float32)
    position = jnp.sum(jnp.where(onehot, before, 0.0), axis=0, keepdims=True).astype(jnp.int32)
    start = jnp.where(cluster == u, 0, jnp.where(cluster == u ^ 2, CAP, -4 * CAP))
    place = (
        lax.broadcasted_iota(jnp.int32, (slots, rows), 0) == start + position
    ).astype(jnp.bfloat16)
    values = jnp.dot(place, emb_ref[...], preferred_element_type=jnp.float32)
    mean = jnp.mean(values * values, axis=1, keepdims=True)
    unit = (values * lax.rsqrt(mean + EPS) * width ** (-0.5)).astype(jnp.bfloat16)
    ids = ids_ref[...]
    row = lax.broadcasted_iota(jnp.int32, (16, rows), 0)
    parts = jnp.where(row == 0, ids >> 8, jnp.where(row == 1, ids & 255, 1))
    moved = lax.dot_general(
        parts.astype(jnp.float32).astype(jnp.bfloat16),
        place,
        (((1,), (1,)), ((), ())),
        preferred_element_type=jnp.float32,
    )
    row = lax.broadcasted_iota(jnp.int32, (16, slots), 0)
    moved = jnp.where((moved[2:3] == 0.0) & (row == 0), 256.0, moved)
    return unit, moved, cluster * CAP + position


def sort_kernel(emb_ref, cluster_ref, ids_ref, keep_ref, target_ref):
    unit, moved, target = sorted_rows(emb_ref, cluster_ref, ids_ref)
    put_slabs(keep_ref, unit)
    keep_ref[keep_ref.shape[0] - 16 :, :] = moved.astype(jnp.bfloat16)
    target_ref[...] = target


def join_kernel(keep_ref, emb_ref, cluster_ref, ids_ref, *out_refs):
    unit, moved, _ = sorted_rows(emb_ref, cluster_ref, ids_ref)
    u, _ = here()
    core = lax.rem(u, 2)
    tail = keep_ref.shape[0] - 16
    own_at = pl.multiple_of(core * CAP, CAP)
    other_at = pl.multiple_of((1 - core) * CAP, CAP)
    kept = keep_ref[tail:, :].astype(jnp.float32)
    for out_ref, start in zip(out_refs, (0, CAP) * 2):
        for t in range(tail // SLABS_ROWS):
            base = t * SLABS_ROWS
            out_ref[pl.ds(base + own_at, CAP), :] = keep_ref[base + start : base + start + CAP, :]
            out_ref[pl.ds(base + other_at, CAP), :] = unit[
                start : start + CAP, t * 128 : (t + 1) * 128
            ]
        own = kept[:, start : start + CAP]
        other = moved[:, start : start + CAP]
        pieces = [jnp.where(core == 0, own, other), jnp.where(core == 0, other, own)]
        out_ref[tail:, :] = jnp.concatenate(pieces, axis=1).astype(jnp.bfloat16)


def take_in(refs, best, first, last):
    tail = refs[0].shape[0] - 16
    ids_of = []
    for r in refs[:last]:
        parts = r[tail:, :].astype(jnp.float32)
        ids_of.append(parts[0:1] * 256.0 + parts[1:2])
    best = list(best)

    def pair(q):
        return jnp.concatenate([get_slabs(refs[q]), get_slabs(refs[q + 1])], axis=0)

    for new in range(first, last, 2):
        rows = pair(new)
        down = jnp.concatenate(
            [jnp.broadcast_to(ids_of[q], (SLABS_ROWS, 128)).T for q in (new, new + 1)], axis=0
        )
        own = jnp.full((2 * SLABS_ROWS, 128), -1.0, jnp.float32)
        for start in range(0, new + 1, 2):
            scores = lax.dot_general(
                rows, pair(start), (((1,), (1,)), ((), ())), preferred_element_type=jnp.float32
            )
            for n in range(2):
                q = start + n
                part = scores[:, n * 128 : (n + 1) * 128]
                own = jnp.maximum(own, jnp.where(ids_of[q] < down, part, -1.0))
                if start != new:
                    theirs = jnp.where(down < ids_of[q], part, -1.0)
                    best[q] = jnp.maximum(best[q], jnp.max(theirs, axis=0, keepdims=True))
        for n in range(2):
            side = own[n * SLABS_ROWS : (n + 1) * SLABS_ROWS]
            best.append(jnp.max(side.T, axis=0, keepdims=True))
    return best


def meet_kernel(first, last, *refs):
    block_refs, best_ref = refs[:last], refs[-1]
    u, b = here()

    @pl.when(b == middle_of(lax.rem(u, 2)))
    def _():
        known = [refs[last][q : q + 1, :] for q in range(first)]
        for q, row in enumerate(take_in(block_refs, known, first, last)):
            best_ref[q : q + 1, :] = row


def last_meet_kernel(first, last, *refs):
    block_refs, best_ref = refs[:last], refs[-1]
    u, b = here()
    core = lax.rem(u, 2)

    @pl.when(b == middle_of(core))
    def _():
        known = [refs[last][q : q + 1, :] for q in range(first)]
        for q, row in enumerate(take_in(block_refs, known, first, last)):
            other, place = BLOCKS[q]
            at_blk = b if place is None else jnp.where(core == 0, place, 3 - place)
            chip = (u >> 1) ^ other
            for c in range(2):
                best_ref[at_blk * 4 + chip * 2 + c] = row


def home_kernel(got_ref, target_ref, out_ref):
    u, _ = here()
    core = lax.rem(u, 2)
    slots = 4 * CAP
    rows = target_ref.shape[1]
    pieces = []
    for c in range(4):
        row = got_ref[middle_of(c % 2) * 4 + c]
        pieces.append(jnp.where(core == 0, row[:, :CAP], row[:, CAP:]))
    best = jnp.concatenate(pieces, axis=1)
    high = best.astype(jnp.bfloat16).astype(jnp.float32)
    rest = best - high
    middle_part = rest.astype(jnp.bfloat16).astype(jnp.float32)
    low = rest - middle_part
    row = lax.broadcasted_iota(jnp.int32, (8, slots), 0)
    parts = jnp.where(row == 0, high, jnp.where(row == 1, middle_part, jnp.where(row == 2, low, 0.0)))
    place = lax.broadcasted_iota(jnp.int32, (slots, rows), 0) == target_ref[...]
    moved = jnp.dot(
        parts.astype(jnp.bfloat16), place.astype(jnp.bfloat16), preferred_element_type=jnp.float32
    )
    out_ref[...] = moved[0:1] + moved[1:2] + moved[2:3]


def meet(embeddings, cluster, row_ids):
    rows, width = embeddings.shape
    everyone = ("blk", "clus")
    payload = jax.ShapeDtypeStruct((width // 128 * SLABS_ROWS + 16, 128), jnp.bfloat16)

    def to_meeting(value, place, cross=0):
        pairs = [
            (blk_of(place, c % 2) * 4 + (c ^ 2 * cross), middle_of(c % 2) * 4 + c) for c in range(4)
        ]
        return lax.ppermute(value, everyone, pairs)

    raw = (embeddings, cluster, row_ids)
    swapped = [lax.ppermute(value, "clus", [(c, c ^ 1) for c in range(4)]) for value in raw]

    def flat(values):
        return [values[0], values[1].reshape(1, rows), values[2].reshape(1, rows)]

    keep, target = pl.pallas_call(
        sort_kernel,
        out_shape=[payload, jax.ShapeDtypeStruct((1, rows), jnp.int32)],
        in_specs=[VMEM] * 3,
        out_specs=[VMEM] * 2,
        compiler_params=SMALL,
        name="sort_rows",
    )(*flat(raw))
    near, direct, first, far = pl.pallas_call(
        join_kernel,
        out_shape=[payload] * 4,
        in_specs=[VMEM] * 4,
        out_specs=[VMEM] * 4,
        compiler_params=SMALL,
        name="join_cores",
    )(keep, *flat(swapped))
    crossed = lax.ppermute(far, "clus", [(c, c ^ 2) for c in range(4)])
    arrived = []
    for other, place in BLOCKS:
        if other and place in (FAR, ACROSS):
            arrived.append(to_meeting(direct, place, cross=1))
        elif not other and place == FAR:
            arrived.append(to_meeting(first, place))
        else:
            value = crossed if other else near
            arrived.append(value if place is None else to_meeting(value, place))

    def meeting(kernel, first, last, known, shape):
        return pl.pallas_call(
            functools.partial(kernel, first, last),
            out_shape=jax.ShapeDtypeStruct(shape, jnp.float32),
            in_specs=[VMEM] * (last + len(known)),
            out_specs=VMEM,
            compiler_params=SMALL,
            name=f"meet_{first}_{last}",
        )(*arrived[:last], *known)

    best = meeting(meet_kernel, 0, 4, [], (8, 128))
    best = meeting(meet_kernel, 4, 6, [best], (8, 128))
    best = meeting(last_meet_kernel, 6, 8, [best], (16, 1, 128))
    returned = lax.all_to_all(best, everyone, split_axis=0, concat_axis=0, tiled=True)
    out = pl.pallas_call(
        home_kernel,
        out_shape=jax.ShapeDtypeStruct((1, rows), jnp.float32),
        in_specs=[VMEM] * 2,
        out_specs=VMEM,
        compiler_params=SMALL,
        name="home_scores",
    )(returned, target)
    return out.reshape(rows)


def solution(mesh):
    takes_a_cluster = mesh.shape["blk"] == 4 and mesh.shape["clus"] == 4
    return jax.shard_map(
        meet if takes_a_cluster else ring,
        mesh=mesh,
        in_specs=(
            P(("groups", "blk", "clus"), None),
            P(("groups", "blk", "clus")),
            P(("groups", "blk", "clus")),
        ),
        out_specs=P(("groups", "blk", "clus")),
        check_vma=False,
    )
```

```python
import functools

import jax
import jax.numpy as jnp
from jax import lax
from jax.experimental import pallas as pl
from jax.experimental.pallas import tpu as pltpu
from jax.sharding import PartitionSpec as P

CAP = 64
EPS = 1e-06
sentinel_id = 1 << 30
VMEM = pl.BlockSpec(memory_space=pltpu.VMEM)


def passed_along(value, axis, by):
    size = lax.axis_size(axis)
    return lax.ppermute(value, axis, [(i, (i + by) % size) for i in range(size)])


def ring(embeddings, cluster, row_ids):
    owners = lax.axis_size("clus")
    loop_size = lax.axis_size("blk")
    feature_width = embeddings.shape[1]
    slot_count = owners * CAP
    values = embeddings.astype(jnp.float32)
    unit_rows = (
        values
        * lax.rsqrt(jnp.mean(values * values, axis=1, keepdims=True) + EPS)
        * feature_width ** (-0.5)
    ).astype(jnp.bfloat16)
    onehot = (cluster[:, None] == jnp.arange(owners, dtype=jnp.int32)[None, :]).astype(jnp.int32)
    before = jnp.cumsum(onehot, axis=0) - onehot
    position = jnp.sum(before * onehot, axis=1)
    target = cluster * CAP + position
    send_unit = jnp.zeros((slot_count, feature_width), jnp.bfloat16).at[target].set(unit_rows)
    send_ids = jnp.full((slot_count,), sentinel_id, jnp.int32).at[target].set(row_ids)
    exchange = functools.partial(
        lax.all_to_all, axis_name="clus", split_axis=0, concat_axis=0, tiled=True
    )
    keys_unit = exchange(send_unit.reshape(owners, CAP, feature_width)).reshape(
        slot_count, feature_width
    )
    keys_ids = exchange(send_ids.reshape(owners, CAP)).reshape(slot_count)

    def absorb(best_now, other_unit, other_ids):
        scores = lax.dot_general(
            keys_unit, other_unit, (((1,), (1,)), ((), ())), preferred_element_type=jnp.float32
        )
        allowed = other_ids[None, :] < keys_ids[:, None]
        return jnp.maximum(best_now, jnp.max(jnp.where(allowed, scores, -1.0), axis=1))

    start_best = jnp.full((slot_count,), -1.0, jnp.float32)

    def advance(step_index, state_now):
        best_now, moving_unit, moving_ids = state_now
        moving_unit, moving_ids = passed_along((moving_unit, moving_ids), "blk", 1)
        return (absorb(best_now, moving_unit, moving_ids), moving_unit, moving_ids)

    best_sim, _, _ = lax.fori_loop(
        0, loop_size - 1, advance, (absorb(start_best, keys_unit, keys_ids), keys_unit, keys_ids)
    )
    returned = exchange(best_sim.reshape(owners, CAP)).reshape(slot_count)
    return returned[target]


SLABS_ROWS = 2 * CAP
SMALL = pltpu.CompilerParams(vmem_limit_bytes=8 << 20)


def middle_of(core):
    return 1 + core


NEAR, ACROSS, FAR = 0, 2, 3
BLOCKS = (
    (0, None), (1, None), (0, FAR), (1, FAR), (0, NEAR), (0, ACROSS), (1, NEAR), (1, ACROSS),
)


def blk_of(far_blk, core):
    return far_blk if core == 0 else 3 - far_blk


def here():
    u = lax.axis_index("clus")
    b = lax.axis_index("blk")
    return u, b


def put_slabs(ref, rows):
    for t in range(rows.shape[1] // 128):
        ref[t * SLABS_ROWS : (t + 1) * SLABS_ROWS, :] = rows[:, t * 128 : (t + 1) * 128]


def get_slabs(ref):
    slabs = (ref.shape[0] - 16) // SLABS_ROWS
    return jnp.concatenate(
        [ref[t * SLABS_ROWS : (t + 1) * SLABS_ROWS, :] for t in range(slabs)], axis=1
    )


def sorted_rows(emb_ref, cluster_ref, ids_ref):
    rows, width = emb_ref.shape
    slots = 2 * CAP
    u, _ = here()
    cluster = cluster_ref[...]
    onehot = lax.broadcasted_iota(jnp.int32, (8, rows), 0) == cluster
    earlier = (
        lax.broadcasted_iota(jnp.int32, (rows, rows), 0)
        < lax.broadcasted_iota(jnp.int32, (rows, rows), 1)
    ).astype(jnp.bfloat16)
    before = jnp.dot(onehot.astype(jnp.bfloat16), earlier, preferred_element_type=jnp.float32)
    position = jnp.sum(jnp.where(onehot, before, 0.0), axis=0, keepdims=True).astype(jnp.int32)
    start = jnp.where(cluster == u, 0, jnp.where(cluster == u ^ 2, CAP, -4 * CAP))
    place = (
        lax.broadcasted_iota(jnp.int32, (slots, rows), 0) == start + position
    ).astype(jnp.bfloat16)
    values = jnp.dot(place, emb_ref[...], preferred_element_type=jnp.float32)
    mean = jnp.mean(values * values, axis=1, keepdims=True)
    unit = (values * lax.rsqrt(mean + EPS) * width ** (-0.5)).astype(jnp.bfloat16)
    ids = ids_ref[...]
    row = lax.broadcasted_iota(jnp.int32, (16, rows), 0)
    parts = jnp.where(row == 0, ids >> 8, jnp.where(row == 1, ids & 255, 1))
    moved = lax.dot_general(
        parts.astype(jnp.float32).astype(jnp.bfloat16),
        place,
        (((1,), (1,)), ((), ())),
        preferred_element_type=jnp.float32,
    )
    row = lax.broadcasted_iota(jnp.int32, (16, slots), 0)
    moved = jnp.where((moved[2:3] == 0.0) & (row == 0), 256.0, moved)
    return unit, moved, cluster * CAP + position


def sort_kernel(emb_ref, cluster_ref, ids_ref, keep_ref, target_ref):
    unit, moved, target = sorted_rows(emb_ref, cluster_ref, ids_ref)
    put_slabs(keep_ref, unit)
    keep_ref[keep_ref.shape[0] - 16 :, :] = moved.astype(jnp.bfloat16)
    target_ref[...] = target


def join_kernel(keep_ref, emb_ref, cluster_ref, ids_ref, *out_refs):
    unit, moved, _ = sorted_rows(emb_ref, cluster_ref, ids_ref)
    u, _ = here()
    core = lax.rem(u, 2)
    tail = keep_ref.shape[0] - 16
    own_at = pl.multiple_of(core * CAP, CAP)
    other_at = pl.multiple_of((1 - core) * CAP, CAP)
    kept = keep_ref[tail:, :].astype(jnp.float32)
    for out_ref, start in zip(out_refs, (0, CAP) * 2):
        for t in range(tail // SLABS_ROWS):
            base = t * SLABS_ROWS
            out_ref[pl.ds(base + own_at, CAP), :] = keep_ref[base + start : base + start + CAP, :]
            out_ref[pl.ds(base + other_at, CAP), :] = unit[
                start : start + CAP, t * 128 : (t + 1) * 128
            ]
        own = kept[:, start : start + CAP]
        other = moved[:, start : start + CAP]
        pieces = [jnp.where(core == 0, own, other), jnp.where(core == 0, other, own)]
        out_ref[tail:, :] = jnp.concatenate(pieces, axis=1).astype(jnp.bfloat16)


def take_in(refs, best, first, last):
    tail = refs[0].shape[0] - 16
    ids_of = []
    for r in refs[:last]:
        parts = r[tail:, :].astype(jnp.float32)
        ids_of.append(parts[0:1] * 256.0 + parts[1:2])
    best = list(best)

    def pair(q):
        return jnp.concatenate([get_slabs(refs[q]), get_slabs(refs[q + 1])], axis=0)

    for new in range(first, last, 2):
        rows = pair(new)
        down = jnp.concatenate(
            [jnp.broadcast_to(ids_of[q], (SLABS_ROWS, 128)).T for q in (new, new + 1)], axis=0
        )
        own = jnp.full((2 * SLABS_ROWS, 128), -1.0, jnp.float32)
        for start in range(0, new + 1, 2):
            scores = lax.dot_general(
                rows, pair(start), (((1,), (1,)), ((), ())), preferred_element_type=jnp.float32
            )
            for n in range(2):
                q = start + n
                part = scores[:, n * 128 : (n + 1) * 128]
                own = jnp.maximum(own, jnp.where(ids_of[q] < down, part, -1.0))
                if start != new:
                    theirs = jnp.where(down < ids_of[q], part, -1.0)
                    best[q] = jnp.maximum(best[q], jnp.max(theirs, axis=0, keepdims=True))
        for n in range(2):
            side = own[n * SLABS_ROWS : (n + 1) * SLABS_ROWS]
            best.append(jnp.max(side.T, axis=0, keepdims=True))
    return best


def meet_kernel(first, last, *refs):
    block_refs, best_ref = refs[:last], refs[-1]
    u, b = here()

    @pl.when(b == middle_of(lax.rem(u, 2)))
    def _():
        known = [refs[last][q : q + 1, :] for q in range(first)]
        for q, row in enumerate(take_in(block_refs, known, first, last)):
            best_ref[q : q + 1, :] = row


def last_meet_kernel(first, last, *refs):
    block_refs, best_ref = refs[:last], refs[-1]
    u, b = here()
    core = lax.rem(u, 2)

    best_ref[...] = jnp.zeros_like(best_ref)

    @pl.when(b == middle_of(core))
    def _():
        known = [refs[last][q : q + 1, :] for q in range(first)]
        for q, row in enumerate(take_in(block_refs, known, first, last)):
            other, place = BLOCKS[q]
            at_blk = b if place is None else jnp.where(core == 0, place, 3 - place)
            chip = (u >> 1) ^ other
            best_ref[u * 8 + at_blk * 2 + chip] = row


def home_kernel(got_ref, target_ref, out_ref):
    u, b = here()
    core = lax.rem(u, 2)
    slots = 4 * CAP
    rows = target_ref.shape[1]
    pieces = []
    for c in range(4):
        row = got_ref[c * 8 + b * 2 + (u >> 1)]
        pieces.append(jnp.where(core == 0, row[:, :CAP], row[:, CAP:]))
    best = jnp.concatenate(pieces, axis=1)
    high = best.astype(jnp.bfloat16).astype(jnp.float32)
    rest = best - high
    middle_part = rest.astype(jnp.bfloat16).astype(jnp.float32)
    low = rest - middle_part
    row = lax.broadcasted_iota(jnp.int32, (8, slots), 0)
    parts = jnp.where(row == 0, high, jnp.where(row == 1, middle_part, jnp.where(row == 2, low, 0.0)))
    place = lax.broadcasted_iota(jnp.int32, (slots, rows), 0) == target_ref[...]
    moved = jnp.dot(
        parts.astype(jnp.bfloat16), place.astype(jnp.bfloat16), preferred_element_type=jnp.float32
    )
    out_ref[...] = moved[0:1] + moved[1:2] + moved[2:3]


def meet(embeddings, cluster, row_ids):
    rows, width = embeddings.shape
    everyone = ("blk", "clus")
    payload = jax.ShapeDtypeStruct((width // 128 * SLABS_ROWS + 16, 128), jnp.bfloat16)

    def to_meeting(value, place, cross=0):
        pairs = [
            (blk_of(place, c % 2) * 4 + (c ^ 2 * cross), middle_of(c % 2) * 4 + c) for c in range(4)
        ]
        return lax.ppermute(value, everyone, pairs)

    raw = (embeddings, cluster, row_ids)
    swapped = [lax.ppermute(value, "clus", [(c, c ^ 1) for c in range(4)]) for value in raw]

    def flat(values):
        return [values[0], values[1].reshape(1, rows), values[2].reshape(1, rows)]

    keep, target = pl.pallas_call(
        sort_kernel,
        out_shape=[payload, jax.ShapeDtypeStruct((1, rows), jnp.int32)],
        in_specs=[VMEM] * 3,
        out_specs=[VMEM] * 2,
        compiler_params=SMALL,
        name="sort_rows",
    )(*flat(raw))
    near, direct, first, far = pl.pallas_call(
        join_kernel,
        out_shape=[payload] * 4,
        in_specs=[VMEM] * 4,
        out_specs=[VMEM] * 4,
        compiler_params=SMALL,
        name="join_cores",
    )(keep, *flat(swapped))
    crossed = lax.ppermute(far, "clus", [(c, c ^ 2) for c in range(4)])
    arrived = []
    for other, place in BLOCKS:
        if other and place == FAR:
            arrived.append(to_meeting(direct, place, cross=1))
        elif not other and place == FAR:
            arrived.append(to_meeting(first, place))
        else:
            value = crossed if other else near
            arrived.append(value if place is None else to_meeting(value, place))

    def meeting(kernel, first, last, known, shape):
        return pl.pallas_call(
            functools.partial(kernel, first, last),
            out_shape=jax.ShapeDtypeStruct(shape, jnp.float32),
            in_specs=[VMEM] * (last + len(known)),
            out_specs=VMEM,
            compiler_params=SMALL,
            name=f"meet_{first}_{last}",
        )(*arrived[:last], *known)

    best = meeting(meet_kernel, 0, 4, [], (8, 128))
    best = meeting(meet_kernel, 4, 6, [best], (8, 128))
    best = meeting(last_meet_kernel, 6, 8, [best], (32, 1, 128))
    returned = lax.psum(best, everyone)
    out = pl.pallas_call(
        home_kernel,
        out_shape=jax.ShapeDtypeStruct((1, rows), jnp.float32),
        in_specs=[VMEM] * 2,
        out_specs=VMEM,
        compiler_params=SMALL,
        name="home_scores",
    )(returned, target)
    return out.reshape(rows)


def solution(mesh):
    takes_a_cluster = mesh.shape["blk"] == 4 and mesh.shape["clus"] == 4
    return jax.shard_map(
        meet if takes_a_cluster else ring,
        mesh=mesh,
        in_specs=(
            P(("groups", "blk", "clus"), None),
            P(("groups", "blk", "clus")),
            P(("groups", "blk", "clus")),
        ),
        out_specs=P(("groups", "blk", "clus")),
        check_vma=False,
    )
```

```python
import functools

import jax
import jax.numpy as jnp
from jax import lax
from jax.experimental import pallas as pl
from jax.experimental.pallas import tpu as pltpu
from jax.sharding import PartitionSpec as P

CAP = 64
EPS = 1e-06
sentinel_id = 1 << 30
VMEM = pl.BlockSpec(memory_space=pltpu.VMEM)


def passed_along(value, axis, by):
    size = lax.axis_size(axis)
    return lax.ppermute(value, axis, [(i, (i + by) % size) for i in range(size)])


def ring(embeddings, cluster, row_ids):
    owners = lax.axis_size("clus")
    loop_size = lax.axis_size("blk")
    feature_width = embeddings.shape[1]
    slot_count = owners * CAP
    values = embeddings.astype(jnp.float32)
    unit_rows = (
        values
        * lax.rsqrt(jnp.mean(values * values, axis=1, keepdims=True) + EPS)
        * feature_width ** (-0.5)
    ).astype(jnp.bfloat16)
    onehot = (cluster[:, None] == jnp.arange(owners, dtype=jnp.int32)[None, :]).astype(jnp.int32)
    before = jnp.cumsum(onehot, axis=0) - onehot
    position = jnp.sum(before * onehot, axis=1)
    target = cluster * CAP + position
    send_unit = jnp.zeros((slot_count, feature_width), jnp.bfloat16).at[target].set(unit_rows)
    send_ids = jnp.full((slot_count,), sentinel_id, jnp.int32).at[target].set(row_ids)
    exchange = functools.partial(
        lax.all_to_all, axis_name="clus", split_axis=0, concat_axis=0, tiled=True
    )
    keys_unit = exchange(send_unit.reshape(owners, CAP, feature_width)).reshape(
        slot_count, feature_width
    )
    keys_ids = exchange(send_ids.reshape(owners, CAP)).reshape(slot_count)

    def absorb(best_now, other_unit, other_ids):
        scores = lax.dot_general(
            keys_unit, other_unit, (((1,), (1,)), ((), ())), preferred_element_type=jnp.float32
        )
        allowed = other_ids[None, :] < keys_ids[:, None]
        return jnp.maximum(best_now, jnp.max(jnp.where(allowed, scores, -1.0), axis=1))

    start_best = jnp.full((slot_count,), -1.0, jnp.float32)

    def advance(step_index, state_now):
        best_now, moving_unit, moving_ids = state_now
        moving_unit, moving_ids = passed_along((moving_unit, moving_ids), "blk", 1)
        return (absorb(best_now, moving_unit, moving_ids), moving_unit, moving_ids)

    best_sim, _, _ = lax.fori_loop(
        0, loop_size - 1, advance, (absorb(start_best, keys_unit, keys_ids), keys_unit, keys_ids)
    )
    returned = exchange(best_sim.reshape(owners, CAP)).reshape(slot_count)
    return returned[target]


SLABS_ROWS = 2 * CAP
SMALL = pltpu.CompilerParams(vmem_limit_bytes=8 << 20)


def middle_of(core):
    return 1 + core


NEAR, ACROSS, FAR = 0, 2, 3
BLOCKS = (
    (0, None), (0, FAR), (1, FAR), (1, None), (0, ACROSS), (1, ACROSS), (0, NEAR), (1, NEAR),
)


def blk_of(far_blk, core):
    return far_blk if core == 0 else 3 - far_blk


def here():
    u = lax.axis_index("clus")
    b = lax.axis_index("blk")
    return u, b


def put_slabs(ref, rows):
    for t in range(rows.shape[1] // 128):
        ref[t * SLABS_ROWS : (t + 1) * SLABS_ROWS, :] = rows[:, t * 128 : (t + 1) * 128]


def get_slabs(ref):
    slabs = (ref.shape[0] - 16) // SLABS_ROWS
    return jnp.concatenate(
        [ref[t * SLABS_ROWS : (t + 1) * SLABS_ROWS, :] for t in range(slabs)], axis=1
    )


def sorted_rows(emb_ref, cluster_ref, ids_ref):
    rows, width = emb_ref.shape
    slots = 2 * CAP
    u, _ = here()
    cluster = cluster_ref[...]
    onehot = lax.broadcasted_iota(jnp.int32, (8, rows), 0) == cluster
    earlier = (
        lax.broadcasted_iota(jnp.int32, (rows, rows), 0)
        < lax.broadcasted_iota(jnp.int32, (rows, rows), 1)
    ).astype(jnp.bfloat16)
    before = jnp.dot(onehot.astype(jnp.bfloat16), earlier, preferred_element_type=jnp.float32)
    position = jnp.sum(jnp.where(onehot, before, 0.0), axis=0, keepdims=True).astype(jnp.int32)
    start = jnp.where(cluster == u, 0, jnp.where(cluster == u ^ 2, CAP, -4 * CAP))
    place = (
        lax.broadcasted_iota(jnp.int32, (slots, rows), 0) == start + position
    ).astype(jnp.bfloat16)
    values = jnp.dot(place, emb_ref[...], preferred_element_type=jnp.float32)
    mean = jnp.mean(values * values, axis=1, keepdims=True)
    unit = (values * lax.rsqrt(mean + EPS) * width ** (-0.5)).astype(jnp.bfloat16)
    ids = ids_ref[...]
    row = lax.broadcasted_iota(jnp.int32, (16, rows), 0)
    parts = jnp.where(row == 0, ids >> 8, jnp.where(row == 1, ids & 255, 1))
    moved = lax.dot_general(
        parts.astype(jnp.float32).astype(jnp.bfloat16),
        place,
        (((1,), (1,)), ((), ())),
        preferred_element_type=jnp.float32,
    )
    row = lax.broadcasted_iota(jnp.int32, (16, slots), 0)
    moved = jnp.where((moved[2:3] == 0.0) & (row == 0), 256.0, moved)
    return unit, moved, cluster * CAP + position


def sort_kernel(emb_ref, cluster_ref, ids_ref, keep_ref, target_ref):
    unit, moved, target = sorted_rows(emb_ref, cluster_ref, ids_ref)
    put_slabs(keep_ref, unit)
    keep_ref[keep_ref.shape[0] - 16 :, :] = moved.astype(jnp.bfloat16)
    target_ref[...] = target


def join_kernel(keep_ref, emb_ref, cluster_ref, ids_ref, *out_refs):
    unit, moved, _ = sorted_rows(emb_ref, cluster_ref, ids_ref)
    u, _ = here()
    core = lax.rem(u, 2)
    tail = keep_ref.shape[0] - 16
    own_at = pl.multiple_of(core * CAP, CAP)
    other_at = pl.multiple_of((1 - core) * CAP, CAP)
    kept = keep_ref[tail:, :].astype(jnp.float32)
    for out_ref, start in zip(out_refs, (0, CAP) * 2):
        for t in range(tail // SLABS_ROWS):
            base = t * SLABS_ROWS
            out_ref[pl.ds(base + own_at, CAP), :] = keep_ref[base + start : base + start + CAP, :]
            out_ref[pl.ds(base + other_at, CAP), :] = unit[
                start : start + CAP, t * 128 : (t + 1) * 128
            ]
        own = kept[:, start : start + CAP]
        other = moved[:, start : start + CAP]
        pieces = [jnp.where(core == 0, own, other), jnp.where(core == 0, other, own)]
        out_ref[tail:, :] = jnp.concatenate(pieces, axis=1).astype(jnp.bfloat16)


def take_in(refs, best, first, last):
    tail = refs[0].shape[0] - 16
    ids_of = []
    for r in refs[:last]:
        parts = r[tail:, :].astype(jnp.float32)
        ids_of.append(parts[0:1] * 256.0 + parts[1:2])
    best = list(best)

    def pair(q):
        return jnp.concatenate([get_slabs(refs[q]), get_slabs(refs[q + 1])], axis=0)

    for new in range(first, last, 2):
        rows = pair(new)
        down = jnp.concatenate(
            [jnp.broadcast_to(ids_of[q], (SLABS_ROWS, 128)).T for q in (new, new + 1)], axis=0
        )
        own = jnp.full((2 * SLABS_ROWS, 128), -1.0, jnp.float32)
        for start in range(0, new + 1, 2):
            scores = lax.dot_general(
                rows, pair(start), (((1,), (1,)), ((), ())), preferred_element_type=jnp.float32
            )
            for n in range(2):
                q = start + n
                part = scores[:, n * 128 : (n + 1) * 128]
                own = jnp.maximum(own, jnp.where(ids_of[q] < down, part, -1.0))
                if start != new:
                    theirs = jnp.where(down < ids_of[q], part, -1.0)
                    best[q] = jnp.maximum(best[q], jnp.max(theirs, axis=0, keepdims=True))
        for n in range(2):
            side = own[n * SLABS_ROWS : (n + 1) * SLABS_ROWS]
            best.append(jnp.max(side.T, axis=0, keepdims=True))
    return best


def meet_kernel(first, last, *refs):
    block_refs, best_ref = refs[:last], refs[-1]
    u, b = here()

    @pl.when(b == middle_of(lax.rem(u, 2)))
    def _():
        known = [refs[last][q : q + 1, :] for q in range(first)]
        for q, row in enumerate(take_in(block_refs, known, first, last)):
            best_ref[q : q + 1, :] = row


def last_meet_kernel(first, last, *refs):
    block_refs, best_ref = refs[:last], refs[-1]
    u, b = here()
    core = lax.rem(u, 2)

    @pl.when(b == middle_of(core))
    def _():
        known = [refs[last][q : q + 1, :] for q in range(first)]
        for q, row in enumerate(take_in(block_refs, known, first, last)):
            other, place = BLOCKS[q]
            at_blk = b if place is None else jnp.where(core == 0, place, 3 - place)
            chip = (u >> 1) ^ other
            for c in range(2):
                best_ref[at_blk * 4 + chip * 2 + c] = row


def after_kernel(_, value_ref, out_ref):
    pass


def home_kernel(got_ref, target_ref, out_ref):
    u, _ = here()
    core = lax.rem(u, 2)
    slots = 4 * CAP
    rows = target_ref.shape[1]
    pieces = []
    for c in range(4):
        row = got_ref[middle_of(c % 2) * 4 + c]
        pieces.append(jnp.where(core == 0, row[:, :CAP], row[:, CAP:]))
    best = jnp.concatenate(pieces, axis=1)
    high = best.astype(jnp.bfloat16).astype(jnp.float32)
    rest = best - high
    middle_part = rest.astype(jnp.bfloat16).astype(jnp.float32)
    low = rest - middle_part
    row = lax.broadcasted_iota(jnp.int32, (8, slots), 0)
    parts = jnp.where(row == 0, high, jnp.where(row == 1, middle_part, jnp.where(row == 2, low, 0.0)))
    place = lax.broadcasted_iota(jnp.int32, (slots, rows), 0) == target_ref[...]
    moved = jnp.dot(
        parts.astype(jnp.bfloat16), place.astype(jnp.bfloat16), preferred_element_type=jnp.float32
    )
    out_ref[...] = moved[0:1] + moved[1:2] + moved[2:3]


def meet(embeddings, cluster, row_ids):
    rows, width = embeddings.shape
    everyone = ("blk", "clus")
    payload = jax.ShapeDtypeStruct((width // 128 * SLABS_ROWS + 16, 128), jnp.bfloat16)

    def to_meeting(value, place, cross=0):
        pairs = [
            (blk_of(place, c % 2) * 4 + (c ^ 2 * cross), middle_of(c % 2) * 4 + c) for c in range(4)
        ]
        return lax.ppermute(value, everyone, pairs)

    raw = (embeddings, cluster, row_ids)
    swapped = [lax.ppermute(value, "clus", [(c, c ^ 1) for c in range(4)]) for value in raw]

    def flat(values):
        return [values[0], values[1].reshape(1, rows), values[2].reshape(1, rows)]

    keep, target = pl.pallas_call(
        sort_kernel,
        out_shape=[payload, jax.ShapeDtypeStruct((1, rows), jnp.int32)],
        in_specs=[VMEM] * 3,
        out_specs=[VMEM] * 2,
        compiler_params=SMALL,
        name="sort_rows",
    )(*flat(raw))
    near, direct, first, far = pl.pallas_call(
        join_kernel,
        out_shape=[payload] * 4,
        in_specs=[VMEM] * 4,
        out_specs=[VMEM] * 4,
        compiler_params=SMALL,
        name="join_cores",
    )(keep, *flat(swapped))
    crossed = lax.ppermute(far, "clus", [(c, c ^ 2) for c in range(4)])
    def meeting(kernel, first, last, known, shape):
        return pl.pallas_call(
            functools.partial(kernel, first, last),
            out_shape=jax.ShapeDtypeStruct(shape, jnp.float32),
            in_specs=[VMEM] * (last + len(known)),
            out_specs=VMEM,
            compiler_params=SMALL,
            name=f"meet_{first}_{last}",
        )(*arrived[:last], *known)

    arrived = [near, to_meeting(first, FAR)]
    best = meeting(meet_kernel, 0, 2, [], (8, 128))
    crossed = pl.pallas_call(
        after_kernel,
        out_shape=payload,
        in_specs=[pl.BlockSpec(memory_space=pl.ANY)] * 2,
        out_specs=pl.BlockSpec(memory_space=pl.ANY),
        input_output_aliases={1: 0},
        compiler_params=SMALL,
        name="after_far",
    )(best, crossed)
    arrived += [to_meeting(direct, FAR, cross=1), crossed]
    arrived += [to_meeting(near, ACROSS), to_meeting(direct, ACROSS, cross=1)]
    arrived += [to_meeting(near, NEAR), to_meeting(crossed, NEAR)]
    best = meeting(meet_kernel, 2, 4, [best], (8, 128))
    best = meeting(meet_kernel, 4, 6, [best], (8, 128))
    best = meeting(last_meet_kernel, 6, 8, [best], (16, 1, 128))
    returned = lax.all_to_all(best, everyone, split_axis=0, concat_axis=0, tiled=True)
    out = pl.pallas_call(
        home_kernel,
        out_shape=jax.ShapeDtypeStruct((1, rows), jnp.float32),
        in_specs=[VMEM] * 2,
        out_specs=VMEM,
        compiler_params=SMALL,
        name="home_scores",
    )(returned, target)
    return out.reshape(rows)


def solution(mesh):
    takes_a_cluster = mesh.shape["blk"] == 4 and mesh.shape["clus"] == 4
    return jax.shard_map(
        meet if takes_a_cluster else ring,
        mesh=mesh,
        in_specs=(
            P(("groups", "blk", "clus"), None),
            P(("groups", "blk", "clus")),
            P(("groups", "blk", "clus")),
        ),
        out_specs=P(("groups", "blk", "clus")),
        check_vma=False,
    )
```

```python
import functools

import jax
import jax.numpy as jnp
from jax import lax
from jax.experimental import pallas as pl
from jax.experimental.pallas import tpu as pltpu
from jax.sharding import PartitionSpec as P

CAP = 64
EPS = 1e-06
sentinel_id = 1 << 30
VMEM = pl.BlockSpec(memory_space=pltpu.VMEM)


def passed_along(value, axis, by):
    size = lax.axis_size(axis)
    return lax.ppermute(value, axis, [(i, (i + by) % size) for i in range(size)])


def ring(embeddings, cluster, row_ids):
    owners = lax.axis_size("clus")
    loop_size = lax.axis_size("blk")
    feature_width = embeddings.shape[1]
    slot_count = owners * CAP
    values = embeddings.astype(jnp.float32)
    unit_rows = (
        values
        * lax.rsqrt(jnp.mean(values * values, axis=1, keepdims=True) + EPS)
        * feature_width ** (-0.5)
    ).astype(jnp.bfloat16)
    onehot = (cluster[:, None] == jnp.arange(owners, dtype=jnp.int32)[None, :]).astype(jnp.int32)
    before = jnp.cumsum(onehot, axis=0) - onehot
    position = jnp.sum(before * onehot, axis=1)
    target = cluster * CAP + position
    send_unit = jnp.zeros((slot_count, feature_width), jnp.bfloat16).at[target].set(unit_rows)
    send_ids = jnp.full((slot_count,), sentinel_id, jnp.int32).at[target].set(row_ids)
    exchange = functools.partial(
        lax.all_to_all, axis_name="clus", split_axis=0, concat_axis=0, tiled=True
    )
    keys_unit = exchange(send_unit.reshape(owners, CAP, feature_width)).reshape(
        slot_count, feature_width
    )
    keys_ids = exchange(send_ids.reshape(owners, CAP)).reshape(slot_count)

    def absorb(best_now, other_unit, other_ids):
        scores = lax.dot_general(
            keys_unit, other_unit, (((1,), (1,)), ((), ())), preferred_element_type=jnp.float32
        )
        allowed = other_ids[None, :] < keys_ids[:, None]
        return jnp.maximum(best_now, jnp.max(jnp.where(allowed, scores, -1.0), axis=1))

    start_best = jnp.full((slot_count,), -1.0, jnp.float32)

    def advance(step_index, state_now):
        best_now, moving_unit, moving_ids = state_now
        moving_unit, moving_ids = passed_along((moving_unit, moving_ids), "blk", 1)
        return (absorb(best_now, moving_unit, moving_ids), moving_unit, moving_ids)

    best_sim, _, _ = lax.fori_loop(
        0, loop_size - 1, advance, (absorb(start_best, keys_unit, keys_ids), keys_unit, keys_ids)
    )
    returned = exchange(best_sim.reshape(owners, CAP)).reshape(slot_count)
    return returned[target]


SLABS_ROWS = 2 * CAP
SMALL = pltpu.CompilerParams(vmem_limit_bytes=8 << 20)


def middle_of(core):
    return 1 + core


NEAR, ACROSS, FAR = 0, 2, 3
BLOCKS = (
    (0, None), (1, None), (0, FAR), (1, FAR), (0, NEAR), (0, ACROSS), (1, ACROSS), (1, NEAR),
)


def blk_of(far_blk, core):
    return far_blk if core == 0 else 3 - far_blk


def here():
    u = lax.axis_index("clus")
    b = lax.axis_index("blk")
    return u, b


def put_slabs(ref, rows):
    for t in range(rows.shape[1] // 128):
        ref[t * SLABS_ROWS : (t + 1) * SLABS_ROWS, :] = rows[:, t * 128 : (t + 1) * 128]


def get_slabs(ref):
    slabs = (ref.shape[0] - 16) // SLABS_ROWS
    return jnp.concatenate(
        [ref[t * SLABS_ROWS : (t + 1) * SLABS_ROWS, :] for t in range(slabs)], axis=1
    )


def earlier_kernel(out_ref):
    shape = out_ref.shape
    row, column = (lax.broadcasted_iota(jnp.int32, shape, n) for n in range(2))
    out_ref[...] = (row < column).astype(jnp.bfloat16)


def ranked(cluster, ids, earlier):
    rows = cluster.shape[1]
    slots = 2 * CAP
    u, _ = here()
    onehot = lax.broadcasted_iota(jnp.int32, (8, rows), 0) == cluster
    before = jnp.dot(onehot.astype(jnp.bfloat16), earlier, preferred_element_type=jnp.float32)
    position = jnp.sum(jnp.where(onehot, before, 0.0), axis=0, keepdims=True).astype(jnp.int32)
    start = jnp.where(cluster == u, 0, jnp.where(cluster == u ^ 2, CAP, -4 * CAP))
    place = (
        lax.broadcasted_iota(jnp.int32, (slots, rows), 0) == start + position
    ).astype(jnp.bfloat16)
    row = lax.broadcasted_iota(jnp.int32, (16, rows), 0)
    parts = jnp.where(row == 0, ids >> 8, jnp.where(row == 1, ids & 255, 1))
    moved = lax.dot_general(
        parts.astype(jnp.float32).astype(jnp.bfloat16),
        place,
        (((1,), (1,)), ((), ())),
        preferred_element_type=jnp.float32,
    )
    row = lax.broadcasted_iota(jnp.int32, (16, slots), 0)
    moved = jnp.where((moved[2:3] == 0.0) & (row == 0), 256.0, moved)
    return cluster * CAP + position, place, moved


def unit_slots(place, emb):
    values = jnp.dot(place, emb, preferred_element_type=jnp.float32)
    mean = jnp.mean(values * values, axis=1, keepdims=True)
    return (values * lax.rsqrt(mean + EPS) * emb.shape[1] ** (-0.5)).astype(jnp.bfloat16)


def rank_kernel(cluster_ref, ids_ref, earlier_ref, target_ref, place_ref, kept_ids_ref):
    found = ranked(cluster_ref[...], ids_ref[...], earlier_ref[...])
    target_ref[...], place_ref[...], kept_ids_ref[...] = found


def sort_kernel(emb_ref, place_ref, keep_ref):
    put_slabs(keep_ref, unit_slots(place_ref[...], emb_ref[...]))


def join_kernel(keep_ref, kept_ids_ref, earlier_ref, emb_ref, cluster_ref, ids_ref, *out_refs):
    _, place, moved = ranked(cluster_ref[...], ids_ref[...], earlier_ref[...])
    unit = unit_slots(place, emb_ref[...])
    u, _ = here()
    core = lax.rem(u, 2)
    tail = keep_ref.shape[0]
    own_at = pl.multiple_of(core * CAP, CAP)
    other_at = pl.multiple_of((1 - core) * CAP, CAP)
    kept = kept_ids_ref[...]
    for out_ref, start in zip(out_refs, (0, CAP) * 2):
        for t in range(tail // SLABS_ROWS):
            base = t * SLABS_ROWS
            out_ref[pl.ds(base + own_at, CAP), :] = keep_ref[base + start : base + start + CAP, :]
            out_ref[pl.ds(base + other_at, CAP), :] = unit[
                start : start + CAP, t * 128 : (t + 1) * 128
            ]
        own = kept[:, start : start + CAP]
        other = moved[:, start : start + CAP]
        pieces = [jnp.where(core == 0, own, other), jnp.where(core == 0, other, own)]
        out_ref[tail:, :] = jnp.concatenate(pieces, axis=1).astype(jnp.bfloat16)


def take_in(refs, best, first, last):
    tail = refs[0].shape[0] - 16
    ids_of = []
    for r in refs[:last]:
        parts = r[tail:, :].astype(jnp.float32)
        ids_of.append(parts[0:1] * 256.0 + parts[1:2])
    best = list(best)

    def pair(q):
        return jnp.concatenate([get_slabs(refs[q]), get_slabs(refs[q + 1])], axis=0)

    for new in range(first, last, 2):
        rows = pair(new)
        down = jnp.concatenate(
            [jnp.broadcast_to(ids_of[q], (SLABS_ROWS, 128)).T for q in (new, new + 1)], axis=0
        )
        own = jnp.full((2 * SLABS_ROWS, 128), -1.0, jnp.float32)
        for start in range(0, new + 1, 2):
            scores = lax.dot_general(
                rows, pair(start), (((1,), (1,)), ((), ())), preferred_element_type=jnp.float32
            )
            for n in range(2):
                q = start + n
                part = scores[:, n * 128 : (n + 1) * 128]
                own = jnp.maximum(own, jnp.where(ids_of[q] < down, part, -1.0))
                if start != new:
                    theirs = jnp.where(down < ids_of[q], part, -1.0)
                    best[q] = jnp.maximum(best[q], jnp.max(theirs, axis=0, keepdims=True))
        for n in range(2):
            side = own[n * SLABS_ROWS : (n + 1) * SLABS_ROWS]
            best.append(jnp.max(side.T, axis=0, keepdims=True))
    return best


def meet_kernel(first, last, *refs):
    block_refs, best_ref = refs[:last], refs[-1]
    u, b = here()

    @pl.when(b == middle_of(lax.rem(u, 2)))
    def _():
        known = [refs[last][q : q + 1, :] for q in range(first)]
        for q, row in enumerate(take_in(block_refs, known, first, last)):
            best_ref[q : q + 1, :] = row


def last_meet_kernel(first, last, *refs):
    block_refs, best_ref = refs[:last], refs[-1]
    u, b = here()
    core = lax.rem(u, 2)

    @pl.when(b == middle_of(core))
    def _():
        known = [refs[last][q : q + 1, :] for q in range(first)]
        for q, row in enumerate(take_in(block_refs, known, first, last)):
            other, place = BLOCKS[q]
            at_blk = b if place is None else jnp.where(core == 0, place, 3 - place)
            chip = (u >> 1) ^ other
            for c in range(2):
                best_ref[at_blk * 4 + chip * 2 + c] = row


def home_kernel(got_ref, target_ref, out_ref):
    u, _ = here()
    core = lax.rem(u, 2)
    slots = 4 * CAP
    rows = target_ref.shape[1]
    pieces = []
    for c in range(4):
        row = got_ref[middle_of(c % 2) * 4 + c]
        pieces.append(jnp.where(core == 0, row[:, :CAP], row[:, CAP:]))
    best = jnp.concatenate(pieces, axis=1)
    high = best.astype(jnp.bfloat16).astype(jnp.float32)
    rest = best - high
    middle_part = rest.astype(jnp.bfloat16).astype(jnp.float32)
    low = rest - middle_part
    row = lax.broadcasted_iota(jnp.int32, (8, slots), 0)
    parts = jnp.where(row == 0, high, jnp.where(row == 1, middle_part, jnp.where(row == 2, low, 0.0)))
    place = lax.broadcasted_iota(jnp.int32, (slots, rows), 0) == target_ref[...]
    moved = jnp.dot(
        parts.astype(jnp.bfloat16), place.astype(jnp.bfloat16), preferred_element_type=jnp.float32
    )
    out_ref[...] = moved[0:1] + moved[1:2] + moved[2:3]


def meet(embeddings, cluster, row_ids):
    rows, width = embeddings.shape
    everyone = ("blk", "clus")
    payload = jax.ShapeDtypeStruct((width // 128 * SLABS_ROWS + 16, 128), jnp.bfloat16)

    def to_meeting(value, place, cross=0):
        pairs = [
            (blk_of(place, c % 2) * 4 + (c ^ 2 * cross), middle_of(c % 2) * 4 + c) for c in range(4)
        ]
        return lax.ppermute(value, everyone, pairs)

    raw = (embeddings, cluster, row_ids)
    swapped = [lax.ppermute(value, "clus", [(c, c ^ 1) for c in range(4)]) for value in raw]

    def row(value):
        return value.reshape(1, rows)

    ahead = pl.CostEstimate(flops=10**10, bytes_accessed=10**7, transcendentals=0)
    earlier = pl.pallas_call(
        earlier_kernel,
        out_shape=jax.ShapeDtypeStruct((rows, rows), jnp.bfloat16),
        out_specs=VMEM,
        compiler_params=SMALL,
        cost_estimate=ahead,
        name="earlier_rows",
    )()
    target, place, kept_ids = pl.pallas_call(
        rank_kernel,
        out_shape=[
            jax.ShapeDtypeStruct((1, rows), jnp.int32),
            jax.ShapeDtypeStruct((2 * CAP, rows), jnp.bfloat16),
            jax.ShapeDtypeStruct((16, 2 * CAP), jnp.float32),
        ],
        in_specs=[VMEM] * 3,
        out_specs=[VMEM] * 3,
        compiler_params=SMALL,
        name="rank_rows",
    )(row(cluster), row(row_ids), earlier)
    keep = pl.pallas_call(
        sort_kernel,
        out_shape=jax.ShapeDtypeStruct((payload.shape[0] - 16, 128), jnp.bfloat16),
        in_specs=[VMEM] * 2,
        out_specs=VMEM,
        compiler_params=SMALL,
        name="sort_rows",
    )(embeddings, place)
    near, direct, first, far = pl.pallas_call(
        join_kernel,
        out_shape=[payload] * 4,
        in_specs=[VMEM] * 6,
        out_specs=[VMEM] * 4,
        compiler_params=SMALL,
        name="join_cores",
    )(keep, kept_ids, earlier, swapped[0], row(swapped[1]), row(swapped[2]))
    crossed = lax.ppermute(far, "clus", [(c, c ^ 2) for c in range(4)])
    arrived = []
    for other, place in BLOCKS:
        if other and place == FAR:
            arrived.append(to_meeting(direct, place, cross=1))
        elif not other and place == FAR:
            arrived.append(to_meeting(first, place))
        else:
            value = crossed if other else near
            arrived.append(value if place is None else to_meeting(value, place))

    def meeting(kernel, first, last, known, shape):
        return pl.pallas_call(
            functools.partial(kernel, first, last),
            out_shape=jax.ShapeDtypeStruct(shape, jnp.float32),
            in_specs=[VMEM] * (last + len(known)),
            out_specs=VMEM,
            compiler_params=SMALL,
            name=f"meet_{first}_{last}",
        )(*arrived[:last], *known)

    best = meeting(meet_kernel, 0, 4, [], (8, 128))
    best = meeting(meet_kernel, 4, 6, [best], (8, 128))
    best = meeting(last_meet_kernel, 6, 8, [best], (16, 1, 128))
    returned = lax.all_to_all(best, everyone, split_axis=0, concat_axis=0, tiled=True)
    out = pl.pallas_call(
        home_kernel,
        out_shape=jax.ShapeDtypeStruct((1, rows), jnp.float32),
        in_specs=[VMEM] * 2,
        out_specs=VMEM,
        compiler_params=SMALL,
        name="home_scores",
    )(returned, target)
    return out.reshape(rows)


def solution(mesh):
    takes_a_cluster = mesh.shape["blk"] == 4 and mesh.shape["clus"] == 4
    return jax.shard_map(
        meet if takes_a_cluster else ring,
        mesh=mesh,
        in_specs=(
            P(("groups", "blk", "clus"), None),
            P(("groups", "blk", "clus")),
            P(("groups", "blk", "clus")),
        ),
        out_specs=P(("groups", "blk", "clus")),
        check_vma=False,
    )
```

```python
import functools

import jax
import jax.numpy as jnp
from jax import lax
from jax.experimental import pallas as pl
from jax.experimental.pallas import tpu as pltpu
from jax.sharding import PartitionSpec as P

CAP = 64
EPS = 1e-06
sentinel_id = 1 << 30
VMEM = pl.BlockSpec(memory_space=pltpu.VMEM)


def passed_along(value, axis, by):
    size = lax.axis_size(axis)
    return lax.ppermute(value, axis, [(i, (i + by) % size) for i in range(size)])


def ring(embeddings, cluster, row_ids):
    owners = lax.axis_size("clus")
    loop_size = lax.axis_size("blk")
    feature_width = embeddings.shape[1]
    slot_count = owners * CAP
    values = embeddings.astype(jnp.float32)
    unit_rows = (
        values
        * lax.rsqrt(jnp.mean(values * values, axis=1, keepdims=True) + EPS)
        * feature_width ** (-0.5)
    ).astype(jnp.bfloat16)
    onehot = (cluster[:, None] == jnp.arange(owners, dtype=jnp.int32)[None, :]).astype(jnp.int32)
    before = jnp.cumsum(onehot, axis=0) - onehot
    position = jnp.sum(before * onehot, axis=1)
    target = cluster * CAP + position
    send_unit = jnp.zeros((slot_count, feature_width), jnp.bfloat16).at[target].set(unit_rows)
    send_ids = jnp.full((slot_count,), sentinel_id, jnp.int32).at[target].set(row_ids)
    exchange = functools.partial(
        lax.all_to_all, axis_name="clus", split_axis=0, concat_axis=0, tiled=True
    )
    keys_unit = exchange(send_unit.reshape(owners, CAP, feature_width)).reshape(
        slot_count, feature_width
    )
    keys_ids = exchange(send_ids.reshape(owners, CAP)).reshape(slot_count)

    def absorb(best_now, other_unit, other_ids):
        scores = lax.dot_general(
            keys_unit, other_unit, (((1,), (1,)), ((), ())), preferred_element_type=jnp.float32
        )
        allowed = other_ids[None, :] < keys_ids[:, None]
        return jnp.maximum(best_now, jnp.max(jnp.where(allowed, scores, -1.0), axis=1))

    start_best = jnp.full((slot_count,), -1.0, jnp.float32)

    def advance(step_index, state_now):
        best_now, moving_unit, moving_ids = state_now
        moving_unit, moving_ids = passed_along((moving_unit, moving_ids), "blk", 1)
        return (absorb(best_now, moving_unit, moving_ids), moving_unit, moving_ids)

    best_sim, _, _ = lax.fori_loop(
        0, loop_size - 1, advance, (absorb(start_best, keys_unit, keys_ids), keys_unit, keys_ids)
    )
    returned = exchange(best_sim.reshape(owners, CAP)).reshape(slot_count)
    return returned[target]


SLABS_ROWS = 2 * CAP
SMALL = pltpu.CompilerParams(vmem_limit_bytes=8 << 20)


def middle_of(core):
    return 1 + core


NEAR, ACROSS, FAR = 0, 2, 3
BLOCKS = (
    (0, None), (1, None), (0, ACROSS), (1, FAR), (0, NEAR), (0, FAR), (1, NEAR), (1, ACROSS),
)


def blk_of(far_blk, core):
    return far_blk if core == 0 else 3 - far_blk


def here():
    u = lax.axis_index("clus")
    b = lax.axis_index("blk")
    return u, b


def put_slabs(ref, rows):
    for t in range(rows.shape[1] // 128):
        ref[t * SLABS_ROWS : (t + 1) * SLABS_ROWS, :] = rows[:, t * 128 : (t + 1) * 128]


def get_slabs(ref):
    slabs = (ref.shape[0] - 16) // SLABS_ROWS
    return jnp.concatenate(
        [ref[t * SLABS_ROWS : (t + 1) * SLABS_ROWS, :] for t in range(slabs)], axis=1
    )


def earlier_kernel(out_ref):
    shape = out_ref.shape
    row, column = (lax.broadcasted_iota(jnp.int32, shape, n) for n in range(2))
    out_ref[...] = (row < column).astype(jnp.bfloat16)


def ranked(cluster, ids, earlier):
    rows = cluster.shape[1]
    slots = 2 * CAP
    u, _ = here()
    onehot = lax.broadcasted_iota(jnp.int32, (8, rows), 0) == cluster
    before = jnp.dot(onehot.astype(jnp.bfloat16), earlier, preferred_element_type=jnp.float32)
    position = jnp.sum(jnp.where(onehot, before, 0.0), axis=0, keepdims=True).astype(jnp.int32)
    start = jnp.where(cluster == u, 0, jnp.where(cluster == u ^ 2, CAP, -4 * CAP))
    place = (
        lax.broadcasted_iota(jnp.int32, (slots, rows), 0) == start + position
    ).astype(jnp.bfloat16)
    row = lax.broadcasted_iota(jnp.int32, (16, rows), 0)
    parts = jnp.where(row == 0, ids >> 8, jnp.where(row == 1, ids & 255, 1))
    moved = lax.dot_general(
        parts.astype(jnp.float32).astype(jnp.bfloat16),
        place,
        (((1,), (1,)), ((), ())),
        preferred_element_type=jnp.float32,
    )
    row = lax.broadcasted_iota(jnp.int32, (16, slots), 0)
    moved = jnp.where((moved[2:3] == 0.0) & (row == 0), 256.0, moved)
    return cluster * CAP + position, place, moved


def unit_slots(place, emb):
    values = jnp.dot(place, emb, preferred_element_type=jnp.float32)
    mean = jnp.mean(values * values, axis=1, keepdims=True)
    return (values * lax.rsqrt(mean + EPS) * emb.shape[1] ** (-0.5)).astype(jnp.bfloat16)


def rank_kernel(cluster_ref, ids_ref, earlier_ref, target_ref, place_ref, kept_ids_ref):
    found = ranked(cluster_ref[...], ids_ref[...], earlier_ref[...])
    target_ref[...], place_ref[...], kept_ids_ref[...] = found


def sort_kernel(emb_ref, place_ref, keep_ref):
    put_slabs(keep_ref, unit_slots(place_ref[...], emb_ref[...]))


def join_kernel(keep_ref, kept_ids_ref, emb_ref, place_ref, ids_ref, *out_refs):
    unit = unit_slots(place_ref[...], emb_ref[...])
    moved = ids_ref[...]
    u, _ = here()
    core = lax.rem(u, 2)
    tail = keep_ref.shape[0]
    own_at = pl.multiple_of(core * CAP, CAP)
    other_at = pl.multiple_of((1 - core) * CAP, CAP)
    kept = kept_ids_ref[...]
    for out_ref, start in zip(out_refs, (0, CAP) * 2):
        for t in range(tail // SLABS_ROWS):
            base = t * SLABS_ROWS
            out_ref[pl.ds(base + own_at, CAP), :] = keep_ref[base + start : base + start + CAP, :]
            out_ref[pl.ds(base + other_at, CAP), :] = unit[
                start : start + CAP, t * 128 : (t + 1) * 128
            ]
        own = kept[:, start : start + CAP]
        other = moved[:, start : start + CAP]
        pieces = [jnp.where(core == 0, own, other), jnp.where(core == 0, other, own)]
        out_ref[tail:, :] = jnp.concatenate(pieces, axis=1).astype(jnp.bfloat16)


def take_in(refs, best, first, last):
    tail = refs[0].shape[0] - 16
    ids_of = []
    for r in refs[:last]:
        parts = r[tail:, :].astype(jnp.float32)
        ids_of.append(parts[0:1] * 256.0 + parts[1:2])
    best = list(best)

    def pair(q):
        return jnp.concatenate([get_slabs(refs[q]), get_slabs(refs[q + 1])], axis=0)

    for new in range(first, last, 2):
        rows = pair(new)
        down = jnp.concatenate(
            [jnp.broadcast_to(ids_of[q], (SLABS_ROWS, 128)).T for q in (new, new + 1)], axis=0
        )
        own = jnp.full((2 * SLABS_ROWS, 128), -1.0, jnp.float32)
        for start in range(0, new + 1, 2):
            scores = lax.dot_general(
                rows, pair(start), (((1,), (1,)), ((), ())), preferred_element_type=jnp.float32
            )
            for n in range(2):
                q = start + n
                part = scores[:, n * 128 : (n + 1) * 128]
                own = jnp.maximum(own, jnp.where(ids_of[q] < down, part, -1.0))
                if start != new:
                    theirs = jnp.where(down < ids_of[q], part, -1.0)
                    best[q] = jnp.maximum(best[q], jnp.max(theirs, axis=0, keepdims=True))
        for n in range(2):
            side = own[n * SLABS_ROWS : (n + 1) * SLABS_ROWS]
            best.append(jnp.max(side.T, axis=0, keepdims=True))
    return best


def meet_kernel(first, last, *refs):
    block_refs, best_ref = refs[:last], refs[-1]
    u, b = here()

    @pl.when(b == middle_of(lax.rem(u, 2)))
    def _():
        known = [refs[last][q : q + 1, :] for q in range(first)]
        for q, row in enumerate(take_in(block_refs, known, first, last)):
            best_ref[q : q + 1, :] = row


def last_meet_kernel(first, last, *refs):
    block_refs, best_ref = refs[:last], refs[-1]
    u, b = here()
    core = lax.rem(u, 2)

    @pl.when(b == middle_of(core))
    def _():
        known = [refs[last][q : q + 1, :] for q in range(first)]
        for q, row in enumerate(take_in(block_refs, known, first, last)):
            other, place = BLOCKS[q]
            at_blk = b if place is None else jnp.where(core == 0, place, 3 - place)
            chip = (u >> 1) ^ other
            for c in range(2):
                best_ref[at_blk * 4 + chip * 2 + c] = row


def home_kernel(got_ref, target_ref, out_ref):
    u, _ = here()
    core = lax.rem(u, 2)
    slots = 4 * CAP
    rows = target_ref.shape[1]
    pieces = []
    for c in range(4):
        row = got_ref[middle_of(c % 2) * 4 + c]
        pieces.append(jnp.where(core == 0, row[:, :CAP], row[:, CAP:]))
    best = jnp.concatenate(pieces, axis=1)
    high = best.astype(jnp.bfloat16).astype(jnp.float32)
    rest = best - high
    middle_part = rest.astype(jnp.bfloat16).astype(jnp.float32)
    low = rest - middle_part
    row = lax.broadcasted_iota(jnp.int32, (8, slots), 0)
    parts = jnp.where(row == 0, high, jnp.where(row == 1, middle_part, jnp.where(row == 2, low, 0.0)))
    place = lax.broadcasted_iota(jnp.int32, (slots, rows), 0) == target_ref[...]
    moved = jnp.dot(
        parts.astype(jnp.bfloat16), place.astype(jnp.bfloat16), preferred_element_type=jnp.float32
    )
    out_ref[...] = moved[0:1] + moved[1:2] + moved[2:3]


def meet(embeddings, cluster, row_ids):
    rows, width = embeddings.shape
    everyone = ("blk", "clus")
    payload = jax.ShapeDtypeStruct((width // 128 * SLABS_ROWS + 16, 128), jnp.bfloat16)

    def to_meeting(value, place, cross=0):
        pairs = [
            (blk_of(place, c % 2) * 4 + (c ^ 2 * cross), middle_of(c % 2) * 4 + c) for c in range(4)
        ]
        return lax.ppermute(value, everyone, pairs)

    raw = (embeddings, cluster, row_ids)
    swapped = [lax.ppermute(value, "clus", [(c, c ^ 1) for c in range(4)]) for value in raw]

    def row(value):
        return value.reshape(1, rows)

    ahead = pl.CostEstimate(flops=10**10, bytes_accessed=10**7, transcendentals=0)
    earlier = pl.pallas_call(
        earlier_kernel,
        out_shape=jax.ShapeDtypeStruct((rows, rows), jnp.bfloat16),
        out_specs=VMEM,
        compiler_params=SMALL,
        cost_estimate=ahead,
        name="earlier_rows",
    )()

    def rank(clusters, ids, name):
        return pl.pallas_call(
            rank_kernel,
            out_shape=[
                jax.ShapeDtypeStruct((1, rows), jnp.int32),
                jax.ShapeDtypeStruct((2 * CAP, rows), jnp.bfloat16),
                jax.ShapeDtypeStruct((16, 2 * CAP), jnp.float32),
            ],
            in_specs=[VMEM] * 3,
            out_specs=[VMEM] * 3,
            compiler_params=SMALL,
            name=name,
        )(row(clusters), row(ids), earlier)

    target, place, kept_ids = rank(cluster, row_ids, "rank_rows")
    _, place2, ids2 = rank(swapped[1], swapped[2], "rank_others")
    keep = pl.pallas_call(
        sort_kernel,
        out_shape=jax.ShapeDtypeStruct((payload.shape[0] - 16, 128), jnp.bfloat16),
        in_specs=[VMEM] * 2,
        out_specs=VMEM,
        compiler_params=SMALL,
        name="sort_rows",
    )(embeddings, place)
    near, direct, first, far = pl.pallas_call(
        join_kernel,
        out_shape=[payload] * 4,
        in_specs=[VMEM] * 5,
        out_specs=[VMEM] * 4,
        compiler_params=SMALL,
        name="join_cores",
    )(keep, kept_ids, swapped[0], place2, ids2)
    crossed = lax.ppermute(far, "clus", [(c, c ^ 2) for c in range(4)])
    arrived = []
    for other, place in BLOCKS:
        if other and place == FAR:
            arrived.append(to_meeting(direct, place, cross=1))
        elif not other and place == ACROSS:
            arrived.append(to_meeting(first, place))
        else:
            value = crossed if other else near
            arrived.append(value if place is None else to_meeting(value, place))

    def meeting(kernel, first, last, known, shape):
        return pl.pallas_call(
            functools.partial(kernel, first, last),
            out_shape=jax.ShapeDtypeStruct(shape, jnp.float32),
            in_specs=[VMEM] * (last + len(known)),
            out_specs=VMEM,
            compiler_params=SMALL,
            name=f"meet_{first}_{last}",
        )(*arrived[:last], *known)

    best = meeting(meet_kernel, 0, 4, [], (8, 128))
    best = meeting(meet_kernel, 4, 6, [best], (8, 128))
    best = meeting(last_meet_kernel, 6, 8, [best], (16, 1, 128))
    returned = lax.all_to_all(best, everyone, split_axis=0, concat_axis=0, tiled=True)
    out = pl.pallas_call(
        home_kernel,
        out_shape=jax.ShapeDtypeStruct((1, rows), jnp.float32),
        in_specs=[VMEM] * 2,
        out_specs=VMEM,
        compiler_params=SMALL,
        name="home_scores",
    )(returned, target)
    return out.reshape(rows)


def solution(mesh):
    takes_a_cluster = mesh.shape["blk"] == 4 and mesh.shape["clus"] == 4
    return jax.shard_map(
        meet if takes_a_cluster else ring,
        mesh=mesh,
        in_specs=(
            P(("groups", "blk", "clus"), None),
            P(("groups", "blk", "clus")),
            P(("groups", "blk", "clus")),
        ),
        out_specs=P(("groups", "blk", "clus")),
        check_vma=False,
    )
```

```python
import functools

import jax
import jax.numpy as jnp
from jax import lax
from jax.experimental import pallas as pl
from jax.experimental.pallas import tpu as pltpu
from jax.sharding import PartitionSpec as P

CAP = 64
EPS = 1e-06
sentinel_id = 1 << 30
VMEM = pl.BlockSpec(memory_space=pltpu.VMEM)


def passed_along(value, axis, by):
    size = lax.axis_size(axis)
    return lax.ppermute(value, axis, [(i, (i + by) % size) for i in range(size)])


def ring(embeddings, cluster, row_ids):
    owners = lax.axis_size("clus")
    loop_size = lax.axis_size("blk")
    feature_width = embeddings.shape[1]
    slot_count = owners * CAP
    values = embeddings.astype(jnp.float32)
    unit_rows = (
        values
        * lax.rsqrt(jnp.mean(values * values, axis=1, keepdims=True) + EPS)
        * feature_width ** (-0.5)
    ).astype(jnp.bfloat16)
    onehot = (cluster[:, None] == jnp.arange(owners, dtype=jnp.int32)[None, :]).astype(jnp.int32)
    before = jnp.cumsum(onehot, axis=0) - onehot
    position = jnp.sum(before * onehot, axis=1)
    target = cluster * CAP + position
    send_unit = jnp.zeros((slot_count, feature_width), jnp.bfloat16).at[target].set(unit_rows)
    send_ids = jnp.full((slot_count,), sentinel_id, jnp.int32).at[target].set(row_ids)
    exchange = functools.partial(
        lax.all_to_all, axis_name="clus", split_axis=0, concat_axis=0, tiled=True
    )
    keys_unit = exchange(send_unit.reshape(owners, CAP, feature_width)).reshape(
        slot_count, feature_width
    )
    keys_ids = exchange(send_ids.reshape(owners, CAP)).reshape(slot_count)

    def absorb(best_now, other_unit, other_ids):
        scores = lax.dot_general(
            keys_unit, other_unit, (((1,), (1,)), ((), ())), preferred_element_type=jnp.float32
        )
        allowed = other_ids[None, :] < keys_ids[:, None]
        return jnp.maximum(best_now, jnp.max(jnp.where(allowed, scores, -1.0), axis=1))

    start_best = jnp.full((slot_count,), -1.0, jnp.float32)

    def advance(step_index, state_now):
        best_now, moving_unit, moving_ids = state_now
        moving_unit, moving_ids = passed_along((moving_unit, moving_ids), "blk", 1)
        return (absorb(best_now, moving_unit, moving_ids), moving_unit, moving_ids)

    best_sim, _, _ = lax.fori_loop(
        0, loop_size - 1, advance, (absorb(start_best, keys_unit, keys_ids), keys_unit, keys_ids)
    )
    returned = exchange(best_sim.reshape(owners, CAP)).reshape(slot_count)
    return returned[target]


SLABS_ROWS = 2 * CAP
SMALL = pltpu.CompilerParams(vmem_limit_bytes=8 << 20)


def middle_of(core):
    return 1 + core


NEAR, ACROSS, FAR = 0, 2, 3
BLOCKS = (
    (0, None), (1, FAR), (1, ACROSS), (1, NEAR), (0, FAR), (1, None), (0, ACROSS), (0, NEAR),
)


def blk_of(far_blk, core):
    return far_blk if core == 0 else 3 - far_blk


def here():
    u = lax.axis_index("clus")
    b = lax.axis_index("blk")
    return u, b


def put_slabs(ref, rows):
    for t in range(rows.shape[1] // 128):
        ref[t * SLABS_ROWS : (t + 1) * SLABS_ROWS, :] = rows[:, t * 128 : (t + 1) * 128]


def get_slabs(ref):
    slabs = (ref.shape[0] - 16) // SLABS_ROWS
    return jnp.concatenate(
        [ref[t * SLABS_ROWS : (t + 1) * SLABS_ROWS, :] for t in range(slabs)], axis=1
    )


def earlier_kernel(out_ref):
    shape = out_ref.shape
    row, column = (lax.broadcasted_iota(jnp.int32, shape, n) for n in range(2))
    out_ref[...] = (row < column).astype(jnp.bfloat16)


def ranked(cluster, ids, earlier):
    rows = cluster.shape[1]
    slots = 2 * CAP
    u, _ = here()
    onehot = lax.broadcasted_iota(jnp.int32, (8, rows), 0) == cluster
    before = jnp.dot(onehot.astype(jnp.bfloat16), earlier, preferred_element_type=jnp.float32)
    position = jnp.sum(jnp.where(onehot, before, 0.0), axis=0, keepdims=True).astype(jnp.int32)
    start = jnp.where(cluster == u, 0, jnp.where(cluster == u ^ 2, CAP, -4 * CAP))
    place = (
        lax.broadcasted_iota(jnp.int32, (slots, rows), 0) == start + position
    ).astype(jnp.bfloat16)
    row = lax.broadcasted_iota(jnp.int32, (16, rows), 0)
    parts = jnp.where(row == 0, ids >> 8, jnp.where(row == 1, ids & 255, 1))
    moved = lax.dot_general(
        parts.astype(jnp.float32).astype(jnp.bfloat16),
        place,
        (((1,), (1,)), ((), ())),
        preferred_element_type=jnp.float32,
    )
    row = lax.broadcasted_iota(jnp.int32, (16, slots), 0)
    moved = jnp.where((moved[2:3] == 0.0) & (row == 0), 256.0, moved)
    return cluster * CAP + position, place, moved


def unit_slots(place, emb):
    values = jnp.dot(place, emb, preferred_element_type=jnp.float32)
    mean = jnp.mean(values * values, axis=1, keepdims=True)
    return (values * lax.rsqrt(mean + EPS) * emb.shape[1] ** (-0.5)).astype(jnp.bfloat16)


def rank_kernel(cluster_ref, ids_ref, earlier_ref, target_ref, place_ref, kept_ids_ref):
    found = ranked(cluster_ref[...], ids_ref[...], earlier_ref[...])
    target_ref[...], place_ref[...], kept_ids_ref[...] = found


def sort_kernel(emb_ref, place_ref, keep_ref):
    put_slabs(keep_ref, unit_slots(place_ref[...], emb_ref[...]))


def join_kernel(keep_ref, kept_ids_ref, earlier_ref, emb_ref, cluster_ref, ids_ref, *out_refs):
    _, place, moved = ranked(cluster_ref[...], ids_ref[...], earlier_ref[...])
    unit = unit_slots(place, emb_ref[...])
    u, b = here()
    core = lax.rem(u, 2)
    meeting = b == middle_of(core)
    tail = keep_ref.shape[0]
    own_at = pl.multiple_of(core * CAP, CAP)
    other_at = pl.multiple_of((1 - core) * CAP, CAP)
    kept = kept_ids_ref[...]
    mixed_at = pl.multiple_of(jnp.where(meeting, CAP, 0), CAP)

    def side(value, which):
        axis = 1 if value.shape[0] == 16 else 0
        near, far = (lax.slice_in_dim(value, n * CAP, (n + 1) * CAP, axis=axis) for n in range(2))
        return (near, far, jnp.where(meeting, far, near))[which]

    for which, out_ref in enumerate(out_refs):
        start = (0, CAP, mixed_at)[which]
        for t in range(tail // SLABS_ROWS):
            base = t * SLABS_ROWS
            out_ref[pl.ds(base + own_at, CAP), :] = keep_ref[pl.ds(base + start, CAP), :]
            out_ref[pl.ds(base + other_at, CAP), :] = side(unit[:, t * 128 : (t + 1) * 128], which)
        own, other = side(kept, which), side(moved, which)
        pieces = [jnp.where(core == 0, own, other), jnp.where(core == 0, other, own)]
        out_ref[tail:, :] = jnp.concatenate(pieces, axis=1).astype(jnp.bfloat16)


def take_in(refs, best, first, last):
    tail = refs[0].shape[0] - 16
    ids_of = []
    for r in refs[:last]:
        parts = r[tail:, :].astype(jnp.float32)
        ids_of.append(parts[0:1] * 256.0 + parts[1:2])
    best = list(best)

    def pair(q):
        return jnp.concatenate([get_slabs(refs[q]), get_slabs(refs[q + 1])], axis=0)

    for new in range(first, last, 2):
        rows = pair(new)
        down = jnp.concatenate(
            [jnp.broadcast_to(ids_of[q], (SLABS_ROWS, 128)).T for q in (new, new + 1)], axis=0
        )
        own = jnp.full((2 * SLABS_ROWS, 128), -1.0, jnp.float32)
        for start in range(0, new + 1, 2):
            scores = lax.dot_general(
                rows, pair(start), (((1,), (1,)), ((), ())), preferred_element_type=jnp.float32
            )
            for n in range(2):
                q = start + n
                part = scores[:, n * 128 : (n + 1) * 128]
                own = jnp.maximum(own, jnp.where(ids_of[q] < down, part, -1.0))
                if start != new:
                    theirs = jnp.where(down < ids_of[q], part, -1.0)
                    best[q] = jnp.maximum(best[q], jnp.max(theirs, axis=0, keepdims=True))
        for n in range(2):
            side = own[n * SLABS_ROWS : (n + 1) * SLABS_ROWS]
            best.append(jnp.max(side.T, axis=0, keepdims=True))
    return best


def meet_kernel(first, last, *refs):
    block_refs, best_ref = refs[:last], refs[-1]
    u, b = here()

    @pl.when(b == middle_of(lax.rem(u, 2)))
    def _():
        known = [refs[last][q : q + 1, :] for q in range(first)]
        for q, row in enumerate(take_in(block_refs, known, first, last)):
            best_ref[q : q + 1, :] = row


def last_meet_kernel(first, last, *refs):
    block_refs, best_ref = refs[:last], refs[-1]
    u, b = here()
    core = lax.rem(u, 2)

    @pl.when(b == middle_of(core))
    def _():
        known = [refs[last][q : q + 1, :] for q in range(first)]
        for q, row in enumerate(take_in(block_refs, known, first, last)):
            other, place = BLOCKS[q]
            at_blk = b if place is None else jnp.where(core == 0, place, 3 - place)
            chip = (u >> 1) ^ other
            for c in range(2):
                best_ref[at_blk * 4 + chip * 2 + c] = row


def home_kernel(got_ref, target_ref, out_ref):
    u, _ = here()
    core = lax.rem(u, 2)
    slots = 4 * CAP
    rows = target_ref.shape[1]
    pieces = []
    for c in range(4):
        row = got_ref[middle_of(c % 2) * 4 + c]
        pieces.append(jnp.where(core == 0, row[:, :CAP], row[:, CAP:]))
    best = jnp.concatenate(pieces, axis=1)
    high = best.astype(jnp.bfloat16).astype(jnp.float32)
    rest = best - high
    middle_part = rest.astype(jnp.bfloat16).astype(jnp.float32)
    low = rest - middle_part
    row = lax.broadcasted_iota(jnp.int32, (8, slots), 0)
    parts = jnp.where(row == 0, high, jnp.where(row == 1, middle_part, jnp.where(row == 2, low, 0.0)))
    place = lax.broadcasted_iota(jnp.int32, (slots, rows), 0) == target_ref[...]
    moved = jnp.dot(
        parts.astype(jnp.bfloat16), place.astype(jnp.bfloat16), preferred_element_type=jnp.float32
    )
    out_ref[...] = moved[0:1] + moved[1:2] + moved[2:3]


def meet(embeddings, cluster, row_ids):
    rows, width = embeddings.shape
    everyone = ("blk", "clus")
    payload = jax.ShapeDtypeStruct((width // 128 * SLABS_ROWS + 16, 128), jnp.bfloat16)

    def to_meeting(value, *moves):
        pairs = []
        for c in range(4):
            for other, place, aside in moves:
                middle = middle_of(c % 2)
                at_blk = middle if place is None else blk_of(place, c % 2)
                pairs.append((at_blk * 4 + (c ^ 2 * other), middle * 4 + (c ^ aside)))
        return lax.ppermute(value, everyone, pairs)

    def to_other_core(value):
        return lax.ppermute(value, "clus", [(c, c ^ 1) for c in range(4)])

    raw = (embeddings, cluster, row_ids)
    swapped = [to_other_core(value) for value in raw]

    def row(value):
        return value.reshape(1, rows)

    ahead = pl.CostEstimate(flops=10**10, bytes_accessed=10**7, transcendentals=0)
    earlier = pl.pallas_call(
        earlier_kernel,
        out_shape=jax.ShapeDtypeStruct((rows, rows), jnp.bfloat16),
        out_specs=VMEM,
        compiler_params=SMALL,
        cost_estimate=ahead,
        name="earlier_rows",
    )()
    target, place, kept_ids = pl.pallas_call(
        rank_kernel,
        out_shape=[
            jax.ShapeDtypeStruct((1, rows), jnp.int32),
            jax.ShapeDtypeStruct((2 * CAP, rows), jnp.bfloat16),
            jax.ShapeDtypeStruct((16, 2 * CAP), jnp.float32),
        ],
        in_specs=[VMEM] * 3,
        out_specs=[VMEM] * 3,
        compiler_params=SMALL,
        name="rank_rows",
    )(row(cluster), row(row_ids), earlier)
    keep = pl.pallas_call(
        sort_kernel,
        out_shape=jax.ShapeDtypeStruct((payload.shape[0] - 16, 128), jnp.bfloat16),
        in_specs=[VMEM] * 2,
        out_specs=VMEM,
        compiler_params=SMALL,
        name="sort_rows",
    )(embeddings, place)
    near, far, mixed = pl.pallas_call(
        join_kernel,
        out_shape=[payload] * 3,
        in_specs=[VMEM] * 6,
        out_specs=[VMEM] * 3,
        compiler_params=SMALL,
        name="join_cores",
    )(keep, kept_ids, earlier, swapped[0], row(swapped[1]), row(swapped[2]))
    far_on = to_meeting(far, (1, FAR, 0))
    second = to_meeting(far, (1, ACROSS, 0), (1, NEAR, 1))
    third = to_meeting(mixed, (0, FAR, 0), (1, None, 1))
    fourth = to_meeting(near, (0, ACROSS, 0), (0, NEAR, 1))
    arrived = [near, far_on]
    for value in (second, third, fourth):
        arrived += [value, to_other_core(value)]

    def meeting(kernel, first, last, known, shape):
        return pl.pallas_call(
            functools.partial(kernel, first, last),
            out_shape=jax.ShapeDtypeStruct(shape, jnp.float32),
            in_specs=[VMEM] * (last + len(known)),
            out_specs=VMEM,
            compiler_params=SMALL,
            name=f"meet_{first}_{last}",
        )(*arrived[:last], *known)

    best = meeting(meet_kernel, 0, 2, [], (8, 128))
    best = meeting(meet_kernel, 2, 4, [best], (8, 128))
    best = meeting(meet_kernel, 4, 6, [best], (8, 128))
    best = meeting(last_meet_kernel, 6, 8, [best], (16, 1, 128))
    returned = lax.all_to_all(best, everyone, split_axis=0, concat_axis=0, tiled=True)
    out = pl.pallas_call(
        home_kernel,
        out_shape=jax.ShapeDtypeStruct((1, rows), jnp.float32),
        in_specs=[VMEM] * 2,
        out_specs=VMEM,
        compiler_params=SMALL,
        name="home_scores",
    )(returned, target)
    return out.reshape(rows)


def solution(mesh):
    takes_a_cluster = mesh.shape["blk"] == 4 and mesh.shape["clus"] == 4
    return jax.shard_map(
        meet if takes_a_cluster else ring,
        mesh=mesh,
        in_specs=(
            P(("groups", "blk", "clus"), None),
            P(("groups", "blk", "clus")),
            P(("groups", "blk", "clus")),
        ),
        out_specs=P(("groups", "blk", "clus")),
        check_vma=False,
    )
```

```python
import functools

import jax
import jax.numpy as jnp
from jax import lax
from jax.experimental import pallas as pl
from jax.experimental.pallas import tpu as pltpu
from jax.sharding import PartitionSpec as P

CAP = 64
EPS = 1e-06
sentinel_id = 1 << 30
VMEM = pl.BlockSpec(memory_space=pltpu.VMEM)


def passed_along(value, axis, by):
    size = lax.axis_size(axis)
    return lax.ppermute(value, axis, [(i, (i + by) % size) for i in range(size)])


def ring(embeddings, cluster, row_ids):
    owners = lax.axis_size("clus")
    loop_size = lax.axis_size("blk")
    feature_width = embeddings.shape[1]
    slot_count = owners * CAP
    values = embeddings.astype(jnp.float32)
    unit_rows = (
        values
        * lax.rsqrt(jnp.mean(values * values, axis=1, keepdims=True) + EPS)
        * feature_width ** (-0.5)
    ).astype(jnp.bfloat16)
    onehot = (cluster[:, None] == jnp.arange(owners, dtype=jnp.int32)[None, :]).astype(jnp.int32)
    before = jnp.cumsum(onehot, axis=0) - onehot
    position = jnp.sum(before * onehot, axis=1)
    target = cluster * CAP + position
    send_unit = jnp.zeros((slot_count, feature_width), jnp.bfloat16).at[target].set(unit_rows)
    send_ids = jnp.full((slot_count,), sentinel_id, jnp.int32).at[target].set(row_ids)
    exchange = functools.partial(
        lax.all_to_all, axis_name="clus", split_axis=0, concat_axis=0, tiled=True
    )
    keys_unit = exchange(send_unit.reshape(owners, CAP, feature_width)).reshape(
        slot_count, feature_width
    )
    keys_ids = exchange(send_ids.reshape(owners, CAP)).reshape(slot_count)

    def absorb(best_now, other_unit, other_ids):
        scores = lax.dot_general(
            keys_unit, other_unit, (((1,), (1,)), ((), ())), preferred_element_type=jnp.float32
        )
        allowed = other_ids[None, :] < keys_ids[:, None]
        return jnp.maximum(best_now, jnp.max(jnp.where(allowed, scores, -1.0), axis=1))

    start_best = jnp.full((slot_count,), -1.0, jnp.float32)

    def advance(step_index, state_now):
        best_now, moving_unit, moving_ids = state_now
        moving_unit, moving_ids = passed_along((moving_unit, moving_ids), "blk", 1)
        return (absorb(best_now, moving_unit, moving_ids), moving_unit, moving_ids)

    best_sim, _, _ = lax.fori_loop(
        0, loop_size - 1, advance, (absorb(start_best, keys_unit, keys_ids), keys_unit, keys_ids)
    )
    returned = exchange(best_sim.reshape(owners, CAP)).reshape(slot_count)
    return returned[target]


SLABS_ROWS = 2 * CAP
SMALL = pltpu.CompilerParams(vmem_limit_bytes=8 << 20)


def middle_of(core):
    return 1 + core


NEAR, ACROSS, FAR = 0, 2, 3
BLOCKS = (
    (0, None), (1, FAR), (1, ACROSS), (1, NEAR), (0, ACROSS), (0, NEAR), (0, FAR), (1, None),
)


def blk_of(far_blk, core):
    return far_blk if core == 0 else 3 - far_blk


def here():
    u = lax.axis_index("clus")
    b = lax.axis_index("blk")
    return u, b


def put_slabs(ref, rows):
    for t in range(rows.shape[1] // 128):
        ref[t * SLABS_ROWS : (t + 1) * SLABS_ROWS, :] = rows[:, t * 128 : (t + 1) * 128]


def get_slabs(ref):
    slabs = (ref.shape[0] - 16) // SLABS_ROWS
    return jnp.concatenate(
        [ref[t * SLABS_ROWS : (t + 1) * SLABS_ROWS, :] for t in range(slabs)], axis=1
    )


def earlier_kernel(out_ref):
    shape = out_ref.shape
    row, column = (lax.broadcasted_iota(jnp.int32, shape, n) for n in range(2))
    out_ref[...] = (row < column).astype(jnp.bfloat16)


def ranked(cluster, ids, earlier):
    rows = cluster.shape[1]
    slots = 2 * CAP
    u, _ = here()
    onehot = lax.broadcasted_iota(jnp.int32, (8, rows), 0) == cluster
    before = jnp.dot(onehot.astype(jnp.bfloat16), earlier, preferred_element_type=jnp.float32)
    position = jnp.sum(jnp.where(onehot, before, 0.0), axis=0, keepdims=True).astype(jnp.int32)
    start = jnp.where(cluster == u, 0, jnp.where(cluster == u ^ 2, CAP, -4 * CAP))
    place = (
        lax.broadcasted_iota(jnp.int32, (slots, rows), 0) == start + position
    ).astype(jnp.bfloat16)
    row = lax.broadcasted_iota(jnp.int32, (16, rows), 0)
    parts = jnp.where(row == 0, ids >> 8, jnp.where(row == 1, ids & 255, 1))
    moved = lax.dot_general(
        parts.astype(jnp.float32).astype(jnp.bfloat16),
        place,
        (((1,), (1,)), ((), ())),
        preferred_element_type=jnp.float32,
    )
    row = lax.broadcasted_iota(jnp.int32, (16, slots), 0)
    moved = jnp.where((moved[2:3] == 0.0) & (row == 0), 256.0, moved)
    return cluster * CAP + position, place, moved


def unit_slots(place, emb):
    values = jnp.dot(place, emb, preferred_element_type=jnp.float32)
    mean = jnp.mean(values * values, axis=1, keepdims=True)
    return (values * lax.rsqrt(mean + EPS) * emb.shape[1] ** (-0.5)).astype(jnp.bfloat16)


def rank_kernel(cluster_ref, ids_ref, earlier_ref, target_ref, place_ref, kept_ids_ref):
    found = ranked(cluster_ref[...], ids_ref[...], earlier_ref[...])
    target_ref[...], place_ref[...], kept_ids_ref[...] = found


def sort_kernel(emb_ref, place_ref, keep_ref):
    put_slabs(keep_ref, unit_slots(place_ref[...], emb_ref[...]))


def join_kernel(keep_ref, kept_ids_ref, earlier_ref, emb_ref, cluster_ref, ids_ref, *out_refs):
    _, place, moved = ranked(cluster_ref[...], ids_ref[...], earlier_ref[...])
    unit = unit_slots(place, emb_ref[...])
    u, b = here()
    core = lax.rem(u, 2)
    meeting = b == middle_of(core)
    tail = keep_ref.shape[0]
    own_at = pl.multiple_of(core * CAP, CAP)
    other_at = pl.multiple_of((1 - core) * CAP, CAP)
    kept = kept_ids_ref[...]
    mixed_at = pl.multiple_of(jnp.where(meeting, CAP, 0), CAP)

    def side(value, which):
        axis = 1 if value.shape[0] == 16 else 0
        near, far = (lax.slice_in_dim(value, n * CAP, (n + 1) * CAP, axis=axis) for n in range(2))
        return (near, far, jnp.where(meeting, far, near))[which]

    for which, out_ref in enumerate(out_refs):
        start = (0, CAP, mixed_at)[which]
        for t in range(tail // SLABS_ROWS):
            base = t * SLABS_ROWS
            out_ref[pl.ds(base + own_at, CAP), :] = keep_ref[pl.ds(base + start, CAP), :]
            out_ref[pl.ds(base + other_at, CAP), :] = side(unit[:, t * 128 : (t + 1) * 128], which)
        own, other = side(kept, which), side(moved, which)
        pieces = [jnp.where(core == 0, own, other), jnp.where(core == 0, other, own)]
        out_ref[tail:, :] = jnp.concatenate(pieces, axis=1).astype(jnp.bfloat16)


def take_in(refs, best, first, last):
    tail = refs[0].shape[0] - 16
    ids_of = []
    for r in refs[:last]:
        parts = r[tail:, :].astype(jnp.float32)
        ids_of.append(parts[0:1] * 256.0 + parts[1:2])
    best = list(best)

    def pair(q):
        return jnp.concatenate([get_slabs(refs[q]), get_slabs(refs[q + 1])], axis=0)

    for new in range(first, last, 2):
        rows = pair(new)
        down = jnp.concatenate(
            [jnp.broadcast_to(ids_of[q], (SLABS_ROWS, 128)).T for q in (new, new + 1)], axis=0
        )
        own = jnp.full((2 * SLABS_ROWS, 128), -1.0, jnp.float32)
        for start in range(0, new + 1, 2):
            scores = lax.dot_general(
                rows, pair(start), (((1,), (1,)), ((), ())), preferred_element_type=jnp.float32
            )
            for n in range(2):
                q = start + n
                part = scores[:, n * 128 : (n + 1) * 128]
                own = jnp.maximum(own, jnp.where(ids_of[q] < down, part, -1.0))
                if start != new:
                    theirs = jnp.where(down < ids_of[q], part, -1.0)
                    best[q] = jnp.maximum(best[q], jnp.max(theirs, axis=0, keepdims=True))
        for n in range(2):
            side = own[n * SLABS_ROWS : (n + 1) * SLABS_ROWS]
            best.append(jnp.max(side.T, axis=0, keepdims=True))
    return best


def meet_kernel(first, last, *refs):
    block_refs, best_ref = refs[:last], refs[-1]
    u, b = here()

    @pl.when(b == middle_of(lax.rem(u, 2)))
    def _():
        known = [refs[last][q : q + 1, :] for q in range(first)]
        for q, row in enumerate(take_in(block_refs, known, first, last)):
            best_ref[q : q + 1, :] = row


def last_meet_kernel(first, last, *refs):
    block_refs, best_ref = refs[:last], refs[-1]
    u, b = here()
    core = lax.rem(u, 2)

    @pl.when(b == middle_of(core))
    def _():
        known = [refs[last][q : q + 1, :] for q in range(first)]
        for q, row in enumerate(take_in(block_refs, known, first, last)):
            other, place = BLOCKS[q]
            at_blk = b if place is None else jnp.where(core == 0, place, 3 - place)
            chip = (u >> 1) ^ other
            for c in range(2):
                best_ref[at_blk * 4 + chip * 2 + c] = row


def home_kernel(got_ref, target_ref, out_ref):
    u, _ = here()
    core = lax.rem(u, 2)
    slots = 4 * CAP
    rows = target_ref.shape[1]
    pieces = []
    for c in range(4):
        row = got_ref[middle_of(c % 2) * 4 + c]
        pieces.append(jnp.where(core == 0, row[:, :CAP], row[:, CAP:]))
    best = jnp.concatenate(pieces, axis=1)
    high = best.astype(jnp.bfloat16).astype(jnp.float32)
    rest = best - high
    middle_part = rest.astype(jnp.bfloat16).astype(jnp.float32)
    low = rest - middle_part
    row = lax.broadcasted_iota(jnp.int32, (8, slots), 0)
    parts = jnp.where(row == 0, high, jnp.where(row == 1, middle_part, jnp.where(row == 2, low, 0.0)))
    place = lax.broadcasted_iota(jnp.int32, (slots, rows), 0) == target_ref[...]
    moved = jnp.dot(
        parts.astype(jnp.bfloat16), place.astype(jnp.bfloat16), preferred_element_type=jnp.float32
    )
    out_ref[...] = moved[0:1] + moved[1:2] + moved[2:3]


def meet(embeddings, cluster, row_ids):
    rows, width = embeddings.shape
    everyone = ("blk", "clus")
    payload = jax.ShapeDtypeStruct((width // 128 * SLABS_ROWS + 16, 128), jnp.bfloat16)

    def to_meeting(value, *moves):
        pairs = []
        for c in range(4):
            for other, place, aside in moves:
                middle = middle_of(c % 2)
                at_blk = middle if place is None else blk_of(place, c % 2)
                pairs.append((at_blk * 4 + (c ^ 2 * other), middle * 4 + (c ^ aside)))
        return lax.ppermute(value, everyone, pairs)

    def to_other_core(value):
        return lax.ppermute(value, "clus", [(c, c ^ 1) for c in range(4)])

    raw = (embeddings, cluster, row_ids)
    swapped = [to_other_core(value) for value in raw]

    def row(value):
        return value.reshape(1, rows)

    ahead = pl.CostEstimate(flops=10**10, bytes_accessed=10**7, transcendentals=0)
    earlier = pl.pallas_call(
        earlier_kernel,
        out_shape=jax.ShapeDtypeStruct((rows, rows), jnp.bfloat16),
        out_specs=VMEM,
        compiler_params=SMALL,
        cost_estimate=ahead,
        name="earlier_rows",
    )()
    target, place, kept_ids = pl.pallas_call(
        rank_kernel,
        out_shape=[
            jax.ShapeDtypeStruct((1, rows), jnp.int32),
            jax.ShapeDtypeStruct((2 * CAP, rows), jnp.bfloat16),
            jax.ShapeDtypeStruct((16, 2 * CAP), jnp.float32),
        ],
        in_specs=[VMEM] * 3,
        out_specs=[VMEM] * 3,
        compiler_params=SMALL,
        name="rank_rows",
    )(row(cluster), row(row_ids), earlier)
    keep = pl.pallas_call(
        sort_kernel,
        out_shape=jax.ShapeDtypeStruct((payload.shape[0] - 16, 128), jnp.bfloat16),
        in_specs=[VMEM] * 2,
        out_specs=VMEM,
        compiler_params=SMALL,
        name="sort_rows",
    )(embeddings, place)
    near, far, mixed = pl.pallas_call(
        join_kernel,
        out_shape=[payload] * 3,
        in_specs=[VMEM] * 6,
        out_specs=[VMEM] * 3,
        compiler_params=SMALL,
        name="join_cores",
    )(keep, kept_ids, earlier, swapped[0], row(swapped[1]), row(swapped[2]))
    rounds = (
        to_meeting(far, (1, ACROSS, 0), (1, NEAR, 1)),
        to_meeting(near, (0, ACROSS, 0), (0, NEAR, 1)),
        to_meeting(mixed, (0, FAR, 0), (1, None, 1)),
    )
    arrived = [near, to_other_core(to_meeting(far, (1, FAR, 1)))]
    for value in rounds:
        arrived += [value, to_other_core(value)]

    def meeting(kernel, first, last, known, shape):
        return pl.pallas_call(
            functools.partial(kernel, first, last),
            out_shape=jax.ShapeDtypeStruct(shape, jnp.float32),
            in_specs=[VMEM] * (last + len(known)),
            out_specs=VMEM,
            compiler_params=SMALL,
            name=f"meet_{first}_{last}",
        )(*arrived[:last], *known)

    best = meeting(meet_kernel, 0, 2, [], (8, 128))
    best = meeting(meet_kernel, 2, 4, [best], (8, 128))
    best = meeting(meet_kernel, 4, 6, [best], (8, 128))
    best = meeting(last_meet_kernel, 6, 8, [best], (16, 1, 128))
    returned = lax.all_to_all(best, everyone, split_axis=0, concat_axis=0, tiled=True)
    out = pl.pallas_call(
        home_kernel,
        out_shape=jax.ShapeDtypeStruct((1, rows), jnp.float32),
        in_specs=[VMEM] * 2,
        out_specs=VMEM,
        compiler_params=SMALL,
        name="home_scores",
    )(returned, target)
    return out.reshape(rows)


def solution(mesh):
    takes_a_cluster = mesh.shape["blk"] == 4 and mesh.shape["clus"] == 4
    return jax.shard_map(
        meet if takes_a_cluster else ring,
        mesh=mesh,
        in_specs=(
            P(("groups", "blk", "clus"), None),
            P(("groups", "blk", "clus")),
            P(("groups", "blk", "clus")),
        ),
        out_specs=P(("groups", "blk", "clus")),
        check_vma=False,
    )
```

```python
import functools

import jax
import jax.numpy as jnp
from jax import lax
from jax.experimental import pallas as pl
from jax.experimental.pallas import tpu as pltpu
from jax.sharding import PartitionSpec as P

CAP = 64
EPS = 1e-06
sentinel_id = 1 << 30
VMEM = pl.BlockSpec(memory_space=pltpu.VMEM)


def passed_along(value, axis, by):
    size = lax.axis_size(axis)
    return lax.ppermute(value, axis, [(i, (i + by) % size) for i in range(size)])


def ring(embeddings, cluster, row_ids):
    owners = lax.axis_size("clus")
    loop_size = lax.axis_size("blk")
    feature_width = embeddings.shape[1]
    slot_count = owners * CAP
    values = embeddings.astype(jnp.float32)
    unit_rows = (
        values
        * lax.rsqrt(jnp.mean(values * values, axis=1, keepdims=True) + EPS)
        * feature_width ** (-0.5)
    ).astype(jnp.bfloat16)
    onehot = (cluster[:, None] == jnp.arange(owners, dtype=jnp.int32)[None, :]).astype(jnp.int32)
    before = jnp.cumsum(onehot, axis=0) - onehot
    position = jnp.sum(before * onehot, axis=1)
    target = cluster * CAP + position
    send_unit = jnp.zeros((slot_count, feature_width), jnp.bfloat16).at[target].set(unit_rows)
    send_ids = jnp.full((slot_count,), sentinel_id, jnp.int32).at[target].set(row_ids)
    exchange = functools.partial(
        lax.all_to_all, axis_name="clus", split_axis=0, concat_axis=0, tiled=True
    )
    keys_unit = exchange(send_unit.reshape(owners, CAP, feature_width)).reshape(
        slot_count, feature_width
    )
    keys_ids = exchange(send_ids.reshape(owners, CAP)).reshape(slot_count)

    def absorb(best_now, other_unit, other_ids):
        scores = lax.dot_general(
            keys_unit, other_unit, (((1,), (1,)), ((), ())), preferred_element_type=jnp.float32
        )
        allowed = other_ids[None, :] < keys_ids[:, None]
        return jnp.maximum(best_now, jnp.max(jnp.where(allowed, scores, -1.0), axis=1))

    start_best = jnp.full((slot_count,), -1.0, jnp.float32)

    def advance(step_index, state_now):
        best_now, moving_unit, moving_ids = state_now
        moving_unit, moving_ids = passed_along((moving_unit, moving_ids), "blk", 1)
        return (absorb(best_now, moving_unit, moving_ids), moving_unit, moving_ids)

    best_sim, _, _ = lax.fori_loop(
        0, loop_size - 1, advance, (absorb(start_best, keys_unit, keys_ids), keys_unit, keys_ids)
    )
    returned = exchange(best_sim.reshape(owners, CAP)).reshape(slot_count)
    return returned[target]


SLABS_ROWS = 2 * CAP
SMALL = pltpu.CompilerParams(vmem_limit_bytes=8 << 20)


def middle_of(core):
    return 1 + core


NEAR, ACROSS, FAR = 0, 2, 3
BLOCKS = (
    (0, None), (1, None), (0, FAR), (1, FAR), (0, NEAR), (1, ACROSS), (0, ACROSS), (1, NEAR),
)


def blk_of(far_blk, core):
    return far_blk if core == 0 else 3 - far_blk


def here():
    u = lax.axis_index("clus")
    b = lax.axis_index("blk")
    return u, b


def put_slabs(ref, rows):
    for t in range(rows.shape[1] // 128):
        ref[t * SLABS_ROWS : (t + 1) * SLABS_ROWS, :] = rows[:, t * 128 : (t + 1) * 128]


def get_slabs(ref):
    slabs = (ref.shape[0] - 16) // SLABS_ROWS
    return jnp.concatenate(
        [ref[t * SLABS_ROWS : (t + 1) * SLABS_ROWS, :] for t in range(slabs)], axis=1
    )


def earlier_kernel(out_ref):
    shape = out_ref.shape
    row, column = (lax.broadcasted_iota(jnp.int32, shape, n) for n in range(2))
    out_ref[...] = (row < column).astype(jnp.bfloat16)


def ranked(cluster, ids, earlier):
    rows = cluster.shape[1]
    slots = 2 * CAP
    u, _ = here()
    onehot = lax.broadcasted_iota(jnp.int32, (8, rows), 0) == cluster
    before = jnp.dot(onehot.astype(jnp.bfloat16), earlier, preferred_element_type=jnp.float32)
    position = jnp.sum(jnp.where(onehot, before, 0.0), axis=0, keepdims=True).astype(jnp.int32)
    start = jnp.where(cluster == u, 0, jnp.where(cluster == u ^ 2, CAP, -4 * CAP))
    place = (
        lax.broadcasted_iota(jnp.int32, (slots, rows), 0) == start + position
    ).astype(jnp.bfloat16)
    row = lax.broadcasted_iota(jnp.int32, (16, rows), 0)
    parts = jnp.where(row == 0, ids >> 8, jnp.where(row == 1, ids & 255, 1))
    moved = lax.dot_general(
        parts.astype(jnp.float32).astype(jnp.bfloat16),
        place,
        (((1,), (1,)), ((), ())),
        preferred_element_type=jnp.float32,
    )
    row = lax.broadcasted_iota(jnp.int32, (16, slots), 0)
    moved = jnp.where((moved[2:3] == 0.0) & (row == 0), 256.0, moved)
    return cluster * CAP + position, place, moved


def unit_slots(place, emb):
    values = jnp.dot(place, emb, preferred_element_type=jnp.float32)
    mean = jnp.mean(values * values, axis=1, keepdims=True)
    return (values * lax.rsqrt(mean + EPS) * emb.shape[1] ** (-0.5)).astype(jnp.bfloat16)


def rank_kernel(cluster_ref, ids_ref, earlier_ref, target_ref, place_ref, kept_ids_ref):
    found = ranked(cluster_ref[...], ids_ref[...], earlier_ref[...])
    target_ref[...], place_ref[...], kept_ids_ref[...] = found


def sort_kernel(emb_ref, place_ref, keep_ref):
    put_slabs(keep_ref, unit_slots(place_ref[...], emb_ref[...]))


def join_kernel(keep_ref, kept_ids_ref, earlier_ref, emb_ref, cluster_ref, ids_ref, *out_refs):
    _, place, moved = ranked(cluster_ref[...], ids_ref[...], earlier_ref[...])
    unit = unit_slots(place, emb_ref[...])
    u, _ = here()
    core = lax.rem(u, 2)
    tail = keep_ref.shape[0]
    own_at = pl.multiple_of(core * CAP, CAP)
    other_at = pl.multiple_of((1 - core) * CAP, CAP)
    kept = kept_ids_ref[...]
    for out_ref, start in zip(out_refs, (0, CAP) * 2):
        for t in range(tail // SLABS_ROWS):
            base = t * SLABS_ROWS
            out_ref[pl.ds(base + own_at, CAP), :] = keep_ref[base + start : base + start + CAP, :]
            out_ref[pl.ds(base + other_at, CAP), :] = unit[
                start : start + CAP, t * 128 : (t + 1) * 128
            ]
        own = kept[:, start : start + CAP]
        other = moved[:, start : start + CAP]
        pieces = [jnp.where(core == 0, own, other), jnp.where(core == 0, other, own)]
        out_ref[tail:, :] = jnp.concatenate(pieces, axis=1).astype(jnp.bfloat16)


def take_in(refs, best, first, last):
    tail = refs[0].shape[0] - 16
    ids_of = []
    for r in refs[:last]:
        parts = r[tail:, :].astype(jnp.float32)
        ids_of.append(parts[0:1] * 256.0 + parts[1:2])
    best = list(best)

    def pair(q):
        return jnp.concatenate([get_slabs(refs[q]), get_slabs(refs[q + 1])], axis=0)

    for new in range(first, last, 2):
        rows = pair(new)
        down = jnp.concatenate(
            [jnp.broadcast_to(ids_of[q], (SLABS_ROWS, 128)).T for q in (new, new + 1)], axis=0
        )
        own = jnp.full((2 * SLABS_ROWS, 128), -1.0, jnp.float32)
        for start in range(0, new + 1, 2):
            scores = lax.dot_general(
                rows, pair(start), (((1,), (1,)), ((), ())), preferred_element_type=jnp.float32
            )
            for n in range(2):
                q = start + n
                part = scores[:, n * 128 : (n + 1) * 128]
                own = jnp.maximum(own, jnp.where(ids_of[q] < down, part, -1.0))
                if start != new:
                    theirs = jnp.where(down < ids_of[q], part, -1.0)
                    best[q] = jnp.maximum(best[q], jnp.max(theirs, axis=0, keepdims=True))
        for n in range(2):
            side = own[n * SLABS_ROWS : (n + 1) * SLABS_ROWS]
            best.append(jnp.max(side.T, axis=0, keepdims=True))
    return best


def meet_kernel(first, last, *refs):
    block_refs, best_ref = refs[:last], refs[-1]
    u, b = here()

    @pl.when(b == middle_of(lax.rem(u, 2)))
    def _():
        known = [refs[last][q : q + 1, :] for q in range(first)]
        for q, row in enumerate(take_in(block_refs, known, first, last)):
            best_ref[q : q + 1, :] = row


def last_meet_kernel(first, last, *refs):
    block_refs, best_ref = refs[:last], refs[-1]
    u, b = here()
    core = lax.rem(u, 2)

    @pl.when(b == middle_of(core))
    def _():
        known = [refs[last][q : q + 1, :] for q in range(first)]
        for q, row in enumerate(take_in(block_refs, known, first, last)):
            other, place = BLOCKS[q]
            at_blk = b if place is None else jnp.where(core == 0, place, 3 - place)
            chip = (u >> 1) ^ other
            for c in range(2):
                best_ref[at_blk * 4 + chip * 2 + c] = row


def home_kernel(got_ref, target_ref, out_ref):
    u, _ = here()
    core = lax.rem(u, 2)
    slots = 4 * CAP
    rows = target_ref.shape[1]
    pieces = []
    for c in range(4):
        row = got_ref[middle_of(c % 2) * 4 + c]
        pieces.append(jnp.where(core == 0, row[:, :CAP], row[:, CAP:]))
    best = jnp.concatenate(pieces, axis=1)
    high = best.astype(jnp.bfloat16).astype(jnp.float32)
    rest = best - high
    middle_part = rest.astype(jnp.bfloat16).astype(jnp.float32)
    low = rest - middle_part
    row = lax.broadcasted_iota(jnp.int32, (8, slots), 0)
    parts = jnp.where(row == 0, high, jnp.where(row == 1, middle_part, jnp.where(row == 2, low, 0.0)))
    place = lax.broadcasted_iota(jnp.int32, (slots, rows), 0) == target_ref[...]
    moved = jnp.dot(
        parts.astype(jnp.bfloat16), place.astype(jnp.bfloat16), preferred_element_type=jnp.float32
    )
    out_ref[...] = moved[0:1] + moved[1:2] + moved[2:3]


def meet(embeddings, cluster, row_ids):
    rows, width = embeddings.shape
    everyone = ("blk", "clus")
    payload = jax.ShapeDtypeStruct((width // 128 * SLABS_ROWS + 16, 128), jnp.bfloat16)

    def to_meeting(value, place, cross=0):
        pairs = [
            (blk_of(place, c % 2) * 4 + (c ^ 2 * cross), middle_of(c % 2) * 4 + c) for c in range(4)
        ]
        return lax.ppermute(value, everyone, pairs)

    raw = (embeddings, cluster, row_ids)
    swapped = [lax.ppermute(value, "clus", [(c, c ^ 1) for c in range(4)]) for value in raw]

    def row(value):
        return value.reshape(1, rows)

    ahead = pl.CostEstimate(flops=10**10, bytes_accessed=10**7, transcendentals=0)
    earlier = pl.pallas_call(
        earlier_kernel,
        out_shape=jax.ShapeDtypeStruct((rows, rows), jnp.bfloat16),
        out_specs=VMEM,
        compiler_params=SMALL,
        cost_estimate=ahead,
        name="earlier_rows",
    )()
    target, place, kept_ids = pl.pallas_call(
        rank_kernel,
        out_shape=[
            jax.ShapeDtypeStruct((1, rows), jnp.int32),
            jax.ShapeDtypeStruct((2 * CAP, rows), jnp.bfloat16),
            jax.ShapeDtypeStruct((16, 2 * CAP), jnp.float32),
        ],
        in_specs=[VMEM] * 3,
        out_specs=[VMEM] * 3,
        compiler_params=SMALL,
        name="rank_rows",
    )(row(cluster), row(row_ids), earlier)
    keep = pl.pallas_call(
        sort_kernel,
        out_shape=jax.ShapeDtypeStruct((payload.shape[0] - 16, 128), jnp.bfloat16),
        in_specs=[VMEM] * 2,
        out_specs=VMEM,
        compiler_params=SMALL,
        name="sort_rows",
    )(embeddings, place)
    near, direct, first, far = pl.pallas_call(
        join_kernel,
        out_shape=[payload] * 4,
        in_specs=[VMEM] * 6,
        out_specs=[VMEM] * 4,
        compiler_params=SMALL,
        name="join_cores",
    )(keep, kept_ids, earlier, swapped[0], row(swapped[1]), row(swapped[2]))
    used = [(b, c) for c in range(4) for b in (middle_of(c % 2), blk_of(NEAR, c % 2))]
    crossed = lax.ppermute(far, everyone, [(b * 4 + c, b * 4 + (c ^ 2)) for b, c in used])
    arrived = []
    for other, place in BLOCKS:
        if other and place in (FAR, ACROSS):
            arrived.append(to_meeting(direct, place, cross=1))
        elif not other and place == FAR:
            arrived.append(to_meeting(first, place))
        else:
            value = crossed if other else near
            arrived.append(value if place is None else to_meeting(value, place))

    def meeting(kernel, first, last, known, shape):
        return pl.pallas_call(
            functools.partial(kernel, first, last),
            out_shape=jax.ShapeDtypeStruct(shape, jnp.float32),
            in_specs=[VMEM] * (last + len(known)),
            out_specs=VMEM,
            compiler_params=SMALL,
            name=f"meet_{first}_{last}",
        )(*arrived[:last], *known)

    best = meeting(meet_kernel, 0, 4, [], (8, 128))
    best = meeting(meet_kernel, 4, 6, [best], (8, 128))
    best = meeting(last_meet_kernel, 6, 8, [best], (16, 1, 128))
    returned = lax.all_to_all(best, everyone, split_axis=0, concat_axis=0, tiled=True)
    out = pl.pallas_call(
        home_kernel,
        out_shape=jax.ShapeDtypeStruct((1, rows), jnp.float32),
        in_specs=[VMEM] * 2,
        out_specs=VMEM,
        compiler_params=SMALL,
        name="home_scores",
    )(returned, target)
    return out.reshape(rows)


def solution(mesh):
    takes_a_cluster = mesh.shape["blk"] == 4 and mesh.shape["clus"] == 4
    return jax.shard_map(
        meet if takes_a_cluster else ring,
        mesh=mesh,
        in_specs=(
            P(("groups", "blk", "clus"), None),
            P(("groups", "blk", "clus")),
            P(("groups", "blk", "clus")),
        ),
        out_specs=P(("groups", "blk", "clus")),
        check_vma=False,
    )
```

```python
import functools

import jax
import jax.numpy as jnp
from jax import lax
from jax.experimental import pallas as pl
from jax.experimental.pallas import tpu as pltpu
from jax.sharding import PartitionSpec as P

CAP = 64
EPS = 1e-06
sentinel_id = 1 << 30
VMEM = pl.BlockSpec(memory_space=pltpu.VMEM)


def passed_along(value, axis, by):
    size = lax.axis_size(axis)
    return lax.ppermute(value, axis, [(i, (i + by) % size) for i in range(size)])


def ring(embeddings, cluster, row_ids):
    owners = lax.axis_size("clus")
    loop_size = lax.axis_size("blk")
    feature_width = embeddings.shape[1]
    slot_count = owners * CAP
    values = embeddings.astype(jnp.float32)
    unit_rows = (
        values
        * lax.rsqrt(jnp.mean(values * values, axis=1, keepdims=True) + EPS)
        * feature_width ** (-0.5)
    ).astype(jnp.bfloat16)
    onehot = (cluster[:, None] == jnp.arange(owners, dtype=jnp.int32)[None, :]).astype(jnp.int32)
    before = jnp.cumsum(onehot, axis=0) - onehot
    position = jnp.sum(before * onehot, axis=1)
    target = cluster * CAP + position
    send_unit = jnp.zeros((slot_count, feature_width), jnp.bfloat16).at[target].set(unit_rows)
    send_ids = jnp.full((slot_count,), sentinel_id, jnp.int32).at[target].set(row_ids)
    exchange = functools.partial(
        lax.all_to_all, axis_name="clus", split_axis=0, concat_axis=0, tiled=True
    )
    keys_unit = exchange(send_unit.reshape(owners, CAP, feature_width)).reshape(
        slot_count, feature_width
    )
    keys_ids = exchange(send_ids.reshape(owners, CAP)).reshape(slot_count)

    def absorb(best_now, other_unit, other_ids):
        scores = lax.dot_general(
            keys_unit, other_unit, (((1,), (1,)), ((), ())), preferred_element_type=jnp.float32
        )
        allowed = other_ids[None, :] < keys_ids[:, None]
        return jnp.maximum(best_now, jnp.max(jnp.where(allowed, scores, -1.0), axis=1))

    start_best = jnp.full((slot_count,), -1.0, jnp.float32)

    def advance(step_index, state_now):
        best_now, moving_unit, moving_ids = state_now
        moving_unit, moving_ids = passed_along((moving_unit, moving_ids), "blk", 1)
        return (absorb(best_now, moving_unit, moving_ids), moving_unit, moving_ids)

    best_sim, _, _ = lax.fori_loop(
        0, loop_size - 1, advance, (absorb(start_best, keys_unit, keys_ids), keys_unit, keys_ids)
    )
    returned = exchange(best_sim.reshape(owners, CAP)).reshape(slot_count)
    return returned[target]


SLABS_ROWS = 2 * CAP
SMALL = pltpu.CompilerParams(vmem_limit_bytes=8 << 20)


def middle_of(core):
    return 1 + core


NEAR, ACROSS, FAR = 0, 2, 3
BLOCKS = (
    (0, None), (1, None), (0, FAR), (1, FAR), (0, NEAR), (0, ACROSS), (1, NEAR), (1, ACROSS),
)


def blk_of(far_blk, core):
    return far_blk if core == 0 else 3 - far_blk


def here():
    u = lax.axis_index("clus")
    b = lax.axis_index("blk")
    return u, b


def put_slabs(ref, rows):
    for t in range(rows.shape[1] // 128):
        ref[t * SLABS_ROWS : (t + 1) * SLABS_ROWS, :] = rows[:, t * 128 : (t + 1) * 128]


def get_slabs(ref):
    slabs = (ref.shape[0] - 16) // SLABS_ROWS
    return jnp.concatenate(
        [ref[t * SLABS_ROWS : (t + 1) * SLABS_ROWS, :] for t in range(slabs)], axis=1
    )


def earlier_kernel(out_ref):
    shape = out_ref.shape
    row, column = (lax.broadcasted_iota(jnp.int32, shape, n) for n in range(2))
    out_ref[...] = (row < column).astype(jnp.bfloat16)


def ranked(cluster, ids, earlier):
    rows = cluster.shape[1]
    slots = 2 * CAP
    u, _ = here()
    onehot = lax.broadcasted_iota(jnp.int32, (8, rows), 0) == cluster
    before = jnp.dot(onehot.astype(jnp.bfloat16), earlier, preferred_element_type=jnp.float32)
    position = jnp.sum(jnp.where(onehot, before, 0.0), axis=0, keepdims=True).astype(jnp.int32)
    start = jnp.where(cluster == u, 0, jnp.where(cluster == u ^ 2, CAP, -4 * CAP))
    place = (
        lax.broadcasted_iota(jnp.int32, (slots, rows), 0) == start + position
    ).astype(jnp.bfloat16)
    row = lax.broadcasted_iota(jnp.int32, (16, rows), 0)
    parts = jnp.where(row == 0, ids >> 8, jnp.where(row == 1, ids & 255, 1))
    moved = lax.dot_general(
        parts.astype(jnp.float32).astype(jnp.bfloat16),
        place,
        (((1,), (1,)), ((), ())),
        preferred_element_type=jnp.float32,
    )
    row = lax.broadcasted_iota(jnp.int32, (16, slots), 0)
    moved = jnp.where((moved[2:3] == 0.0) & (row == 0), 256.0, moved)
    return cluster * CAP + position, place, moved


def unit_slots(place, emb):
    values = jnp.dot(place, emb, preferred_element_type=jnp.float32)
    mean = jnp.mean(values * values, axis=1, keepdims=True)
    return (values * lax.rsqrt(mean + EPS) * emb.shape[1] ** (-0.5)).astype(jnp.bfloat16)


def rank_kernel(cluster_ref, ids_ref, earlier_ref, target_ref, place_ref, kept_ids_ref):
    found = ranked(cluster_ref[...], ids_ref[...], earlier_ref[...])
    target_ref[...], place_ref[...], kept_ids_ref[...] = found


def sort_kernel(emb_ref, place_ref, keep_ref):
    put_slabs(keep_ref, unit_slots(place_ref[...], emb_ref[...]))


def join_kernel(keep_ref, kept_ids_ref, earlier_ref, emb_ref, cluster_ref, ids_ref, *out_refs):
    _, place, moved = ranked(cluster_ref[...], ids_ref[...], earlier_ref[...])
    unit = unit_slots(place, emb_ref[...])
    u, _ = here()
    core = lax.rem(u, 2)
    tail = keep_ref.shape[0]
    own_at = pl.multiple_of(core * CAP, CAP)
    other_at = pl.multiple_of((1 - core) * CAP, CAP)
    kept = kept_ids_ref[...]
    for out_ref, start in zip(out_refs, (0, CAP) * 2):
        for t in range(tail // SLABS_ROWS):
            base = t * SLABS_ROWS
            out_ref[pl.ds(base + own_at, CAP), :] = keep_ref[base + start : base + start + CAP, :]
            out_ref[pl.ds(base + other_at, CAP), :] = unit[
                start : start + CAP, t * 128 : (t + 1) * 128
            ]
        own = kept[:, start : start + CAP]
        other = moved[:, start : start + CAP]
        pieces = [jnp.where(core == 0, own, other), jnp.where(core == 0, other, own)]
        out_ref[tail:, :] = jnp.concatenate(pieces, axis=1).astype(jnp.bfloat16)


def take_in(refs, best, first, last):
    tail = refs[0].shape[0] - 16
    ids_of = []
    for r in refs[:last]:
        parts = r[tail:, :].astype(jnp.float32)
        ids_of.append(parts[0:1] * 256.0 + parts[1:2])
    best = list(best)

    def pair(q):
        return jnp.concatenate([get_slabs(refs[q]), get_slabs(refs[q + 1])], axis=0)

    for new in range(first, last, 2):
        rows = pair(new)
        down = jnp.concatenate(
            [jnp.broadcast_to(ids_of[q], (SLABS_ROWS, 128)).T for q in (new, new + 1)], axis=0
        )
        own = jnp.full((2 * SLABS_ROWS, 128), -1.0, jnp.float32)
        for start in range(0, new + 1, 2):
            scores = lax.dot_general(
                rows, pair(start), (((1,), (1,)), ((), ())), preferred_element_type=jnp.float32
            )
            for n in range(2):
                q = start + n
                part = scores[:, n * 128 : (n + 1) * 128]
                own = jnp.maximum(own, jnp.where(ids_of[q] < down, part, -1.0))
                if start != new:
                    theirs = jnp.where(down < ids_of[q], part, -1.0)
                    best[q] = jnp.maximum(best[q], jnp.max(theirs, axis=0, keepdims=True))
        for n in range(2):
            side = own[n * SLABS_ROWS : (n + 1) * SLABS_ROWS]
            best.append(jnp.max(side.T, axis=0, keepdims=True))
    return best


def meet_kernel(first, last, *refs):
    block_refs, best_ref = refs[:last], refs[-1]
    u, b = here()

    @pl.when(b == middle_of(lax.rem(u, 2)))
    def _():
        known = [refs[last][q : q + 1, :] for q in range(first)]
        for q, row in enumerate(take_in(block_refs, known, first, last)):
            best_ref[q : q + 1, :] = row


def last_meet_kernel(first, last, *refs):
    block_refs, best_ref = refs[:last], refs[-1]
    u, b = here()
    core = lax.rem(u, 2)

    @pl.when(b == middle_of(core))
    def _():
        known = [refs[last][q : q + 1, :] for q in range(first)]
        for q, row in enumerate(take_in(block_refs, known, first, last)):
            other, place = BLOCKS[q]
            at_blk = b if place is None else jnp.where(core == 0, place, 3 - place)
            chip = (u >> 1) ^ other
            for c in range(2):
                best_ref[at_blk * 4 + chip * 2 + c] = row


def home_kernel(got_ref, target_ref, out_ref):
    u, _ = here()
    core = lax.rem(u, 2)
    slots = 4 * CAP
    rows = target_ref.shape[1]
    pieces = []
    for c in range(4):
        row = got_ref[middle_of(c % 2) * 4 + c]
        pieces.append(jnp.where(core == 0, row[:, :CAP], row[:, CAP:]))
    best = jnp.concatenate(pieces, axis=1)
    high = best.astype(jnp.bfloat16).astype(jnp.float32)
    rest = best - high
    middle_part = rest.astype(jnp.bfloat16).astype(jnp.float32)
    low = rest - middle_part
    row = lax.broadcasted_iota(jnp.int32, (8, slots), 0)
    parts = jnp.where(row == 0, high, jnp.where(row == 1, middle_part, jnp.where(row == 2, low, 0.0)))
    place = lax.broadcasted_iota(jnp.int32, (slots, rows), 0) == target_ref[...]
    moved = jnp.dot(
        parts.astype(jnp.bfloat16), place.astype(jnp.bfloat16), preferred_element_type=jnp.float32
    )
    out_ref[...] = moved[0:1] + moved[1:2] + moved[2:3]


def meet(embeddings, cluster, row_ids):
    rows, width = embeddings.shape
    everyone = ("blk", "clus")
    payload = jax.ShapeDtypeStruct((width // 128 * SLABS_ROWS + 16, 128), jnp.bfloat16)

    def to_meeting(value, place, cross=0):
        pairs = [
            (blk_of(place, c % 2) * 4 + (c ^ 2 * cross), middle_of(c % 2) * 4 + c) for c in range(4)
        ]
        return lax.ppermute(value, everyone, pairs)

    raw = (embeddings, cluster, row_ids)
    swapped = [lax.ppermute(value, "clus", [(c, c ^ 1) for c in range(4)]) for value in raw]

    def row(value):
        return value.reshape(1, rows)

    ahead = pl.CostEstimate(flops=10**10, bytes_accessed=10**7, transcendentals=0)
    earlier = pl.pallas_call(
        earlier_kernel,
        out_shape=jax.ShapeDtypeStruct((rows, rows), jnp.bfloat16),
        out_specs=VMEM,
        compiler_params=SMALL,
        cost_estimate=ahead,
        name="earlier_rows",
    )()
    target, place, kept_ids = pl.pallas_call(
        rank_kernel,
        out_shape=[
            jax.ShapeDtypeStruct((1, rows), jnp.int32),
            jax.ShapeDtypeStruct((2 * CAP, rows), jnp.bfloat16),
            jax.ShapeDtypeStruct((16, 2 * CAP), jnp.float32),
        ],
        in_specs=[VMEM] * 3,
        out_specs=[VMEM] * 3,
        compiler_params=SMALL,
        name="rank_rows",
    )(row(cluster), row(row_ids), earlier)
    keep = pl.pallas_call(
        sort_kernel,
        out_shape=jax.ShapeDtypeStruct((payload.shape[0] - 16, 128), jnp.bfloat16),
        in_specs=[VMEM] * 2,
        out_specs=VMEM,
        compiler_params=SMALL,
        name="sort_rows",
    )(embeddings, place)
    near, direct, first, far = pl.pallas_call(
        join_kernel,
        out_shape=[payload] * 4,
        in_specs=[VMEM] * 6,
        out_specs=[VMEM] * 4,
        compiler_params=SMALL,
        name="join_cores",
    )(keep, kept_ids, earlier, swapped[0], row(swapped[1]), row(swapped[2]))
    crossed = lax.ppermute(far, "clus", [(c, c ^ 2) for c in range(4)])
    arrived = []
    for other, place in BLOCKS:
        if other and place == FAR:
            arrived.append(to_meeting(direct, place, cross=1))
        elif not other and place == FAR:
            arrived.append(to_meeting(first, place))
        else:
            value = crossed if other else near
            arrived.append(value if place is None else to_meeting(value, place))

    def meeting(kernel, first, last, known, shape):
        return pl.pallas_call(
            functools.partial(kernel, first, last),
            out_shape=jax.ShapeDtypeStruct(shape, jnp.float32),
            in_specs=[VMEM] * (last + len(known)),
            out_specs=VMEM,
            compiler_params=SMALL,
            name=f"meet_{first}_{last}",
        )(*arrived[:last], *known)

    best = meeting(meet_kernel, 0, 4, [], (8, 128))
    best = meeting(meet_kernel, 4, 6, [best], (8, 128))
    best = meeting(last_meet_kernel, 6, 8, [best], (16, 1, 128))
    returned = lax.all_to_all(best, everyone, split_axis=0, concat_axis=0, tiled=True)
    out = pl.pallas_call(
        home_kernel,
        out_shape=jax.ShapeDtypeStruct((1, rows), jnp.float32),
        in_specs=[VMEM] * 2,
        out_specs=VMEM,
        compiler_params=SMALL,
        name="home_scores",
    )(returned, target)
    return out.reshape(rows)


def solution(mesh):
    takes_a_cluster = mesh.shape["blk"] == 4 and mesh.shape["clus"] == 4
    return jax.shard_map(
        meet if takes_a_cluster else ring,
        mesh=mesh,
        in_specs=(
            P(("groups", "blk", "clus"), None),
            P(("groups", "blk", "clus")),
            P(("groups", "blk", "clus")),
        ),
        out_specs=P(("groups", "blk", "clus")),
        check_vma=False,
    )
```

```python
import functools

import jax
import jax.numpy as jnp
from jax import lax
from jax.experimental import pallas as pl
from jax.experimental.pallas import tpu as pltpu
from jax.sharding import PartitionSpec as P

CAP = 64
EPS = 1e-06
sentinel_id = 1 << 30
VMEM = pl.BlockSpec(memory_space=pltpu.VMEM)


def passed_along(value, axis, by):
    size = lax.axis_size(axis)
    return lax.ppermute(value, axis, [(i, (i + by) % size) for i in range(size)])


def ring(embeddings, cluster, row_ids):
    owners = lax.axis_size("clus")
    loop_size = lax.axis_size("blk")
    feature_width = embeddings.shape[1]
    slot_count = owners * CAP
    values = embeddings.astype(jnp.float32)
    unit_rows = (
        values
        * lax.rsqrt(jnp.mean(values * values, axis=1, keepdims=True) + EPS)
        * feature_width ** (-0.5)
    ).astype(jnp.bfloat16)
    onehot = (cluster[:, None] == jnp.arange(owners, dtype=jnp.int32)[None, :]).astype(jnp.int32)
    before = jnp.cumsum(onehot, axis=0) - onehot
    position = jnp.sum(before * onehot, axis=1)
    target = cluster * CAP + position
    send_unit = jnp.zeros((slot_count, feature_width), jnp.bfloat16).at[target].set(unit_rows)
    send_ids = jnp.full((slot_count,), sentinel_id, jnp.int32).at[target].set(row_ids)
    exchange = functools.partial(
        lax.all_to_all, axis_name="clus", split_axis=0, concat_axis=0, tiled=True
    )
    keys_unit = exchange(send_unit.reshape(owners, CAP, feature_width)).reshape(
        slot_count, feature_width
    )
    keys_ids = exchange(send_ids.reshape(owners, CAP)).reshape(slot_count)

    def absorb(best_now, other_unit, other_ids):
        scores = lax.dot_general(
            keys_unit, other_unit, (((1,), (1,)), ((), ())), preferred_element_type=jnp.float32
        )
        allowed = other_ids[None, :] < keys_ids[:, None]
        return jnp.maximum(best_now, jnp.max(jnp.where(allowed, scores, -1.0), axis=1))

    start_best = jnp.full((slot_count,), -1.0, jnp.float32)

    def advance(step_index, state_now):
        best_now, moving_unit, moving_ids = state_now
        moving_unit, moving_ids = passed_along((moving_unit, moving_ids), "blk", 1)
        return (absorb(best_now, moving_unit, moving_ids), moving_unit, moving_ids)

    best_sim, _, _ = lax.fori_loop(
        0, loop_size - 1, advance, (absorb(start_best, keys_unit, keys_ids), keys_unit, keys_ids)
    )
    returned = exchange(best_sim.reshape(owners, CAP)).reshape(slot_count)
    return returned[target]


SLABS_ROWS = 2 * CAP
SMALL = pltpu.CompilerParams(vmem_limit_bytes=8 << 20)


def middle_of(core):
    return 1 + core


NEAR, ACROSS, FAR = 0, 2, 3
BLOCKS = (
    (0, None), (1, None), (0, FAR), (1, FAR), (0, ACROSS), (0, NEAR), (1, NEAR), (1, ACROSS),
)


def blk_of(far_blk, core):
    return far_blk if core == 0 else 3 - far_blk


def here():
    u = lax.axis_index("clus")
    b = lax.axis_index("blk")
    return u, b


def put_slabs(ref, rows):
    for t in range(rows.shape[1] // 128):
        ref[t * SLABS_ROWS : (t + 1) * SLABS_ROWS, :] = rows[:, t * 128 : (t + 1) * 128]


def get_slabs(ref):
    slabs = (ref.shape[0] - 16) // SLABS_ROWS
    return jnp.concatenate(
        [ref[t * SLABS_ROWS : (t + 1) * SLABS_ROWS, :] for t in range(slabs)], axis=1
    )


def earlier_kernel(out_ref):
    shape = out_ref.shape
    row, column = (lax.broadcasted_iota(jnp.int32, shape, n) for n in range(2))
    out_ref[...] = (row < column).astype(jnp.bfloat16)


def ranked(cluster, ids, earlier):
    rows = cluster.shape[1]
    slots = 2 * CAP
    u, _ = here()
    onehot = lax.broadcasted_iota(jnp.int32, (8, rows), 0) == cluster
    before = jnp.dot(onehot.astype(jnp.bfloat16), earlier, preferred_element_type=jnp.float32)
    position = jnp.sum(jnp.where(onehot, before, 0.0), axis=0, keepdims=True).astype(jnp.int32)
    start = jnp.where(cluster == u, 0, jnp.where(cluster == u ^ 2, CAP, -4 * CAP))
    place = (
        lax.broadcasted_iota(jnp.int32, (slots, rows), 0) == start + position
    ).astype(jnp.bfloat16)
    row = lax.broadcasted_iota(jnp.int32, (16, rows), 0)
    parts = jnp.where(row == 0, ids >> 8, jnp.where(row == 1, ids & 255, 1))
    moved = lax.dot_general(
        parts.astype(jnp.float32).astype(jnp.bfloat16),
        place,
        (((1,), (1,)), ((), ())),
        preferred_element_type=jnp.float32,
    )
    row = lax.broadcasted_iota(jnp.int32, (16, slots), 0)
    moved = jnp.where((moved[2:3] == 0.0) & (row == 0), 256.0, moved)
    return cluster * CAP + position, place, moved


def unit_slots(place, emb):
    values = jnp.dot(place, emb, preferred_element_type=jnp.float32)
    mean = jnp.mean(values * values, axis=1, keepdims=True)
    return (values * lax.rsqrt(mean + EPS) * emb.shape[1] ** (-0.5)).astype(jnp.bfloat16)


def rank_kernel(cluster_ref, ids_ref, earlier_ref, target_ref, place_ref, kept_ids_ref):
    found = ranked(cluster_ref[...], ids_ref[...], earlier_ref[...])
    target_ref[...], place_ref[...], kept_ids_ref[...] = found


def sort_kernel(emb_ref, place_ref, keep_ref):
    put_slabs(keep_ref, unit_slots(place_ref[...], emb_ref[...]))


def join_kernel(keep_ref, kept_ids_ref, earlier_ref, emb_ref, cluster_ref, ids_ref, *out_refs):
    _, place, moved = ranked(cluster_ref[...], ids_ref[...], earlier_ref[...])
    unit = unit_slots(place, emb_ref[...])
    u, _ = here()
    core = lax.rem(u, 2)
    tail = keep_ref.shape[0]
    own_at = pl.multiple_of(core * CAP, CAP)
    other_at = pl.multiple_of((1 - core) * CAP, CAP)
    kept = kept_ids_ref[...]
    for out_ref, start in zip(out_refs, (0, CAP) * 2):
        for t in range(tail // SLABS_ROWS):
            base = t * SLABS_ROWS
            out_ref[pl.ds(base + own_at, CAP), :] = keep_ref[base + start : base + start + CAP, :]
            out_ref[pl.ds(base + other_at, CAP), :] = unit[
                start : start + CAP, t * 128 : (t + 1) * 128
            ]
        own = kept[:, start : start + CAP]
        other = moved[:, start : start + CAP]
        pieces = [jnp.where(core == 0, own, other), jnp.where(core == 0, other, own)]
        out_ref[tail:, :] = jnp.concatenate(pieces, axis=1).astype(jnp.bfloat16)


def take_in(refs, best, first, last):
    tail = refs[0].shape[0] - 16
    ids_of = []
    for r in refs[:last]:
        parts = r[tail:, :].astype(jnp.float32)
        ids_of.append(parts[0:1] * 256.0 + parts[1:2])
    best = list(best)

    def pair(q):
        return jnp.concatenate([get_slabs(refs[q]), get_slabs(refs[q + 1])], axis=0)

    for new in range(first, last, 2):
        rows = pair(new)
        down = jnp.concatenate(
            [jnp.broadcast_to(ids_of[q], (SLABS_ROWS, 128)).T for q in (new, new + 1)], axis=0
        )
        own = jnp.full((2 * SLABS_ROWS, 128), -1.0, jnp.float32)
        for start in range(0, new + 1, 2):
            scores = lax.dot_general(
                rows, pair(start), (((1,), (1,)), ((), ())), preferred_element_type=jnp.float32
            )
            for n in range(2):
                q = start + n
                part = scores[:, n * 128 : (n + 1) * 128]
                own = jnp.maximum(own, jnp.where(ids_of[q] < down, part, -1.0))
                if start != new:
                    theirs = jnp.where(down < ids_of[q], part, -1.0)
                    best[q] = jnp.maximum(best[q], jnp.max(theirs, axis=0, keepdims=True))
        for n in range(2):
            side = own[n * SLABS_ROWS : (n + 1) * SLABS_ROWS]
            best.append(jnp.max(side.T, axis=0, keepdims=True))
    return best


def meet_kernel(first, last, *refs):
    block_refs, best_ref = refs[:last], refs[-1]
    u, b = here()

    @pl.when(b == middle_of(lax.rem(u, 2)))
    def _():
        known = [refs[last][q : q + 1, :] for q in range(first)]
        for q, row in enumerate(take_in(block_refs, known, first, last)):
            best_ref[q : q + 1, :] = row


def last_meet_kernel(first, last, *refs):
    block_refs, best_ref = refs[:last], refs[-1]
    u, b = here()
    core = lax.rem(u, 2)

    @pl.when(b == middle_of(core))
    def _():
        known = [refs[last][q : q + 1, :] for q in range(first)]
        for q, row in enumerate(take_in(block_refs, known, first, last)):
            other, place = BLOCKS[q]
            at_blk = b if place is None else jnp.where(core == 0, place, 3 - place)
            chip = (u >> 1) ^ other
            for c in range(2):
                best_ref[at_blk * 4 + chip * 2 + c] = row


def home_kernel(got_ref, target_ref, out_ref):
    u, _ = here()
    core = lax.rem(u, 2)
    slots = 4 * CAP
    rows = target_ref.shape[1]
    pieces = []
    for c in range(4):
        row = got_ref[middle_of(c % 2) * 4 + c]
        pieces.append(jnp.where(core == 0, row[:, :CAP], row[:, CAP:]))
    best = jnp.concatenate(pieces, axis=1)
    high = best.astype(jnp.bfloat16).astype(jnp.float32)
    rest = best - high
    middle_part = rest.astype(jnp.bfloat16).astype(jnp.float32)
    low = rest - middle_part
    row = lax.broadcasted_iota(jnp.int32, (8, slots), 0)
    parts = jnp.where(row == 0, high, jnp.where(row == 1, middle_part, jnp.where(row == 2, low, 0.0)))
    place = lax.broadcasted_iota(jnp.int32, (slots, rows), 0) == target_ref[...]
    moved = jnp.dot(
        parts.astype(jnp.bfloat16), place.astype(jnp.bfloat16), preferred_element_type=jnp.float32
    )
    out_ref[...] = moved[0:1] + moved[1:2] + moved[2:3]


def meet(embeddings, cluster, row_ids):
    rows, width = embeddings.shape
    everyone = ("blk", "clus")
    payload = jax.ShapeDtypeStruct((width // 128 * SLABS_ROWS + 16, 128), jnp.bfloat16)

    def to_meeting(value, place, cross=0):
        pairs = [
            (blk_of(place, c % 2) * 4 + (c ^ 2 * cross), middle_of(c % 2) * 4 + c) for c in range(4)
        ]
        return lax.ppermute(value, everyone, pairs)

    raw = (embeddings, cluster, row_ids)
    swapped = [lax.ppermute(value, "clus", [(c, c ^ 1) for c in range(4)]) for value in raw]

    def row(value):
        return value.reshape(1, rows)

    ahead = pl.CostEstimate(flops=10**10, bytes_accessed=10**7, transcendentals=0)
    earlier = pl.pallas_call(
        earlier_kernel,
        out_shape=jax.ShapeDtypeStruct((rows, rows), jnp.bfloat16),
        out_specs=VMEM,
        compiler_params=SMALL,
        cost_estimate=ahead,
        name="earlier_rows",
    )()
    target, place, kept_ids = pl.pallas_call(
        rank_kernel,
        out_shape=[
            jax.ShapeDtypeStruct((1, rows), jnp.int32),
            jax.ShapeDtypeStruct((2 * CAP, rows), jnp.bfloat16),
            jax.ShapeDtypeStruct((16, 2 * CAP), jnp.float32),
        ],
        in_specs=[VMEM] * 3,
        out_specs=[VMEM] * 3,
        compiler_params=SMALL,
        name="rank_rows",
    )(row(cluster), row(row_ids), earlier)
    keep = pl.pallas_call(
        sort_kernel,
        out_shape=jax.ShapeDtypeStruct((payload.shape[0] - 16, 128), jnp.bfloat16),
        in_specs=[VMEM] * 2,
        out_specs=VMEM,
        compiler_params=SMALL,
        name="sort_rows",
    )(embeddings, place)
    near, direct, first, far = pl.pallas_call(
        join_kernel,
        out_shape=[payload] * 4,
        in_specs=[VMEM] * 6,
        out_specs=[VMEM] * 4,
        compiler_params=SMALL,
        name="join_cores",
    )(keep, kept_ids, earlier, swapped[0], row(swapped[1]), row(swapped[2]))
    crossed = lax.ppermute(far, "clus", [(c, c ^ 2) for c in range(4)])
    arrived = []
    for other, place in BLOCKS:
        if other and place == FAR:
            arrived.append(to_meeting(direct, place, cross=1))
        elif not other and place == FAR:
            arrived.append(to_meeting(first, place))
        else:
            value = crossed if other else near
            arrived.append(value if place is None else to_meeting(value, place))

    def meeting(kernel, first, last, known, shape):
        return pl.pallas_call(
            functools.partial(kernel, first, last),
            out_shape=jax.ShapeDtypeStruct(shape, jnp.float32),
            in_specs=[VMEM] * (last + len(known)),
            out_specs=VMEM,
            compiler_params=SMALL,
            name=f"meet_{first}_{last}",
        )(*arrived[:last], *known)

    best = meeting(meet_kernel, 0, 4, [], (8, 128))
    best = meeting(meet_kernel, 4, 6, [best], (8, 128))
    best = meeting(last_meet_kernel, 6, 8, [best], (16, 1, 128))
    returned = lax.all_to_all(best, everyone, split_axis=0, concat_axis=0, tiled=True)
    out = pl.pallas_call(
        home_kernel,
        out_shape=jax.ShapeDtypeStruct((1, rows), jnp.float32),
        in_specs=[VMEM] * 2,
        out_specs=VMEM,
        compiler_params=SMALL,
        name="home_scores",
    )(returned, target)
    return out.reshape(rows)


def solution(mesh):
    takes_a_cluster = mesh.shape["blk"] == 4 and mesh.shape["clus"] == 4
    return jax.shard_map(
        meet if takes_a_cluster else ring,
        mesh=mesh,
        in_specs=(
            P(("groups", "blk", "clus"), None),
            P(("groups", "blk", "clus")),
            P(("groups", "blk", "clus")),
        ),
        out_specs=P(("groups", "blk", "clus")),
        check_vma=False,
    )
```

```python
import functools

import jax
import jax.numpy as jnp
from jax import lax
from jax.experimental import pallas as pl
from jax.experimental.pallas import tpu as pltpu
from jax.sharding import PartitionSpec as P

CAP = 64
EPS = 1e-06
sentinel_id = 1 << 30
VMEM = pl.BlockSpec(memory_space=pltpu.VMEM)


def passed_along(value, axis, by):
    size = lax.axis_size(axis)
    return lax.ppermute(value, axis, [(i, (i + by) % size) for i in range(size)])


def ring(embeddings, cluster, row_ids):
    owners = lax.axis_size("clus")
    loop_size = lax.axis_size("blk")
    feature_width = embeddings.shape[1]
    slot_count = owners * CAP
    values = embeddings.astype(jnp.float32)
    unit_rows = (
        values
        * lax.rsqrt(jnp.mean(values * values, axis=1, keepdims=True) + EPS)
        * feature_width ** (-0.5)
    ).astype(jnp.bfloat16)
    onehot = (cluster[:, None] == jnp.arange(owners, dtype=jnp.int32)[None, :]).astype(jnp.int32)
    before = jnp.cumsum(onehot, axis=0) - onehot
    position = jnp.sum(before * onehot, axis=1)
    target = cluster * CAP + position
    send_unit = jnp.zeros((slot_count, feature_width), jnp.bfloat16).at[target].set(unit_rows)
    send_ids = jnp.full((slot_count,), sentinel_id, jnp.int32).at[target].set(row_ids)
    exchange = functools.partial(
        lax.all_to_all, axis_name="clus", split_axis=0, concat_axis=0, tiled=True
    )
    keys_unit = exchange(send_unit.reshape(owners, CAP, feature_width)).reshape(
        slot_count, feature_width
    )
    keys_ids = exchange(send_ids.reshape(owners, CAP)).reshape(slot_count)

    def absorb(best_now, other_unit, other_ids):
        scores = lax.dot_general(
            keys_unit, other_unit, (((1,), (1,)), ((), ())), preferred_element_type=jnp.float32
        )
        allowed = other_ids[None, :] < keys_ids[:, None]
        return jnp.maximum(best_now, jnp.max(jnp.where(allowed, scores, -1.0), axis=1))

    start_best = jnp.full((slot_count,), -1.0, jnp.float32)

    def advance(step_index, state_now):
        best_now, moving_unit, moving_ids = state_now
        moving_unit, moving_ids = passed_along((moving_unit, moving_ids), "blk", 1)
        return (absorb(best_now, moving_unit, moving_ids), moving_unit, moving_ids)

    best_sim, _, _ = lax.fori_loop(
        0, loop_size - 1, advance, (absorb(start_best, keys_unit, keys_ids), keys_unit, keys_ids)
    )
    returned = exchange(best_sim.reshape(owners, CAP)).reshape(slot_count)
    return returned[target]


SLABS_ROWS = 2 * CAP
SMALL = pltpu.CompilerParams(vmem_limit_bytes=8 << 20)


def middle_of(core):
    return 1 + core


NEAR, ACROSS, FAR = 0, 2, 3
BLOCKS = (
    (0, None), (1, None), (0, ACROSS), (0, FAR), (0, NEAR), (1, FAR), (1, NEAR), (1, ACROSS),
)


def blk_of(far_blk, core):
    return far_blk if core == 0 else 3 - far_blk


def here():
    u = lax.axis_index("clus")
    b = lax.axis_index("blk")
    return u, b


def put_slabs(ref, rows):
    for t in range(rows.shape[1] // 128):
        ref[t * SLABS_ROWS : (t + 1) * SLABS_ROWS, :] = rows[:, t * 128 : (t + 1) * 128]


def get_slabs(ref):
    slabs = (ref.shape[0] - 16) // SLABS_ROWS
    return jnp.concatenate(
        [ref[t * SLABS_ROWS : (t + 1) * SLABS_ROWS, :] for t in range(slabs)], axis=1
    )


def earlier_kernel(out_ref):
    shape = out_ref.shape
    row, column = (lax.broadcasted_iota(jnp.int32, shape, n) for n in range(2))
    out_ref[...] = (row < column).astype(jnp.bfloat16)


def ranked(cluster, ids, earlier):
    rows = cluster.shape[1]
    slots = 2 * CAP
    u, _ = here()
    onehot = lax.broadcasted_iota(jnp.int32, (8, rows), 0) == cluster
    before = jnp.dot(onehot.astype(jnp.bfloat16), earlier, preferred_element_type=jnp.float32)
    position = jnp.sum(jnp.where(onehot, before, 0.0), axis=0, keepdims=True).astype(jnp.int32)
    start = jnp.where(cluster == u, 0, jnp.where(cluster == u ^ 2, CAP, -4 * CAP))
    place = (
        lax.broadcasted_iota(jnp.int32, (slots, rows), 0) == start + position
    ).astype(jnp.bfloat16)
    row = lax.broadcasted_iota(jnp.int32, (16, rows), 0)
    parts = jnp.where(row == 0, ids >> 8, jnp.where(row == 1, ids & 255, 1))
    moved = lax.dot_general(
        parts.astype(jnp.float32).astype(jnp.bfloat16),
        place,
        (((1,), (1,)), ((), ())),
        preferred_element_type=jnp.float32,
    )
    row = lax.broadcasted_iota(jnp.int32, (16, slots), 0)
    moved = jnp.where((moved[2:3] == 0.0) & (row == 0), 256.0, moved)
    return cluster * CAP + position, place, moved


def unit_slots(place, emb):
    values = jnp.dot(place, emb, preferred_element_type=jnp.float32)
    mean = jnp.mean(values * values, axis=1, keepdims=True)
    return (values * lax.rsqrt(mean + EPS) * emb.shape[1] ** (-0.5)).astype(jnp.bfloat16)


def rank_kernel(cluster_ref, ids_ref, earlier_ref, target_ref, place_ref, kept_ids_ref):
    found = ranked(cluster_ref[...], ids_ref[...], earlier_ref[...])
    target_ref[...], place_ref[...], kept_ids_ref[...] = found


def sort_kernel(emb_ref, place_ref, keep_ref):
    put_slabs(keep_ref, unit_slots(place_ref[...], emb_ref[...]))


def join_kernel(keep_ref, kept_ids_ref, earlier_ref, emb_ref, cluster_ref, ids_ref, *out_refs):
    _, place, moved = ranked(cluster_ref[...], ids_ref[...], earlier_ref[...])
    unit = unit_slots(place, emb_ref[...])
    u, _ = here()
    core = lax.rem(u, 2)
    tail = keep_ref.shape[0]
    own_at = pl.multiple_of(core * CAP, CAP)
    other_at = pl.multiple_of((1 - core) * CAP, CAP)
    kept = kept_ids_ref[...]
    for out_ref, start in zip(out_refs, (0, CAP) * 2):
        for t in range(tail // SLABS_ROWS):
            base = t * SLABS_ROWS
            out_ref[pl.ds(base + own_at, CAP), :] = keep_ref[base + start : base + start + CAP, :]
            out_ref[pl.ds(base + other_at, CAP), :] = unit[
                start : start + CAP, t * 128 : (t + 1) * 128
            ]
        own = kept[:, start : start + CAP]
        other = moved[:, start : start + CAP]
        pieces = [jnp.where(core == 0, own, other), jnp.where(core == 0, other, own)]
        out_ref[tail:, :] = jnp.concatenate(pieces, axis=1).astype(jnp.bfloat16)


def take_in(refs, best, first, last):
    tail = refs[0].shape[0] - 16
    ids_of = []
    for r in refs[:last]:
        parts = r[tail:, :].astype(jnp.float32)
        ids_of.append(parts[0:1] * 256.0 + parts[1:2])
    best = list(best)

    def pair(q):
        return jnp.concatenate([get_slabs(refs[q]), get_slabs(refs[q + 1])], axis=0)

    for new in range(first, last, 2):
        rows = pair(new)
        down = jnp.concatenate(
            [jnp.broadcast_to(ids_of[q], (SLABS_ROWS, 128)).T for q in (new, new + 1)], axis=0
        )
        own = jnp.full((2 * SLABS_ROWS, 128), -1.0, jnp.float32)
        for start in range(0, new + 1, 2):
            scores = lax.dot_general(
                rows, pair(start), (((1,), (1,)), ((), ())), preferred_element_type=jnp.float32
            )
            for n in range(2):
                q = start + n
                part = scores[:, n * 128 : (n + 1) * 128]
                own = jnp.maximum(own, jnp.where(ids_of[q] < down, part, -1.0))
                if start != new:
                    theirs = jnp.where(down < ids_of[q], part, -1.0)
                    best[q] = jnp.maximum(best[q], jnp.max(theirs, axis=0, keepdims=True))
        for n in range(2):
            side = own[n * SLABS_ROWS : (n + 1) * SLABS_ROWS]
            best.append(jnp.max(side.T, axis=0, keepdims=True))
    return best


def meet_kernel(first, last, *refs):
    block_refs, best_ref = refs[:last], refs[-1]
    u, b = here()

    @pl.when(b == middle_of(lax.rem(u, 2)))
    def _():
        known = [refs[last][q : q + 1, :] for q in range(first)]
        for q, row in enumerate(take_in(block_refs, known, first, last)):
            best_ref[q : q + 1, :] = row


def last_meet_kernel(first, last, *refs):
    block_refs, best_ref = refs[:last], refs[-1]
    u, b = here()
    core = lax.rem(u, 2)

    @pl.when(b == middle_of(core))
    def _():
        known = [refs[last][q : q + 1, :] for q in range(first)]
        for q, row in enumerate(take_in(block_refs, known, first, last)):
            other, place = BLOCKS[q]
            at_blk = b if place is None else jnp.where(core == 0, place, 3 - place)
            chip = (u >> 1) ^ other
            for c in range(2):
                best_ref[at_blk * 4 + chip * 2 + c] = row


def home_kernel(got_ref, target_ref, out_ref):
    u, _ = here()
    core = lax.rem(u, 2)
    slots = 4 * CAP
    rows = target_ref.shape[1]
    pieces = []
    for c in range(4):
        row = got_ref[middle_of(c % 2) * 4 + c]
        pieces.append(jnp.where(core == 0, row[:, :CAP], row[:, CAP:]))
    best = jnp.concatenate(pieces, axis=1)
    high = best.astype(jnp.bfloat16).astype(jnp.float32)
    rest = best - high
    middle_part = rest.astype(jnp.bfloat16).astype(jnp.float32)
    low = rest - middle_part
    row = lax.broadcasted_iota(jnp.int32, (8, slots), 0)
    parts = jnp.where(row == 0, high, jnp.where(row == 1, middle_part, jnp.where(row == 2, low, 0.0)))
    place = lax.broadcasted_iota(jnp.int32, (slots, rows), 0) == target_ref[...]
    moved = jnp.dot(
        parts.astype(jnp.bfloat16), place.astype(jnp.bfloat16), preferred_element_type=jnp.float32
    )
    out_ref[...] = moved[0:1] + moved[1:2] + moved[2:3]


def meet(embeddings, cluster, row_ids):
    rows, width = embeddings.shape
    everyone = ("blk", "clus")
    payload = jax.ShapeDtypeStruct((width // 128 * SLABS_ROWS + 16, 128), jnp.bfloat16)

    def to_meeting(value, place, cross=0):
        pairs = [
            (blk_of(place, c % 2) * 4 + (c ^ 2 * cross), middle_of(c % 2) * 4 + c) for c in range(4)
        ]
        return lax.ppermute(value, everyone, pairs)

    raw = (embeddings, cluster, row_ids)
    swapped = [lax.ppermute(value, "clus", [(c, c ^ 1) for c in range(4)]) for value in raw]

    def row(value):
        return value.reshape(1, rows)

    ahead = pl.CostEstimate(flops=10**10, bytes_accessed=10**7, transcendentals=0)
    earlier = pl.pallas_call(
        earlier_kernel,
        out_shape=jax.ShapeDtypeStruct((rows, rows), jnp.bfloat16),
        out_specs=VMEM,
        compiler_params=SMALL,
        cost_estimate=ahead,
        name="earlier_rows",
    )()
    target, place, kept_ids = pl.pallas_call(
        rank_kernel,
        out_shape=[
            jax.ShapeDtypeStruct((1, rows), jnp.int32),
            jax.ShapeDtypeStruct((2 * CAP, rows), jnp.bfloat16),
            jax.ShapeDtypeStruct((16, 2 * CAP), jnp.float32),
        ],
        in_specs=[VMEM] * 3,
        out_specs=[VMEM] * 3,
        compiler_params=SMALL,
        name="rank_rows",
    )(row(cluster), row(row_ids), earlier)
    keep = pl.pallas_call(
        sort_kernel,
        out_shape=jax.ShapeDtypeStruct((payload.shape[0] - 16, 128), jnp.bfloat16),
        in_specs=[VMEM] * 2,
        out_specs=VMEM,
        compiler_params=SMALL,
        name="sort_rows",
    )(embeddings, place)
    near, direct, first, far = pl.pallas_call(
        join_kernel,
        out_shape=[payload] * 4,
        in_specs=[VMEM] * 6,
        out_specs=[VMEM] * 4,
        compiler_params=SMALL,
        name="join_cores",
    )(keep, kept_ids, earlier, swapped[0], row(swapped[1]), row(swapped[2]))
    crossed = lax.ppermute(far, "clus", [(c, c ^ 2) for c in range(4)])
    arrived = []
    for other, place in BLOCKS:
        if other and place == FAR:
            arrived.append(to_meeting(direct, place, cross=1))
        elif not other and place in (FAR, ACROSS):
            arrived.append(to_meeting(first, place))
        else:
            value = crossed if other else near
            arrived.append(value if place is None else to_meeting(value, place))

    def meeting(kernel, first, last, known, shape):
        return pl.pallas_call(
            functools.partial(kernel, first, last),
            out_shape=jax.ShapeDtypeStruct(shape, jnp.float32),
            in_specs=[VMEM] * (last + len(known)),
            out_specs=VMEM,
            compiler_params=SMALL,
            name=f"meet_{first}_{last}",
        )(*arrived[:last], *known)

    best = meeting(meet_kernel, 0, 4, [], (8, 128))
    best = meeting(meet_kernel, 4, 6, [best], (8, 128))
    best = meeting(last_meet_kernel, 6, 8, [best], (16, 1, 128))
    returned = lax.all_to_all(best, everyone, split_axis=0, concat_axis=0, tiled=True)
    out = pl.pallas_call(
        home_kernel,
        out_shape=jax.ShapeDtypeStruct((1, rows), jnp.float32),
        in_specs=[VMEM] * 2,
        out_specs=VMEM,
        compiler_params=SMALL,
        name="home_scores",
    )(returned, target)
    return out.reshape(rows)


def solution(mesh):
    takes_a_cluster = mesh.shape["blk"] == 4 and mesh.shape["clus"] == 4
    return jax.shard_map(
        meet if takes_a_cluster else ring,
        mesh=mesh,
        in_specs=(
            P(("groups", "blk", "clus"), None),
            P(("groups", "blk", "clus")),
            P(("groups", "blk", "clus")),
        ),
        out_specs=P(("groups", "blk", "clus")),
        check_vma=False,
    )
```
